32 devices in a mesh: rows: 8 (over z, y), src: 4 (over x, core).
Axes of the slice: x: 2, y: 2, z: 4, core: 2. Of those that a mesh axis runs over, the one named last changes fastest.
Arguments:
- misfit: float32 [32, 64, 1024], P('rows', 'src'), may hold values from -6 to 6
- forward_fields: bfloat16 [32, 64, 1024], P('rows', 'src'), may hold values from -6 to 6
- contrast: float32 [32, 1024], P('rows'), may hold values from 0.2 to 0.6
- u_factors: bfloat16 [32, 16, 96, 1024], P('rows'), may hold values from -0.1875 to 0.1875
- v_factors: bfloat16 [32, 16, 96, 1024], P('rows'), may hold values from -0.1796875 to 0.1796875
- ranks: int32 [32, 16], P('rows'), may hold values from 32 to 96
- tile_cols: int32 [32, 16], replicated, may hold values from 0 to 31, as said below
- owner_slot: int32 [32], replicated, may hold values from 0 to 31, as said below
Outputs:
- adjoint_field: float32 [32, 64, 1024], P('rows', 'src')
- gradient: float32 [32, 1024], P('rows')
The draws below stay inside these ranges and needn't reach their ends.
Inputs may be any that keep to these rules, and one draw needn't show every extreme that they name: The 16 entries of each row of tile_cols differ. With a tile's receiving device taken as owner_slot[tile_cols[s, k]] // 4 and its sending device as s // 4, at most 8 tiles of one sending device go to one receiving device, and every sending device sends exactly 8 to some receiving device. Each block of unknowns has exactly one slot: owner_slot is a permutation.
All inputs are finite; a program needn't handle non-finite values.
Results may differ from the reference program's by a relative error of at most 0.005.
Values may be sent and summed in bfloat16 or wider, within the bound.
No kernel may reach another device: no remote copies, remote signals or barrier semaphores. Data moves between devices by JAX's collectives and lax.ppermute only.
A program may use at most 192 MiB of HBM per device.

```python
import math
import jax
import jax.numpy as jnp
from jax import lax

B = 1024
K = 16
RMAX = 96
R_DEV = 4
APPS = 4
NT = 32
S = 64


def route_helper(key):
    devices = NT // R_DEV
    keys = jax.random.split(jax.random.fold_in(key, 11), devices)
    orders = jax.vmap(lambda single: jax.random.permutation(single, devices))(keys).astype(jnp.int32)
    position = jnp.arange(R_DEV, dtype=jnp.int32)[:, None] * K + jnp.arange(K, dtype=jnp.int32)[None, :]
    wraps = position // devices
    reach = orders[:, position % devices]
    offset = jax.random.randint(jax.random.fold_in(key, 12), (devices, devices), 0, R_DEV).astype(jnp.int32)
    shifted = jnp.take_along_axis(offset, reach.reshape(devices, R_DEV * K), axis=1).reshape(devices, R_DEV, K)
    local = (wraps[None, :, :] + shifted) % R_DEV
    slots = (reach * R_DEV + local).reshape(NT, K)
    owner = jax.random.permutation(jax.random.fold_in(key, 13), NT).astype(jnp.int32)
    inverse = jnp.zeros((NT,), jnp.int32).at[owner].set(jnp.arange(NT, dtype=jnp.int32))
    return (inverse[slots], owner)


def draw_tile_cols(key, part):
    return route_helper(key)[0].astype(jnp.int32)


def draw_owner_slot(key, part):
    return route_helper(key)[1].astype(jnp.int32)


def touch_ends(values, key, smallest, high):
    longest = values.shape.index(max(values.shape))
    spots = []
    for shift in (0, 1):
        where = [jax.random.randint(jax.random.fold_in(key, axis), (), 0, length) for axis, length in enumerate(values.shape)]
        where[longest] = (where[longest] + shift) % values.shape[longest]
        spots.append(tuple(where))
    return values.at[spots[0]].set(smallest).at[spots[1]].set(high)


def block_levels(rng, shape, shards, least, top_value):
    def one(dim, shards_of):
        steps = jax.random.uniform(jax.random.fold_in(jax.random.fold_in(rng, 6), dim), (shards_of,), jnp.float32, least / len(shards), top_value / len(shards))
        return jnp.repeat(jnp.exp(steps), shape[dim] // shards_of).reshape((-1,) + (1,) * (len(shape) - dim - 1))

    factor_of = one(*shards[0])
    for cut in shards[1:]:
        factor_of = factor_of * one(*cut)
    return factor_of


def centred(stream_key, shape, scale, most, pieces=(), kind=jnp.bfloat16):
    result = scale * jax.random.normal(stream_key, shape, jnp.float32)
    if pieces:
        result = result * block_levels(stream_key, shape, pieces, -0.22, 0.18)
    return jnp.clip(result, -most, most).astype(kind)


def setup_inputs(seed: int = 0) -> dict:
    arg_keys = jax.random.split(jax.random.key(seed), 9)
    misfit = centred(arg_keys[0], (NT, S, B), 1.0, 6.0, ((0, 8), (1, 4)), jnp.float32)
    forward_fields = centred(arg_keys[1], (NT, S, B), 1.0, 6.0, ((0, 8), (1, 4)))
    contrast = jnp.clip(jnp.exp(math.log(0.6) - 1.0986123 * jax.random.uniform(arg_keys[2], (NT, B), jnp.float32) ** block_levels(arg_keys[2], (NT, B), ((0, 8),), -0.2, 0.2)), 0.2, 0.6)
    u_factors = centred(arg_keys[3], (NT, K, RMAX, B), B ** -0.5, 0.1875, ((0, 8),))
    v_factors = centred(arg_keys[4], (NT, K, RMAX, B), 0.03, 0.1796875, ((0, 8),))
    ranks = touch_ends(jax.random.randint(arg_keys[5], (NT, K), RMAX // 3, RMAX + 1), jax.random.fold_in(arg_keys[5], 1), RMAX // 3, RMAX).astype(jnp.int32)
    tile_cols = draw_tile_cols(jax.random.fold_in(arg_keys[8], 71), 0)
    owner_slot = draw_owner_slot(jax.random.fold_in(arg_keys[8], 71), 0)
    return {"misfit": misfit, "forward_fields": forward_fields, "contrast": contrast, "u_factors": u_factors, "v_factors": v_factors, "ranks": ranks, "tile_cols": tile_cols, "owner_slot": owner_slot}


def reference(misfit, forward_fields, contrast, u_factors, v_factors, ranks, tile_cols, owner_slot):
    target = owner_slot[tile_cols].astype(jnp.int32)
    keep = (jnp.arange(RMAX, dtype=jnp.int32)[None, None, :] < ranks[:, :, None]).astype(jnp.float32)
    field = misfit
    for step in range(APPS):
        low = field.astype(jnp.bfloat16)

        def add_row(total, row):
            u_row, v_row, keep_row, low_row, dest = row
            coeff = jnp.einsum('sb,krb->ksr', low_row.astype(jnp.float32), u_row.astype(jnp.float32))
            coeff = (coeff * keep_row[:, None, :]).astype(jnp.bfloat16)
            coeff = lax.optimization_barrier(coeff).astype(jnp.float32)
            terms = jnp.einsum('ksr,krb->ksb', coeff, v_row.astype(jnp.float32))
            return (total.at[dest].add(terms), None)
        total, unused = lax.scan(add_row, jnp.zeros(misfit.shape, jnp.float32), (u_factors, v_factors, keep, low, target))
        field = misfit + contrast[:, None, :] * total
    gradient = lax.optimization_barrier(jnp.sum(forward_fields.astype(jnp.float32) * field, axis=1)) * lax.rsqrt(jnp.float32(S))
    return (field, gradient)
```

```python
import functools

import jax
import jax.numpy as jnp
from jax import lax
from jax.experimental import pallas as pl
from jax.experimental.pallas import tpu as pltpu
from jax.sharding import PartitionSpec as P

APPS = 4
GROUP = 8


def sends(rows_dev, peers):
    bits = peers.bit_length() - 1
    near = list(range(bits))
    half = rows_dev // 2
    return [(half, near), (rows_dev - half, near[1:] + near[:1])]


def spot(bits_order, rel):
    place = 0
    for bit in bits_order:
        place = place * 2 + ((rel >> bit) & 1)
    return place


def tile_kernel(dims, first, *refs):
    rows_dev, tiles_row, rank_max, peers, plan = dims
    refs = list(refs)
    cols_ref, owner_ref, ranks_ref, contrast_ref, base_ref = refs[:5]
    if first:
        u_from, v_from = refs[5:7]
        outs, u_ref, v_ref, acc, u_sem, v_sem = refs[7:11], *refs[11:16]
    else:
        arrived, u_ref, v_ref = refs[5:7], *refs[7:9]
        outs, acc = refs[9:13], refs[13]
    here = lax.axis_index("rows")
    half = plan[0][0]
    width = GROUP * rank_max
    steps = rows_dev * (tiles_row // GROUP)

    def load(step, whence, to, sem):
        piece = pl.ds(step * width, width)
        return pltpu.make_async_copy(whence.at[piece], to.at[piece], sem.at[step])

    if first:
        for step in range(steps):
            load(step, u_from, u_ref, u_sem).start()
            load(step, v_from, v_ref, v_sem).start()
    acc[...] = jnp.zeros_like(acc)
    lane = lax.broadcasted_iota(jnp.int32, (base_ref.shape[1], width), 1)
    for step in range(steps):
        row, group = divmod(step, tiles_row // GROUP)
        if group == 0:
            field = base_ref[row]
            if not first:
                part = arrived[0][row] if row < half else arrived[1][row - half]
                field = field + contrast_ref[pl.ds(row, 1), :] * part.astype(jnp.float32)
            low = field.astype(jnp.bfloat16)
        piece = pl.ds(step * width, width)
        if first:
            load(step, u_from, u_ref, u_sem).wait()
        coeff = lax.dot_general(
            low, u_ref[piece, :], (((1,), (1,)), ((), ())), preferred_element_type=jnp.float32
        )
        blocks = []
        for i in range(GROUP):
            rank = ranks_ref[row, group * GROUP + i]
            inside = (lane >= i * rank_max) & (lane < i * rank_max + rank)
            blocks.append(jnp.where(inside, coeff, 0.0).astype(jnp.bfloat16))
        spread = jnp.concatenate(blocks, axis=0)
        if first:
            load(step, v_from, v_ref, v_sem).wait()
        terms = jnp.dot(spread, v_ref[piece, :], preferred_element_type=jnp.float32)
        sources = low.shape[0]
        for i in range(GROUP):
            slot = owner_ref[cols_ref[here * rows_dev + row, group * GROUP + i]]
            rel = jnp.bitwise_xor(slot // rows_dev, here)
            local = slot % rows_dev
            place = jnp.where(
                local < half,
                spot(plan[0][1], rel) * half + local,
                peers * half + spot(plan[1][1], rel) * (rows_dev - half) + local - half,
            )
            acc[place] += terms[i * sources : (i + 1) * sources]
    base = 0
    for part, (count, _) in enumerate(plan):
        kept = peers * count // 2
        outs[2 * part][...] = acc[base : base + kept]
        outs[2 * part + 1][...] = acc[base + kept : base + 2 * kept].astype(jnp.bfloat16)
        base += 2 * kept


def apply_tiles(plan, peers, cols, owner, ranks, contrast, base, arrived, u, v):
    rows_dev, tiles_row = ranks.shape
    rank_max = u.shape[0] // (rows_dev * tiles_row)
    sources, unknowns = base.shape[1:]
    first = arrived is None
    smem = pl.BlockSpec(memory_space=pltpu.SMEM)
    vmem = pl.BlockSpec(memory_space=pltpu.VMEM)
    outs = []
    for count, _ in plan:
        outs.append(jax.ShapeDtypeStruct((peers * count // 2, sources, unknowns), jnp.float32))
        outs.append(jax.ShapeDtypeStruct((peers * count // 2, sources, unknowns), jnp.bfloat16))
    scratch = [pltpu.VMEM((peers * rows_dev, sources, unknowns), jnp.float32)]
    if first:
        specs = [vmem] * 2 + [pl.BlockSpec(memory_space=pl.ANY)] * 2
        outs += [pltpu.VMEM(x.shape, x.dtype) for x in (u, v)]
        steps = rows_dev * tiles_row // GROUP
        scratch += [pltpu.SemaphoreType.DMA((steps,))] * 2
        extra = []
    else:
        specs = [vmem] * 6
        u, v = (pltpu.with_memory_space_constraint(x, pltpu.VMEM) for x in (u, v))
        extra = list(arrived)
    flops = 4 * u.shape[0] * unknowns * sources
    got = pl.pallas_call(
        functools.partial(tile_kernel, (rows_dev, tiles_row, rank_max, peers, plan), first),
        out_shape=outs,
        in_specs=[smem] * 3 + specs,
        out_specs=[vmem] * len(outs),
        scratch_shapes=scratch,
        compiler_params=pltpu.CompilerParams(vmem_limit_bytes=24 * 1024 * 1024),
        cost_estimate=pl.CostEstimate(flops=flops, bytes_accessed=4 * u.size, transcendentals=0),
    )(cols, owner, ranks, contrast, base, *extra, u, v)
    return got[:4], got[4:]


def swap(x, bit, peers):
    return lax.ppermute(x, "rows", [(i, i ^ (1 << bit)) for i in range(peers)])


def slot_sums(misfit, contrast, u_factors, v_factors, ranks, tile_cols, owner_slot):
    peers = lax.axis_size("rows")
    rows_dev = ranks.shape[0]
    unknowns = misfit.shape[-1]
    plan = sends(rows_dev, peers)
    factors = [x.reshape(-1, unknowns) for x in (u_factors, v_factors)]
    base, arrived = misfit, None
    for step in range(APPS):
        got, held = apply_tiles(
            plan, peers, tile_cols, owner_slot, ranks, contrast, base, arrived, *factors
        )
        factors = held or factors
        keeps, goes = [got[0], got[2]], [got[1], got[3]]
        for level in range(len(plan[0][1])):
            came = [swap(goes[p], plan[p][1][level], peers) for p in range(2)]
            if level == len(plan[0][1]) - 1:
                break
            for p in range(2):
                mid = keeps[p].shape[0] // 2
                goes[p] = (keeps[p][mid:] + came[p][mid:].astype(jnp.float32)).astype(jnp.bfloat16)
                keeps[p] = keeps[p][:mid] + came[p][:mid].astype(jnp.float32)
        base = misfit + contrast[:, None, :] * jnp.concatenate(keeps, axis=0)
        arrived = came
    return base + contrast[:, None, :] * jnp.concatenate(arrived, axis=0).astype(jnp.float32)


def route_tiles(tile_cols, owner_slot, rows_dev, peers):
    tiles = rows_dev * tile_cols.shape[1]
    target_slot = owner_slot[tile_cols.reshape(peers, tiles)]
    target_dev = target_slot // rows_dev
    local_slot = target_slot % rows_dev
    same = target_dev[:, :, None] == target_dev[:, None, :]
    before = jnp.arange(tiles)[None, :] < jnp.arange(tiles)[:, None]
    order = jnp.sum(jnp.where(same & before[None, :, :], 1, 0), axis=2).astype(jnp.int32)
    return target_dev, local_slot, order


def tile_terms(misfit, contrast, u_factors, v_factors, ranks, tile_cols, owner_slot):
    rows_dev, tiles_row, rank_max, unknowns = u_factors.shape
    tiles = rows_dev * tiles_row
    peers = lax.axis_size("rows")
    cap = (tiles + peers - 1) // peers
    sources = misfit.shape[1]
    here = lax.axis_index("rows")
    target_dev, local_slot, order = route_tiles(tile_cols, owner_slot, rows_dev, peers)
    mine_dev = lax.dynamic_index_in_dim(target_dev, here, 0, keepdims=False)
    mine_order = lax.dynamic_index_in_dim(order, here, 0, keepdims=False)
    box = mine_dev * cap + mine_order
    sender = jnp.arange(peers, dtype=jnp.int32)[:, None] * cap + order
    entry = jnp.where(target_dev == here, sender, peers * cap).reshape(-1)
    arrival = (
        jnp.full((peers * cap,), -1, jnp.int32).at[entry].set(local_slot.reshape(-1), mode="drop")
    )
    pick = (arrival[:, None] == jnp.arange(rows_dev, dtype=jnp.int32)[None, :]).astype(jnp.float32)
    keep = (jnp.arange(rank_max, dtype=jnp.int32)[None, None, :] < ranks[:, :, None]).astype(
        jnp.float32
    )
    field = misfit
    for step in range(APPS):
        coeff = jnp.einsum(
            "lsb,lkrb->lksr",
            field.astype(jnp.bfloat16),
            u_factors,
            preferred_element_type=jnp.float32,
        )
        tile_coeff = (coeff * keep[:, :, None, :]).astype(jnp.bfloat16)
        terms = jnp.einsum(
            "lksr,lkrb->lksb", tile_coeff, v_factors, preferred_element_type=jnp.float32
        )
        terms = terms.reshape(tiles, sources, unknowns)
        outgoing = jnp.zeros((peers * cap, sources, unknowns), jnp.float32).at[box].set(terms)
        incoming = lax.all_to_all(
            outgoing.reshape(peers, cap, sources, unknowns).astype(jnp.bfloat16),
            "rows",
            split_axis=0,
            concat_axis=0,
            tiled=True,
        ).astype(jnp.float32)
        field = misfit + contrast[:, None, :] * jnp.einsum(
            "eq,esb->qsb",
            pick,
            incoming.reshape(peers * cap, sources, unknowns),
            precision=lax.Precision.HIGHEST,
        )
    return field


def src_sum(x):
    count = lax.axis_size("src")
    if count & (count - 1):
        return lax.psum(x, "src")
    terms = [x]
    for step in range(1, count):
        terms.append(lax.ppermute(x, "src", [(i, i ^ step) for i in range(count)]))
    while len(terms) > 1:
        terms = [a + b for a, b in zip(terms[::2], terms[1::2])]
    return terms[0]


def per_device(
    misfit, forward_fields, contrast, u_factors, v_factors, ranks, tile_cols, owner_slot
):
    rows_dev, tiles_row = ranks.shape
    peers = lax.axis_size("rows")
    dense = (
        peers & (peers - 1) == 0
        and peers > 1
        and rows_dev % 2 == 0
        and tiles_row % GROUP == 0
        and peers <= tiles_row
    )
    run = slot_sums if dense else tile_terms
    field = run(misfit, contrast, u_factors, v_factors, ranks, tile_cols, owner_slot)
    partial_sum = jnp.sum(forward_fields.astype(jnp.float32) * field, axis=1)
    total = src_sum(partial_sum)
    sources = misfit.shape[1] * lax.axis_size("src")
    gradient = total * lax.rsqrt(jnp.float32(sources))
    return (field, gradient)


def solution(mesh):
    placed = (
        P("rows", "src", None),
        P("rows", "src", None),
        P("rows", None),
        P("rows", None, None, None),
        P("rows", None, None, None),
        P("rows", None),
        P(),
        P(),
    )
    return jax.shard_map(
        per_device,
        mesh=mesh,
        in_specs=placed,
        out_specs=(P("rows", "src", None), P("rows", None)),
        check_vma=False,
    )
```

```python
import functools

import jax
import jax.numpy as jnp
from jax import lax
from jax.experimental import pallas as pl
from jax.experimental.pallas import tpu as pltpu
from jax.sharding import PartitionSpec as P

APPS = 4
GROUP = 8


def sends(rows_dev, peers):
    bits = peers.bit_length() - 1
    near = list(range(bits))
    half = rows_dev // 2
    return [(half, near), (rows_dev - half, near[1:] + near[:1])]


def spot(bits_order, rel):
    place = 0
    for bit in bits_order:
        place = place * 2 + ((rel >> bit) & 1)
    return place


def tile_kernel(dims, first, *refs):
    rows_dev, tiles_row, rank_max, peers, plan = dims
    refs = list(refs)
    cols_ref, owner_ref, ranks_ref, contrast_ref, base_ref = refs[:5]
    if first:
        u_from, v_from = refs[5:7]
        outs, u_ref, v_ref, acc, u_sem, v_sem = refs[7:8], *refs[8:13]
    else:
        arrived, u_ref, v_ref = refs[5:6], *refs[6:8]
        outs, acc = refs[8:9], refs[9]
    here = lax.axis_index("rows")
    half = plan[0][0]
    width = GROUP * rank_max
    steps = rows_dev * (tiles_row // GROUP)

    def load(step, whence, to, sem):
        piece = pl.ds(step * width, width)
        return pltpu.make_async_copy(whence.at[piece], to.at[piece], sem.at[step])

    if first:
        for step in range(steps):
            load(step, u_from, u_ref, u_sem).start()
            load(step, v_from, v_ref, v_sem).start()
    acc[...] = jnp.zeros_like(acc)
    lane = lax.broadcasted_iota(jnp.int32, (base_ref.shape[1], width), 1)
    for step in range(steps):
        row, group = divmod(step, tiles_row // GROUP)
        if group == 0:
            field = base_ref[row]
            if not first:
                part = arrived[0][row].astype(jnp.float32)
                field = field + contrast_ref[pl.ds(row, 1), :] * part
            low = field.astype(jnp.bfloat16)
        piece = pl.ds(step * width, width)
        if first:
            load(step, u_from, u_ref, u_sem).wait()
        coeff = lax.dot_general(
            low, u_ref[piece, :], (((1,), (1,)), ((), ())), preferred_element_type=jnp.float32
        )
        blocks = []
        for i in range(GROUP):
            rank = ranks_ref[row, group * GROUP + i]
            inside = (lane >= i * rank_max) & (lane < i * rank_max + rank)
            blocks.append(jnp.where(inside, coeff, 0.0).astype(jnp.bfloat16))
        spread = jnp.concatenate(blocks, axis=0)
        if first:
            load(step, v_from, v_ref, v_sem).wait()
        terms = jnp.dot(spread, v_ref[piece, :], preferred_element_type=jnp.float32)
        sources = low.shape[0]
        for i in range(GROUP):
            slot = owner_ref[cols_ref[here * rows_dev + row, group * GROUP + i]]
            place = slot
            acc[place] += terms[i * sources : (i + 1) * sources]
    outs[0][...] = acc[...].astype(jnp.bfloat16)


def apply_tiles(plan, peers, cols, owner, ranks, contrast, base, arrived, u, v):
    rows_dev, tiles_row = ranks.shape
    rank_max = u.shape[0] // (rows_dev * tiles_row)
    sources, unknowns = base.shape[1:]
    first = arrived is None
    smem = pl.BlockSpec(memory_space=pltpu.SMEM)
    vmem = pl.BlockSpec(memory_space=pltpu.VMEM)
    outs = []
    outs.append(jax.ShapeDtypeStruct((peers * rows_dev, sources, unknowns), jnp.bfloat16))
    scratch = [pltpu.VMEM((peers * rows_dev, sources, unknowns), jnp.float32)]
    if first:
        specs = [vmem] * 2 + [pl.BlockSpec(memory_space=pl.ANY)] * 2
        outs += [pltpu.VMEM(x.shape, x.dtype) for x in (u, v)]
        steps = rows_dev * tiles_row // GROUP
        scratch += [pltpu.SemaphoreType.DMA((steps,))] * 2
        extra = []
    else:
        specs = [vmem] * 5
        u, v = (pltpu.with_memory_space_constraint(x, pltpu.VMEM) for x in (u, v))
        extra = list(arrived)
    flops = 4 * u.shape[0] * unknowns * sources
    got = pl.pallas_call(
        functools.partial(tile_kernel, (rows_dev, tiles_row, rank_max, peers, plan), first),
        out_shape=outs,
        in_specs=[smem] * 3 + specs,
        out_specs=[vmem] * len(outs),
        scratch_shapes=scratch,
        compiler_params=pltpu.CompilerParams(vmem_limit_bytes=24 * 1024 * 1024),
        cost_estimate=pl.CostEstimate(flops=flops, bytes_accessed=4 * u.size, transcendentals=0),
    )(cols, owner, ranks, contrast, base, *extra, u, v)
    return got[:1], got[1:]


def swap(x, bit, peers):
    return lax.ppermute(x, "rows", [(i, i ^ (1 << bit)) for i in range(peers)])


def slot_sums(misfit, contrast, u_factors, v_factors, ranks, tile_cols, owner_slot):
    peers = lax.axis_size("rows")
    rows_dev = ranks.shape[0]
    unknowns = misfit.shape[-1]
    plan = sends(rows_dev, peers)
    factors = [x.reshape(-1, unknowns) for x in (u_factors, v_factors)]
    base, arrived = misfit, None
    for step in range(APPS):
        got, held = apply_tiles(
            plan, peers, tile_cols, owner_slot, ranks, contrast, misfit, arrived, *factors
        )
        factors = held or factors
        total = lax.psum_scatter(got[0], "rows", scatter_dimension=0, tiled=True)
        arrived = (total,)
    return misfit + contrast[:, None, :] * total.astype(jnp.float32)


def route_tiles(tile_cols, owner_slot, rows_dev, peers):
    tiles = rows_dev * tile_cols.shape[1]
    target_slot = owner_slot[tile_cols.reshape(peers, tiles)]
    target_dev = target_slot // rows_dev
    local_slot = target_slot % rows_dev
    same = target_dev[:, :, None] == target_dev[:, None, :]
    before = jnp.arange(tiles)[None, :] < jnp.arange(tiles)[:, None]
    order = jnp.sum(jnp.where(same & before[None, :, :], 1, 0), axis=2).astype(jnp.int32)
    return target_dev, local_slot, order


def tile_terms(misfit, contrast, u_factors, v_factors, ranks, tile_cols, owner_slot):
    rows_dev, tiles_row, rank_max, unknowns = u_factors.shape
    tiles = rows_dev * tiles_row
    peers = lax.axis_size("rows")
    cap = (tiles + peers - 1) // peers
    sources = misfit.shape[1]
    here = lax.axis_index("rows")
    target_dev, local_slot, order = route_tiles(tile_cols, owner_slot, rows_dev, peers)
    mine_dev = lax.dynamic_index_in_dim(target_dev, here, 0, keepdims=False)
    mine_order = lax.dynamic_index_in_dim(order, here, 0, keepdims=False)
    box = mine_dev * cap + mine_order
    sender = jnp.arange(peers, dtype=jnp.int32)[:, None] * cap + order
    entry = jnp.where(target_dev == here, sender, peers * cap).reshape(-1)
    arrival = (
        jnp.full((peers * cap,), -1, jnp.int32).at[entry].set(local_slot.reshape(-1), mode="drop")
    )
    pick = (arrival[:, None] == jnp.arange(rows_dev, dtype=jnp.int32)[None, :]).astype(jnp.float32)
    keep = (jnp.arange(rank_max, dtype=jnp.int32)[None, None, :] < ranks[:, :, None]).astype(
        jnp.float32
    )
    field = misfit
    for step in range(APPS):
        coeff = jnp.einsum(
            "lsb,lkrb->lksr",
            field.astype(jnp.bfloat16),
            u_factors,
            preferred_element_type=jnp.float32,
        )
        tile_coeff = (coeff * keep[:, :, None, :]).astype(jnp.bfloat16)
        terms = jnp.einsum(
            "lksr,lkrb->lksb", tile_coeff, v_factors, preferred_element_type=jnp.float32
        )
        terms = terms.reshape(tiles, sources, unknowns)
        outgoing = jnp.zeros((peers * cap, sources, unknowns), jnp.float32).at[box].set(terms)
        incoming = lax.all_to_all(
            outgoing.reshape(peers, cap, sources, unknowns).astype(jnp.bfloat16),
            "rows",
            split_axis=0,
            concat_axis=0,
            tiled=True,
        ).astype(jnp.float32)
        field = misfit + contrast[:, None, :] * jnp.einsum(
            "eq,esb->qsb",
            pick,
            incoming.reshape(peers * cap, sources, unknowns),
            precision=lax.Precision.HIGHEST,
        )
    return field


def src_sum(x):
    count = lax.axis_size("src")
    if count & (count - 1):
        return lax.psum(x, "src")
    terms = [x]
    for step in range(1, count):
        terms.append(lax.ppermute(x, "src", [(i, i ^ step) for i in range(count)]))
    while len(terms) > 1:
        terms = [a + b for a, b in zip(terms[::2], terms[1::2])]
    return terms[0]


def per_device(
    misfit, forward_fields, contrast, u_factors, v_factors, ranks, tile_cols, owner_slot
):
    rows_dev, tiles_row = ranks.shape
    peers = lax.axis_size("rows")
    dense = (
        peers & (peers - 1) == 0
        and peers > 1
        and rows_dev % 2 == 0
        and tiles_row % GROUP == 0
        and peers <= tiles_row
    )
    run = slot_sums if dense else tile_terms
    field = run(misfit, contrast, u_factors, v_factors, ranks, tile_cols, owner_slot)
    partial_sum = jnp.sum(forward_fields.astype(jnp.float32) * field, axis=1)
    total = src_sum(partial_sum)
    sources = misfit.shape[1] * lax.axis_size("src")
    gradient = total * lax.rsqrt(jnp.float32(sources))
    return (field, gradient)


def solution(mesh):
    placed = (
        P("rows", "src", None),
        P("rows", "src", None),
        P("rows", None),
        P("rows", None, None, None),
        P("rows", None, None, None),
        P("rows", None),
        P(),
        P(),
    )
    return jax.shard_map(
        per_device,
        mesh=mesh,
        in_specs=placed,
        out_specs=(P("rows", "src", None), P("rows", None)),
        check_vma=False,
    )
```

```python
import functools

import jax
import jax.numpy as jnp
from jax import lax
from jax.experimental import pallas as pl
from jax.experimental.pallas import tpu as pltpu
from jax.sharding import PartitionSpec as P

APPS = 4

def parts_of(unknowns, peers):
    bits = list(range(peers.bit_length() - 1))
    near, far = bits, bits[1:] + bits[:1]
    width = unknowns // 4
    return [(i * width, width, far if i == 3 else near) for i in range(4)]


def spot(order, rel):
    place = 0
    for bit in order:
        place = place * 2 + ((rel >> bit) & 1)
    return place


def in_order(order, peers):
    return sorted(range(peers), key=lambda rel: spot(order, rel))


def vmem(count):
    return [pl.BlockSpec(memory_space=pltpu.VMEM)] * count


def params():
    return pltpu.CompilerParams(vmem_limit_bytes=24 * 1024 * 1024)


def cost(rows, columns, sources):
    return pl.CostEstimate(
        flops=2 * rows * columns * sources, bytes_accessed=2 * rows * columns, transcendentals=0
    )


def in_vmem(x):
    return pltpu.with_memory_space_constraint(x, pltpu.VMEM)


def in_hbm(x):
    return pltpu.with_memory_space_constraint(x, pltpu.HBM)


def pick_rows(every, code, sources, rows_dev):
    row = code // rows_dev
    total = jnp.zeros((sources, every.shape[1]), jnp.float32)
    for index in range(rows_dev):
        mine = every[index * sources : (index + 1) * sources]
        total = total + jnp.where(row == index, mine, 0.0)
    return total


def by_slot(coeff, code, rows_dev):
    local = code % rows_dev
    low = [
        jnp.where(local == index, coeff, 0.0).astype(jnp.bfloat16) for index in range(rows_dev)
    ]
    return jnp.concatenate(low, axis=0)


def times_u(low, factors):
    return lax.dot_general(
        low, factors, (((1,), (1,)), ((), ())), preferred_element_type=jnp.float32
    )


def put_terms(lhs, v_ref, group, part, outs, rows_dev, peers):
    first, width, order = part
    deep = lhs.shape[1]
    terms = jnp.dot(
        lhs,
        v_ref[pl.ds(group * deep, deep), pl.ds(first, width)],
        preferred_element_type=jnp.float32,
    )
    place = spot(order, group)
    out = outs[place >= peers // 2]
    place = place % (peers // 2) * rows_dev
    out[place : place + rows_dev] = terms.reshape(rows_dev, -1, width).astype(out.dtype)


def start_kernel(dims, *refs):
    rows_dev, tiles_row, rank_max, peers, parts = dims
    cols_hbm, owner_hbm, ranks_hbm, misfit_hbm, u_hbm, v_hbm = refs[:6]
    u_ref, v_ref, code_ref = refs[6:9]
    outs = refs[9 : 9 + 2 * len(parts)]
    cols, owner, ranks, misfit, tile_at, code_at, rank_at, count, small, u_sem, v_sem = refs[
        9 + 2 * len(parts) :
    ]
    here = lax.axis_index("rows")
    tiles = rows_dev * tiles_row
    group_tiles = tiles // peers
    deep = group_tiles * rank_max
    sources = misfit.shape[1]
    copies = [
        pltpu.make_async_copy(whence, to, small.at[i])
        for i, (whence, to) in enumerate(
            zip((cols_hbm, owner_hbm, ranks_hbm, misfit_hbm), (cols, owner, ranks, misfit))
        )
    ]
    for copy in copies:
        copy.start()
    for rel in range(peers):
        count[rel] = 0
    for copy in copies[:3]:
        copy.wait()

    def sort_tile(tile, carry):
        row, k = lax.div(tile, tiles_row), lax.rem(tile, tiles_row)
        slot = owner[cols[k, here * rows_dev + row]]
        rel = jnp.bitwise_xor(lax.div(slot, rows_dev), here)
        at = rel * group_tiles + count[rel]
        count[rel] = count[rel] + 1
        tile_at[at] = tile
        code_at[at] = row * rows_dev + lax.rem(slot, rows_dev)
        rank_at[at] = ranks[row, k]
        return carry

    lax.fori_loop(0, tiles, sort_tile, 0)

    def load(whence, to, sem, group):
        def one(i, carry):
            at = group * group_tiles + i
            pltpu.make_async_copy(
                whence.at[pl.ds(pl.multiple_of(tile_at[at] * rank_max, rank_max), rank_max)],
                to.at[pl.ds(pl.multiple_of(at * rank_max, rank_max), rank_max)],
                sem.at[group],
            ).start()
            return carry

        lax.fori_loop(0, group_tiles, one, 0)

    def loaded(ref, sem, group):
        piece = ref.at[pl.ds(group * deep, deep)]
        pltpu.make_async_copy(piece, piece, sem.at[group]).wait()

    for group in range(peers):
        load(u_hbm, u_ref, u_sem, group)
        load(v_hbm, v_ref, v_sem, group)
    lane = lax.broadcasted_iota(jnp.int32, (1, deep), 1)
    for group in range(peers):
        code = jnp.full((1, deep), -1, jnp.int32)
        for i in range(group_tiles):
            at = group * group_tiles + i
            inside = (lane >= i * rank_max) & (lane < i * rank_max + rank_at[at])
            code = jnp.where(inside, code_at[at], code)
        code_ref[pl.ds(group, 1), :] = code
    copies[3].wait()
    low = misfit[...].astype(jnp.bfloat16).reshape(rows_dev * sources, -1)
    for group in range(peers):
        loaded(u_ref, u_sem, group)
        code = code_ref[pl.ds(group, 1), :]
        every = times_u(low, u_ref[pl.ds(group * deep, deep), :])
        lhs = by_slot(pick_rows(every, code, sources, rows_dev), code, rows_dev)
        loaded(v_ref, v_sem, group)
        for i, part in enumerate(parts):
            put_terms(lhs, v_ref, group, part, outs[2 * i : 2 * i + 2], rows_dev, peers)


def low_field(base_ref, came_ref, contrast_ref, part):
    first, width, _ = part
    rows = []
    for row in range(base_ref.shape[0]):
        scale = contrast_ref[pl.ds(row, 1), pl.ds(first, width)]
        field = base_ref[row] + scale * came_ref[row].astype(jnp.float32)
        rows.append(field.astype(jnp.bfloat16))
    return jnp.concatenate(rows, axis=0)


def early_kernel(dims, parts, code_ref, contrast_ref, *refs):
    rows_dev, peers = dims
    fields, (u_ref, out_ref) = refs[: 2 * len(parts)], refs[2 * len(parts) :]
    deep = code_ref.shape[1]
    sources = out_ref.shape[1]
    lows = [
        low_field(fields[2 * i], fields[2 * i + 1], contrast_ref, part)
        for i, part in enumerate(parts)
    ]
    for group in range(peers):
        every = 0.0
        for low, (first, width, _) in zip(lows, parts):
            every = every + times_u(low, u_ref[pl.ds(group * deep, deep), pl.ds(first, width)])
        code = code_ref[pl.ds(group, 1), :]
        out_ref[group] = pick_rows(every, code, sources, rows_dev)


def ready_kernel(dims, late, parts, code_ref, contrast_ref, sum_ref, base_ref, came_ref, *refs):
    rows_dev, peers = dims
    u_ref, v_ref, lhs_ref = refs[:3]
    outs = refs[3:]
    deep = code_ref.shape[1]
    sources = sum_ref.shape[1]
    low = low_field(base_ref, came_ref, contrast_ref, late)
    first, width, _ = late
    for group in reversed(range(peers)):
        every = times_u(low, u_ref[pl.ds(group * deep, deep), pl.ds(first, width)])
        code = code_ref[pl.ds(group, 1), :]
        coeff = sum_ref[group] + pick_rows(every, code, sources, rows_dev)
        lhs = by_slot(coeff, code, rows_dev)
        lhs_ref[group] = lhs
        for out, part in zip(outs, parts):
            if spot(part[2], group) >= peers // 2:
                put_terms(lhs, v_ref, group, part, (None, out), rows_dev, peers)


def rest_kernel(dims, sent, parts, lhs_ref, v_ref, *refs):
    rows_dev, peers = dims
    sends = refs[: len(sent)]
    keeps = refs[len(sent) :]
    for out, i in zip(sends, sent):
        for group in in_order(parts[i][2], peers)[peers // 2 :]:
            put_terms(lhs_ref[group], v_ref, group, parts[i], (None, out), rows_dev, peers)
    for keep, part in zip(keeps, parts):
        for group in in_order(part[2], peers)[: peers // 2]:
            put_terms(lhs_ref[group], v_ref, group, part, (keep, None), rows_dev, peers)


def finish_kernel(parts, contrast_ref, forward_ref, *refs):
    fields, (field_ref, total_ref) = refs[: 2 * len(parts)], refs[2 * len(parts) :]
    for i, (first, width, _) in enumerate(parts):
        here = pl.ds(first, width)
        for row in range(field_ref.shape[0]):
            scale = contrast_ref[pl.ds(row, 1), here]
            field = fields[2 * i][row] + scale * fields[2 * i + 1][row].astype(jnp.float32)
            field_ref[row, :, here] = field
            product = forward_ref[row, :, here].astype(jnp.float32) * field
            total_ref[pl.ds(row, 1), here] = jnp.sum(product, axis=0, keepdims=True)


def swap(x, bit, peers):
    return lax.ppermute(x, "rows", [(i, i ^ (1 << bit)) for i in range(peers)])


def slot_sums(
    misfit, forward_fields, contrast, u_factors, v_factors, ranks, tile_cols, owner_slot
):
    peers = lax.axis_size("rows")
    rows_dev, tiles_row, rank_max, unknowns = u_factors.shape
    sources = misfit.shape[1]
    tiles = rows_dev * tiles_row
    deep = tiles // peers * rank_max
    parts = parts_of(unknowns, peers)
    first_sent, then_sent, late = [0, 3], [1, 2], 2
    early = [i for i in range(len(parts)) if i != late]
    half = (peers // 2 * rows_dev, sources)
    sent = [jax.ShapeDtypeStruct((*half, part[1]), jnp.bfloat16) for part in parts]
    kept = [jax.ShapeDtypeStruct((*half, part[1]), jnp.float32) for part in parts]
    u, v = (x.reshape(tiles * rank_max, unknowns) for x in (u_factors, v_factors))
    hbm = [pl.BlockSpec(memory_space=pl.ANY)]
    smem = lambda *shape: pltpu.SMEM(shape, jnp.int32)
    u, v, code, *got = pl.pallas_call(
        functools.partial(start_kernel, (rows_dev, tiles_row, rank_max, peers, parts)),
        out_shape=[pltpu.VMEM(x.shape, x.dtype) for x in (u, v)]
        + [jax.ShapeDtypeStruct((peers, deep), jnp.int32)]
        + [x for pair in zip(kept, sent) for x in pair],
        in_specs=hbm * 6,
        out_specs=vmem(3 + 2 * len(parts)),
        scratch_shapes=[
            smem(*tile_cols.shape[::-1]),
            smem(*owner_slot.shape),
            smem(*ranks.shape),
            pltpu.VMEM(misfit.shape, misfit.dtype),
            smem(tiles),
            smem(tiles),
            smem(tiles),
            smem(peers),
            pltpu.SemaphoreType.DMA((4,)),
            pltpu.SemaphoreType.DMA((peers,)),
            pltpu.SemaphoreType.DMA((peers,)),
        ],
        compiler_params=params(),
        cost_estimate=cost(2 * tiles * rank_max, unknowns, sources),
        name="start",
    )(*(in_hbm(x) for x in (tile_cols.T, owner_slot, ranks, misfit, u, v)))
    dims = (rows_dev, peers)
    scale = contrast[:, None, :]
    columns = [(slice(None), slice(None), slice(part[0], part[0] + part[1])) for part in parts]
    for step in range(APPS):
        if step == 0:
            keeps, goes = list(got[::2]), list(got[1::2])
        else:
            coeff = pl.pallas_call(
                functools.partial(early_kernel, dims, [parts[i] for i in early]),
                out_shape=jax.ShapeDtypeStruct((peers, sources, deep), jnp.float32),
                in_specs=vmem(3 + 2 * len(early)),
                out_specs=vmem(1)[0],
                compiler_params=params(),
                cost_estimate=cost(u.shape[0], unknowns * 3 // 4, sources),
                name="early",
            )(code, contrast, *(x for i in early for x in (base[i], came[i])), in_vmem(u))
            lhs, *some = pl.pallas_call(
                functools.partial(ready_kernel, dims, parts[late], [parts[i] for i in first_sent]),
                out_shape=[jax.ShapeDtypeStruct((peers, rows_dev * sources, deep), jnp.bfloat16)]
                + [sent[i] for i in first_sent],
                in_specs=vmem(7),
                out_specs=vmem(1 + len(first_sent)),
                compiler_params=params(),
                cost_estimate=cost(u.shape[0], unknowns // 2, sources),
                name="ready",
            )(code, contrast, coeff, base[late], came[late], in_vmem(u), in_vmem(v))
            rest = pl.pallas_call(
                functools.partial(rest_kernel, dims, then_sent, parts),
                out_shape=[sent[i] for i in then_sent] + kept,
                in_specs=vmem(2),
                out_specs=vmem(len(then_sent) + len(parts)),
                compiler_params=params(),
                cost_estimate=cost(u.shape[0], unknowns * 3 // 4, sources),
                name="rest",
            )(lhs, in_vmem(v))
            goes = [None] * len(parts)
            for i, x in zip(first_sent + then_sent, [*some, *rest[: len(then_sent)]]):
                goes[i] = x
            keeps = list(rest[len(then_sent) :])
        base, came = [None] * len(parts), [None] * len(parts)
        levels = len(parts[0][2])
        for level in range(levels):
            for i, part in enumerate(parts):
                came[i] = swap(goes[i], part[2][level], peers)
                if level < levels - 1:
                    mid = keeps[i].shape[0] // 2
                    goes[i] = keeps[i][mid:] + came[i][mid:].astype(jnp.float32)
                    goes[i] = goes[i].astype(jnp.bfloat16)
                    keeps[i] = keeps[i][:mid] + came[i][:mid].astype(jnp.float32)
        for i in range(len(parts)):
            base[i] = misfit[columns[i]] + scale[columns[i]] * keeps[i]
    return pl.pallas_call(
        functools.partial(finish_kernel, parts),
        out_shape=[
            jax.ShapeDtypeStruct(misfit.shape, jnp.float32),
            jax.ShapeDtypeStruct(contrast.shape, jnp.float32),
        ],
        in_specs=vmem(2 + 2 * len(parts)),
        out_specs=vmem(2),
        compiler_params=params(),
        name="finish",
    )(contrast, forward_fields, *(x for pair in zip(base, came) for x in pair))


def route_tiles(tile_cols, owner_slot, rows_dev, peers):
    tiles = rows_dev * tile_cols.shape[1]
    target_slot = owner_slot[tile_cols.reshape(peers, tiles)]
    target_dev = target_slot // rows_dev
    local_slot = target_slot % rows_dev
    same = target_dev[:, :, None] == target_dev[:, None, :]
    before = jnp.arange(tiles)[None, :] < jnp.arange(tiles)[:, None]
    order = jnp.sum(jnp.where(same & before[None, :, :], 1, 0), axis=2).astype(jnp.int32)
    return target_dev, local_slot, order


def tile_terms(
    misfit, forward_fields, contrast, u_factors, v_factors, ranks, tile_cols, owner_slot
):
    rows_dev, tiles_row, rank_max, unknowns = u_factors.shape
    tiles = rows_dev * tiles_row
    peers = lax.axis_size("rows")
    cap = (tiles + peers - 1) // peers
    sources = misfit.shape[1]
    here = lax.axis_index("rows")
    target_dev, local_slot, order = route_tiles(tile_cols, owner_slot, rows_dev, peers)
    mine_dev = lax.dynamic_index_in_dim(target_dev, here, 0, keepdims=False)
    mine_order = lax.dynamic_index_in_dim(order, here, 0, keepdims=False)
    box = mine_dev * cap + mine_order
    sender = jnp.arange(peers, dtype=jnp.int32)[:, None] * cap + order
    entry = jnp.where(target_dev == here, sender, peers * cap).reshape(-1)
    arrival = (
        jnp.full((peers * cap,), -1, jnp.int32).at[entry].set(local_slot.reshape(-1), mode="drop")
    )
    pick = (arrival[:, None] == jnp.arange(rows_dev, dtype=jnp.int32)[None, :]).astype(jnp.float32)
    keep = (jnp.arange(rank_max, dtype=jnp.int32)[None, None, :] < ranks[:, :, None]).astype(
        jnp.float32
    )
    field = misfit
    for step in range(APPS):
        coeff = jnp.einsum(
            "lsb,lkrb->lksr",
            field.astype(jnp.bfloat16),
            u_factors,
            preferred_element_type=jnp.float32,
        )
        tile_coeff = (coeff * keep[:, :, None, :]).astype(jnp.bfloat16)
        terms = jnp.einsum(
            "lksr,lkrb->lksb", tile_coeff, v_factors, preferred_element_type=jnp.float32
        )
        terms = terms.reshape(tiles, sources, unknowns)
        outgoing = jnp.zeros((peers * cap, sources, unknowns), jnp.float32).at[box].set(terms)
        incoming = lax.all_to_all(
            outgoing.reshape(peers, cap, sources, unknowns).astype(jnp.bfloat16),
            "rows",
            split_axis=0,
            concat_axis=0,
            tiled=True,
        ).astype(jnp.float32)
        field = misfit + contrast[:, None, :] * jnp.einsum(
            "eq,esb->qsb",
            pick,
            incoming.reshape(peers * cap, sources, unknowns),
            precision=lax.Precision.HIGHEST,
        )
    return field, jnp.sum(forward_fields.astype(jnp.float32) * field, axis=1)


def src_sum(x):
    count = lax.axis_size("src")
    if count & (count - 1):
        return lax.psum(x, "src")
    terms = [x]
    for step in range(1, count):
        terms.append(lax.ppermute(x, "src", [(i, i ^ step) for i in range(count)]))
    while len(terms) > 1:
        terms = [a + b for a, b in zip(terms[::2], terms[1::2])]
    return terms[0]


def per_device(
    misfit, forward_fields, contrast, u_factors, v_factors, ranks, tile_cols, owner_slot
):
    rows_dev, tiles_row = ranks.shape
    peers = lax.axis_size("rows")
    tiles = rows_dev * tiles_row
    cap = (tiles + peers - 1) // peers
    dense = (
        peers > 1
        and peers & (peers - 1) == 0
        and tiles == cap * peers
        and cap >= rows_dev
        and cap * u_factors.shape[2] % 128 == 0
        and misfit.shape[2] % 512 == 0
        and misfit.shape[1] % 16 == 0
    )
    run = slot_sums if dense else tile_terms
    field, partial_sum = run(
        misfit, forward_fields, contrast, u_factors, v_factors, ranks, tile_cols, owner_slot
    )
    total = src_sum(partial_sum)
    sources = misfit.shape[1] * lax.axis_size("src")
    gradient = total * lax.rsqrt(jnp.float32(sources))
    return (field, gradient)


def solution(mesh):
    placed = (
        P("rows", "src", None),
        P("rows", "src", None),
        P("rows", None),
        P("rows", None, None, None),
        P("rows", None, None, None),
        P("rows", None),
        P(),
        P(),
    )
    return jax.shard_map(
        per_device,
        mesh=mesh,
        in_specs=placed,
        out_specs=(P("rows", "src", None), P("rows", None)),
        check_vma=False,
    )
```

```python
import functools

import jax
import jax.numpy as jnp
from jax import lax
from jax.experimental import pallas as pl
from jax.experimental.pallas import tpu as pltpu
from jax.sharding import PartitionSpec as P

APPS = 4

def parts_of(unknowns, peers):
    bits = list(range(peers.bit_length() - 1))
    turned = bits[1:2] + bits[:1] + bits[2:]
    width = unknowns // 2
    return [(0, width, bits), (width, width, turned)]


def spot(order, rel):
    place = 0
    for bit in order:
        place = place * 2 + ((rel >> bit) & 1)
    return place


def in_order(order, peers):
    return sorted(range(peers), key=lambda rel: spot(order, rel))


def vmem(count):
    return [pl.BlockSpec(memory_space=pltpu.VMEM)] * count


def params():
    return pltpu.CompilerParams(vmem_limit_bytes=24 * 1024 * 1024)


def cost(rows, columns, sources):
    return pl.CostEstimate(
        flops=2 * rows * columns * sources, bytes_accessed=2 * rows * columns, transcendentals=0
    )


def in_vmem(x):
    return pltpu.with_memory_space_constraint(x, pltpu.VMEM)


def in_hbm(x):
    return pltpu.with_memory_space_constraint(x, pltpu.HBM)


def pick_rows(every, code, sources, rows_dev):
    row = code // rows_dev
    total = jnp.zeros((sources, every.shape[1]), jnp.float32)
    for index in range(rows_dev):
        mine = every[index * sources : (index + 1) * sources]
        total = total + jnp.where(row == index, mine, 0.0)
    return total


def by_slot(coeff, code, rows_dev):
    local = code % rows_dev
    low = [
        jnp.where(local == index, coeff, 0.0).astype(jnp.bfloat16) for index in range(rows_dev)
    ]
    return jnp.concatenate(low, axis=0)


def times_u(low, factors):
    return lax.dot_general(
        low, factors, (((1,), (1,)), ((), ())), preferred_element_type=jnp.float32
    )


def put_terms(lhs, v_ref, group, part, outs, rows_dev, peers):
    first, width, order = part
    deep = lhs.shape[1]
    terms = jnp.dot(
        lhs,
        v_ref[pl.ds(group * deep, deep), pl.ds(first, width)],
        preferred_element_type=jnp.float32,
    )
    place = spot(order, group)
    out = outs[place >= peers // 2]
    place = place % (peers // 2) * rows_dev
    out[place : place + rows_dev] = terms.reshape(rows_dev, -1, width).astype(out.dtype)


def start_kernel(dims, *refs):
    rows_dev, tiles_row, rank_max, peers, parts = dims
    cols_hbm, owner_hbm, ranks_hbm, misfit_hbm, u_hbm, v_hbm = refs[:6]
    u_ref, v_ref, code_ref = refs[6:9]
    outs = refs[9 : 9 + 2 * len(parts)]
    cols, owner, ranks, misfit, tile_at, code_at, rank_at, count, lhs_ref, small, u_sem, v_sem = refs[
        9 + 2 * len(parts) :
    ]
    here = lax.axis_index("rows")
    tiles = rows_dev * tiles_row
    group_tiles = tiles // peers
    deep = group_tiles * rank_max
    sources = misfit.shape[1]
    copies = [
        pltpu.make_async_copy(whence, to, small.at[i])
        for i, (whence, to) in enumerate(
            zip((cols_hbm, owner_hbm, ranks_hbm, misfit_hbm), (cols, owner, ranks, misfit))
        )
    ]
    for copy in copies:
        copy.start()
    for rel in range(peers):
        count[rel] = 0
    for copy in copies[:3]:
        copy.wait()

    def load(whence, to, sem, tile, at):
        pltpu.make_async_copy(
            whence.at[pl.ds(pl.multiple_of(tile * rank_max, rank_max), rank_max)],
            to.at[pl.ds(pl.multiple_of(at * rank_max, rank_max), rank_max)],
            sem.at[lax.div(at, group_tiles)],
        ).start()

    def sort_tile(tile, carry):
        row, k = lax.div(tile, tiles_row), lax.rem(tile, tiles_row)
        slot = owner[cols[k, here * rows_dev + row]]
        rel = jnp.bitwise_xor(lax.div(slot, rows_dev), here)
        at = rel * group_tiles + count[rel]
        count[rel] = count[rel] + 1
        load(u_hbm, u_ref, u_sem, tile, at)
        tile_at[at] = tile
        code_at[at] = row * rows_dev + lax.rem(slot, rows_dev)
        rank_at[at] = ranks[row, k]
        return carry

    def load_v(at, carry):
        load(v_hbm, v_ref, v_sem, tile_at[at], at)
        return carry

    def loaded(ref, sem, group):
        piece = ref.at[pl.ds(group * deep, deep)]
        pltpu.make_async_copy(piece, piece, sem.at[group]).wait()

    lax.fori_loop(0, tiles, sort_tile, 0)
    lax.fori_loop(0, tiles, load_v, 0)
    lane = lax.broadcasted_iota(jnp.int32, (1, deep), 1)
    for group in range(peers):
        code = jnp.full((1, deep), -1, jnp.int32)
        for i in range(group_tiles):
            at = group * group_tiles + i
            inside = (lane >= i * rank_max) & (lane < i * rank_max + rank_at[at])
            code = jnp.where(inside, code_at[at], code)
        code_ref[pl.ds(group, 1), :] = code
    copies[3].wait()
    low = misfit[...].astype(jnp.bfloat16).reshape(rows_dev * sources, -1)
    for group in range(peers):
        loaded(u_ref, u_sem, group)
        code = code_ref[pl.ds(group, 1), :]
        every = times_u(low, u_ref[pl.ds(group * deep, deep), :])
        lhs_ref[group] = by_slot(pick_rows(every, code, sources, rows_dev), code, rows_dev)
    for group in range(peers):
        loaded(v_ref, v_sem, group)
        lhs = lhs_ref[group]
        for i, part in enumerate(parts):
            put_terms(lhs, v_ref, group, part, outs[2 * i : 2 * i + 2], rows_dev, peers)


def low_field(base_ref, came_ref, contrast_ref, part):
    first, width, _ = part
    rows = []
    for row in range(base_ref.shape[0]):
        scale = contrast_ref[pl.ds(row, 1), pl.ds(first, width)]
        field = base_ref[row] + scale * came_ref[row].astype(jnp.float32)
        rows.append(field.astype(jnp.bfloat16))
    return jnp.concatenate(rows, axis=0)


def early_kernel(dims, parts, code_ref, contrast_ref, *refs):
    rows_dev, peers = dims
    fields, (u_ref, out_ref) = refs[: 2 * len(parts)], refs[2 * len(parts) :]
    deep = code_ref.shape[1]
    sources = out_ref.shape[1]
    lows = [
        low_field(fields[2 * i], fields[2 * i + 1], contrast_ref, part)
        for i, part in enumerate(parts)
    ]
    for group in range(peers):
        every = 0.0
        for low, (first, width, _) in zip(lows, parts):
            every = every + times_u(low, u_ref[pl.ds(group * deep, deep), pl.ds(first, width)])
        code = code_ref[pl.ds(group, 1), :]
        out_ref[group] = pick_rows(every, code, sources, rows_dev)


def ready_kernel(dims, late, parts, code_ref, contrast_ref, sum_ref, base_ref, came_ref, *refs):
    rows_dev, peers = dims
    u_ref, v_ref, lhs_ref = refs[:3]
    outs = refs[3:]
    deep = code_ref.shape[1]
    sources = sum_ref.shape[1]
    low = low_field(base_ref, came_ref, contrast_ref, late)
    first, width, _ = late
    for group in reversed(range(peers)):
        every = times_u(low, u_ref[pl.ds(group * deep, deep), pl.ds(first, width)])
        code = code_ref[pl.ds(group, 1), :]
        coeff = sum_ref[group] + pick_rows(every, code, sources, rows_dev)
        lhs = by_slot(coeff, code, rows_dev)
        lhs_ref[group] = lhs
        for out, part in zip(outs, parts):
            if spot(part[2], group) >= peers // 2:
                put_terms(lhs, v_ref, group, part, (None, out), rows_dev, peers)


def rest_kernel(dims, sent, parts, lhs_ref, v_ref, *refs):
    rows_dev, peers = dims
    sends = refs[: len(sent)]
    keeps = refs[len(sent) :]
    for out, i in zip(sends, sent):
        for group in in_order(parts[i][2], peers)[peers // 2 :]:
            put_terms(lhs_ref[group], v_ref, group, parts[i], (None, out), rows_dev, peers)
    for keep, part in zip(keeps, parts):
        for group in in_order(part[2], peers)[: peers // 2]:
            put_terms(lhs_ref[group], v_ref, group, part, (keep, None), rows_dev, peers)


def finish_kernel(parts, contrast_ref, forward_ref, *refs):
    fields, (field_ref, total_ref) = refs[: 2 * len(parts)], refs[2 * len(parts) :]
    for i, (first, width, _) in enumerate(parts):
        here = pl.ds(first, width)
        for row in range(field_ref.shape[0]):
            scale = contrast_ref[pl.ds(row, 1), here]
            field = fields[2 * i][row] + scale * fields[2 * i + 1][row].astype(jnp.float32)
            field_ref[row, :, here] = field
            product = forward_ref[row, :, here].astype(jnp.float32) * field
            total_ref[pl.ds(row, 1), here] = jnp.sum(product, axis=0, keepdims=True)


def swap(x, bit, peers):
    return lax.ppermute(x, "rows", [(i, i ^ (1 << bit)) for i in range(peers)])


def slot_sums(
    misfit, forward_fields, contrast, u_factors, v_factors, ranks, tile_cols, owner_slot
):
    peers = lax.axis_size("rows")
    rows_dev, tiles_row, rank_max, unknowns = u_factors.shape
    sources = misfit.shape[1]
    tiles = rows_dev * tiles_row
    deep = tiles // peers * rank_max
    parts = parts_of(unknowns, peers)
    first_sent, then_sent, late = [0, 1], [], 1
    early = [i for i in range(len(parts)) if i != late]
    half = (peers // 2 * rows_dev, sources)
    sent = [jax.ShapeDtypeStruct((*half, part[1]), jnp.bfloat16) for part in parts]
    kept = [jax.ShapeDtypeStruct((*half, part[1]), jnp.float32) for part in parts]
    u, v = (x.reshape(tiles * rank_max, unknowns) for x in (u_factors, v_factors))
    hbm = [pl.BlockSpec(memory_space=pl.ANY)]
    smem = lambda *shape: pltpu.SMEM(shape, jnp.int32)
    u, v, code, *got = pl.pallas_call(
        functools.partial(start_kernel, (rows_dev, tiles_row, rank_max, peers, parts)),
        out_shape=[pltpu.VMEM(x.shape, x.dtype) for x in (u, v)]
        + [jax.ShapeDtypeStruct((peers, deep), jnp.int32)]
        + [x for pair in zip(kept, sent) for x in pair],
        in_specs=hbm * 6,
        out_specs=vmem(3 + 2 * len(parts)),
        scratch_shapes=[
            smem(*tile_cols.shape[::-1]),
            smem(*owner_slot.shape),
            smem(*ranks.shape),
            pltpu.VMEM(misfit.shape, misfit.dtype),
            smem(tiles),
            smem(tiles),
            smem(tiles),
            smem(peers),
            pltpu.VMEM((peers, rows_dev * sources, deep), jnp.bfloat16),
            pltpu.SemaphoreType.DMA((4,)),
            pltpu.SemaphoreType.DMA((peers,)),
            pltpu.SemaphoreType.DMA((peers,)),
        ],
        compiler_params=params(),
        cost_estimate=cost(2 * tiles * rank_max, unknowns, sources),
        name="start",
    )(*(in_hbm(x) for x in (tile_cols.T, owner_slot, ranks, misfit, u, v)))
    dims = (rows_dev, peers)
    scale = contrast[:, None, :]
    columns = [(slice(None), slice(None), slice(part[0], part[0] + part[1])) for part in parts]
    for step in range(APPS):
        if step == 0:
            keeps, goes = list(got[::2]), list(got[1::2])
        else:
            coeff = pl.pallas_call(
                functools.partial(early_kernel, dims, [parts[i] for i in early]),
                out_shape=jax.ShapeDtypeStruct((peers, sources, deep), jnp.float32),
                in_specs=vmem(3 + 2 * len(early)),
                out_specs=vmem(1)[0],
                compiler_params=params(),
                cost_estimate=cost(u.shape[0], unknowns // 2, sources),
                name="early",
            )(code, contrast, *(x for i in early for x in (base[i], came[i])), in_vmem(u))
            lhs, *some = pl.pallas_call(
                functools.partial(ready_kernel, dims, parts[late], [parts[i] for i in first_sent]),
                out_shape=[jax.ShapeDtypeStruct((peers, rows_dev * sources, deep), jnp.bfloat16)]
                + [sent[i] for i in first_sent],
                in_specs=vmem(7),
                out_specs=vmem(1 + len(first_sent)),
                compiler_params=params(),
                cost_estimate=cost(u.shape[0], unknowns // 2, sources),
                name="ready",
            )(code, contrast, coeff, base[late], came[late], in_vmem(u), in_vmem(v))
            rest = pl.pallas_call(
                functools.partial(rest_kernel, dims, then_sent, parts),
                out_shape=[sent[i] for i in then_sent] + kept,
                in_specs=vmem(2),
                out_specs=vmem(len(then_sent) + len(parts)),
                compiler_params=params(),
                cost_estimate=cost(u.shape[0], unknowns // 2, sources),
                name="rest",
            )(lhs, in_vmem(v))
            goes = [None] * len(parts)
            for i, x in zip(first_sent + then_sent, [*some, *rest[: len(then_sent)]]):
                goes[i] = x
            keeps = list(rest[len(then_sent) :])
        base, came = [None] * len(parts), [None] * len(parts)
        levels = len(parts[0][2])
        for level in range(levels):
            for i, part in enumerate(parts):
                came[i] = swap(goes[i], part[2][level], peers)
                if level < levels - 1:
                    mid = keeps[i].shape[0] // 2
                    goes[i] = keeps[i][mid:] + came[i][mid:].astype(jnp.float32)
                    goes[i] = goes[i].astype(jnp.bfloat16)
                    keeps[i] = keeps[i][:mid] + came[i][:mid].astype(jnp.float32)
        for i in range(len(parts)):
            base[i] = misfit[columns[i]] + scale[columns[i]] * keeps[i]
    return pl.pallas_call(
        functools.partial(finish_kernel, parts),
        out_shape=[
            jax.ShapeDtypeStruct(misfit.shape, jnp.float32),
            jax.ShapeDtypeStruct(contrast.shape, jnp.float32),
        ],
        in_specs=vmem(2 + 2 * len(parts)),
        out_specs=vmem(2),
        compiler_params=params(),
        name="finish",
    )(contrast, forward_fields, *(x for pair in zip(base, came) for x in pair))


def route_tiles(tile_cols, owner_slot, rows_dev, peers):
    tiles = rows_dev * tile_cols.shape[1]
    target_slot = owner_slot[tile_cols.reshape(peers, tiles)]
    target_dev = target_slot // rows_dev
    local_slot = target_slot % rows_dev
    same = target_dev[:, :, None] == target_dev[:, None, :]
    before = jnp.arange(tiles)[None, :] < jnp.arange(tiles)[:, None]
    order = jnp.sum(jnp.where(same & before[None, :, :], 1, 0), axis=2).astype(jnp.int32)
    return target_dev, local_slot, order


def tile_terms(
    misfit, forward_fields, contrast, u_factors, v_factors, ranks, tile_cols, owner_slot
):
    rows_dev, tiles_row, rank_max, unknowns = u_factors.shape
    tiles = rows_dev * tiles_row
    peers = lax.axis_size("rows")
    cap = (tiles + peers - 1) // peers
    sources = misfit.shape[1]
    here = lax.axis_index("rows")
    target_dev, local_slot, order = route_tiles(tile_cols, owner_slot, rows_dev, peers)
    mine_dev = lax.dynamic_index_in_dim(target_dev, here, 0, keepdims=False)
    mine_order = lax.dynamic_index_in_dim(order, here, 0, keepdims=False)
    box = mine_dev * cap + mine_order
    sender = jnp.arange(peers, dtype=jnp.int32)[:, None] * cap + order
    entry = jnp.where(target_dev == here, sender, peers * cap).reshape(-1)
    arrival = (
        jnp.full((peers * cap,), -1, jnp.int32).at[entry].set(local_slot.reshape(-1), mode="drop")
    )
    pick = (arrival[:, None] == jnp.arange(rows_dev, dtype=jnp.int32)[None, :]).astype(jnp.float32)
    keep = (jnp.arange(rank_max, dtype=jnp.int32)[None, None, :] < ranks[:, :, None]).astype(
        jnp.float32
    )
    field = misfit
    for step in range(APPS):
        coeff = jnp.einsum(
            "lsb,lkrb->lksr",
            field.astype(jnp.bfloat16),
            u_factors,
            preferred_element_type=jnp.float32,
        )
        tile_coeff = (coeff * keep[:, :, None, :]).astype(jnp.bfloat16)
        terms = jnp.einsum(
            "lksr,lkrb->lksb", tile_coeff, v_factors, preferred_element_type=jnp.float32
        )
        terms = terms.reshape(tiles, sources, unknowns)
        outgoing = jnp.zeros((peers * cap, sources, unknowns), jnp.float32).at[box].set(terms)
        incoming = lax.all_to_all(
            outgoing.reshape(peers, cap, sources, unknowns).astype(jnp.bfloat16),
            "rows",
            split_axis=0,
            concat_axis=0,
            tiled=True,
        ).astype(jnp.float32)
        field = misfit + contrast[:, None, :] * jnp.einsum(
            "eq,esb->qsb",
            pick,
            incoming.reshape(peers * cap, sources, unknowns),
            precision=lax.Precision.HIGHEST,
        )
    return field, jnp.sum(forward_fields.astype(jnp.float32) * field, axis=1)


def src_sum(x):
    count = lax.axis_size("src")
    if count & (count - 1):
        return lax.psum(x, "src")
    terms = [x]
    for step in range(1, count):
        terms.append(lax.ppermute(x, "src", [(i, i ^ step) for i in range(count)]))
    while len(terms) > 1:
        terms = [a + b for a, b in zip(terms[::2], terms[1::2])]
    return terms[0]


def per_device(
    misfit, forward_fields, contrast, u_factors, v_factors, ranks, tile_cols, owner_slot
):
    rows_dev, tiles_row = ranks.shape
    peers = lax.axis_size("rows")
    tiles = rows_dev * tiles_row
    cap = (tiles + peers - 1) // peers
    dense = (
        peers > 1
        and peers & (peers - 1) == 0
        and tiles == cap * peers
        and cap >= rows_dev
        and cap * u_factors.shape[2] % 128 == 0
        and misfit.shape[2] % 512 == 0
        and misfit.shape[1] % 16 == 0
    )
    run = slot_sums if dense else tile_terms
    field, partial_sum = run(
        misfit, forward_fields, contrast, u_factors, v_factors, ranks, tile_cols, owner_slot
    )
    total = src_sum(partial_sum)
    sources = misfit.shape[1] * lax.axis_size("src")
    gradient = total * lax.rsqrt(jnp.float32(sources))
    return (field, gradient)


def solution(mesh):
    placed = (
        P("rows", "src", None),
        P("rows", "src", None),
        P("rows", None),
        P("rows", None, None, None),
        P("rows", None, None, None),
        P("rows", None),
        P(),
        P(),
    )
    return jax.shard_map(
        per_device,
        mesh=mesh,
        in_specs=placed,
        out_specs=(P("rows", "src", None), P("rows", None)),
        check_vma=False,
    )
```

```python
import functools

import jax
import jax.numpy as jnp
from jax import lax
from jax.experimental import pallas as pl
from jax.experimental.pallas import tpu as pltpu
from jax.sharding import PartitionSpec as P

APPS = 4

def parts_of(unknowns, peers):
    bits = list(range(peers.bit_length() - 1))
    turned = bits[1:2] + bits[:1] + bits[2:]
    width = unknowns // 2
    return [(0, width, bits), (width, width, turned)]


def spot(order, rel):
    place = 0
    for bit in order:
        place = place * 2 + ((rel >> bit) & 1)
    return place


def in_order(order, peers):
    return sorted(range(peers), key=lambda rel: spot(order, rel))


def vmem(count):
    return [pl.BlockSpec(memory_space=pltpu.VMEM)] * count


def params():
    return pltpu.CompilerParams(vmem_limit_bytes=24 * 1024 * 1024)


def cost(rows, columns, sources):
    return pl.CostEstimate(
        flops=2 * rows * columns * sources, bytes_accessed=2 * rows * columns, transcendentals=0
    )


def in_vmem(x):
    return pltpu.with_memory_space_constraint(x, pltpu.VMEM)


def in_hbm(x):
    return pltpu.with_memory_space_constraint(x, pltpu.HBM)


def pick_rows(every, code, sources, rows_dev):
    row = code // rows_dev
    total = jnp.zeros((sources, every.shape[1]), jnp.float32)
    for index in range(rows_dev):
        mine = every[index * sources : (index + 1) * sources]
        total = total + jnp.where(row == index, mine, 0.0)
    return total


def by_slot(coeff, code, rows_dev):
    local = code % rows_dev
    low = [
        jnp.where(local == index, coeff, 0.0).astype(jnp.bfloat16) for index in range(rows_dev)
    ]
    return jnp.concatenate(low, axis=0)


def times_u(low, factors):
    return lax.dot_general(
        low, factors, (((1,), (1,)), ((), ())), preferred_element_type=jnp.float32
    )


def put_terms(lhs, v_ref, group, part, outs, rows_dev, peers):
    first, width, order = part
    deep = lhs.shape[1]
    terms = jnp.dot(
        lhs,
        v_ref[pl.ds(group * deep, deep), pl.ds(first, width)],
        preferred_element_type=jnp.float32,
    )
    place = spot(order, group)
    out = outs[place >= peers // 2]
    place = place % (peers // 2) * rows_dev
    out[place : place + rows_dev] = terms.reshape(rows_dev, -1, width).astype(out.dtype)


def start_kernel(dims, *refs):
    rows_dev, tiles_row, rank_max, peers, parts = dims
    cols_hbm, owner_hbm, ranks_hbm, misfit_hbm, u_hbm, v_hbm = refs[:6]
    u_ref, v_ref, code_ref = refs[6:9]
    outs = refs[9 : 9 + 2 * len(parts)]
    cols, owner, ranks, misfit, tile_at, code_at, rank_at, count, lhs_ref, small, u_sem, v_sem = refs[
        9 + 2 * len(parts) :
    ]
    here = lax.axis_index("rows")
    tiles = rows_dev * tiles_row
    group_tiles = tiles // peers
    deep = group_tiles * rank_max
    sources = misfit.shape[1]
    copies = [
        pltpu.make_async_copy(whence, to, small.at[i])
        for i, (whence, to) in enumerate(
            zip((cols_hbm, owner_hbm, ranks_hbm, misfit_hbm), (cols, owner, ranks, misfit))
        )
    ]
    for copy in copies:
        copy.start()
    for rel in range(peers):
        count[rel] = 0
    for copy in copies[:3]:
        copy.wait()

    def load(whence, to, sem, tile, at, group):
        pltpu.make_async_copy(
            whence.at[pl.ds(pl.multiple_of(tile * rank_max, rank_max), rank_max)],
            to.at[pl.ds(pl.multiple_of(at * rank_max, rank_max), rank_max)],
            sem.at[group],
        ).start()

    for tile in range(tiles):
        row, k = divmod(tile, tiles_row)
        slot = owner[cols[k, here * rows_dev + row]]
        rel = jnp.bitwise_xor(lax.div(slot, rows_dev), here)
        at = rel * group_tiles + count[rel]
        load(u_hbm, u_ref, u_sem, tile, at, rel)
        count[rel] = count[rel] + 1
        tile_at[at] = tile
        code_at[at] = row * rows_dev + lax.rem(slot, rows_dev)
        rank_at[at] = ranks[row, k]

    def loaded(ref, sem, group):
        piece = ref.at[pl.ds(group * deep, deep)]
        pltpu.make_async_copy(piece, piece, sem.at[group]).wait()

    for at in range(tiles):
        load(v_hbm, v_ref, v_sem, tile_at[at], at, at // group_tiles)
    lane = lax.broadcasted_iota(jnp.int32, (1, deep), 1)
    for group in range(peers):
        code = jnp.full((1, deep), -1, jnp.int32)
        for i in range(group_tiles):
            at = group * group_tiles + i
            inside = (lane >= i * rank_max) & (lane < i * rank_max + rank_at[at])
            code = jnp.where(inside, code_at[at], code)
        code_ref[pl.ds(group, 1), :] = code
    copies[3].wait()
    low = misfit[...].astype(jnp.bfloat16).reshape(rows_dev * sources, -1)
    for group in range(peers):
        loaded(u_ref, u_sem, group)
        code = code_ref[pl.ds(group, 1), :]
        every = times_u(low, u_ref[pl.ds(group * deep, deep), :])
        lhs_ref[group] = by_slot(pick_rows(every, code, sources, rows_dev), code, rows_dev)
    for group in range(peers):
        loaded(v_ref, v_sem, group)
        lhs = lhs_ref[group]
        for i, part in enumerate(parts):
            put_terms(lhs, v_ref, group, part, outs[2 * i : 2 * i + 2], rows_dev, peers)


def low_field(base_ref, came_ref, contrast_ref, part):
    first, width, _ = part
    rows = []
    for row in range(base_ref.shape[0]):
        scale = contrast_ref[pl.ds(row, 1), pl.ds(first, width)]
        field = base_ref[row] + scale * came_ref[row].astype(jnp.float32)
        rows.append(field.astype(jnp.bfloat16))
    return jnp.concatenate(rows, axis=0)


def early_kernel(dims, parts, code_ref, contrast_ref, *refs):
    rows_dev, peers = dims
    fields, (u_ref, out_ref) = refs[: 2 * len(parts)], refs[2 * len(parts) :]
    deep = code_ref.shape[1]
    sources = out_ref.shape[1]
    lows = [
        low_field(fields[2 * i], fields[2 * i + 1], contrast_ref, part)
        for i, part in enumerate(parts)
    ]
    for group in range(peers):
        every = 0.0
        for low, (first, width, _) in zip(lows, parts):
            every = every + times_u(low, u_ref[pl.ds(group * deep, deep), pl.ds(first, width)])
        code = code_ref[pl.ds(group, 1), :]
        out_ref[group] = pick_rows(every, code, sources, rows_dev)


def ready_kernel(dims, late, parts, code_ref, contrast_ref, sum_ref, base_ref, came_ref, *refs):
    rows_dev, peers = dims
    u_ref, v_ref, lhs_ref = refs[:3]
    outs = refs[3:]
    deep = code_ref.shape[1]
    sources = sum_ref.shape[1]
    low = low_field(base_ref, came_ref, contrast_ref, late)
    first, width, _ = late
    for group in reversed(range(peers)):
        every = times_u(low, u_ref[pl.ds(group * deep, deep), pl.ds(first, width)])
        code = code_ref[pl.ds(group, 1), :]
        coeff = sum_ref[group] + pick_rows(every, code, sources, rows_dev)
        lhs = by_slot(coeff, code, rows_dev)
        lhs_ref[group] = lhs
        for out, part in zip(outs, parts):
            if spot(part[2], group) >= peers // 2:
                put_terms(lhs, v_ref, group, part, (None, out), rows_dev, peers)


def more_kernel(dims, parts, lhs_ref, v_ref, *outs):
    rows_dev, peers = dims
    for out, (part, kept) in zip(outs, parts):
        for group in range(peers):
            if (spot(part[2], group) < peers // 2) == kept:
                put_terms(lhs_ref[group], v_ref, group, part, (out, out), rows_dev, peers)


def finish_kernel(parts, contrast_ref, forward_ref, *refs):
    fields, (field_ref, total_ref) = refs[: 2 * len(parts)], refs[2 * len(parts) :]
    for i, (first, width, _) in enumerate(parts):
        here = pl.ds(first, width)
        for row in range(field_ref.shape[0]):
            scale = contrast_ref[pl.ds(row, 1), here]
            field = fields[2 * i][row] + scale * fields[2 * i + 1][row].astype(jnp.float32)
            field_ref[row, :, here] = field
            product = forward_ref[row, :, here].astype(jnp.float32) * field
            total_ref[pl.ds(row, 1), here] = jnp.sum(product, axis=0, keepdims=True)


def swap(x, bit, peers):
    return lax.ppermute(x, "rows", [(i, i ^ (1 << bit)) for i in range(peers)])


def slot_sums(
    misfit, forward_fields, contrast, u_factors, v_factors, ranks, tile_cols, owner_slot
):
    peers = lax.axis_size("rows")
    rows_dev, tiles_row, rank_max, unknowns = u_factors.shape
    sources = misfit.shape[1]
    tiles = rows_dev * tiles_row
    deep = tiles // peers * rank_max
    parts = parts_of(unknowns, peers)
    first_sent, late = [0], 1
    early = [i for i in range(len(parts)) if i != late]
    half = (peers // 2 * rows_dev, sources)
    sent = [jax.ShapeDtypeStruct((*half, part[1]), jnp.bfloat16) for part in parts]
    kept = [jax.ShapeDtypeStruct((*half, part[1]), jnp.float32) for part in parts]
    u, v = (x.reshape(tiles * rank_max, unknowns) for x in (u_factors, v_factors))
    hbm = [pl.BlockSpec(memory_space=pl.ANY)]
    smem = lambda *shape: pltpu.SMEM(shape, jnp.int32)
    u, v, code, *got = pl.pallas_call(
        functools.partial(start_kernel, (rows_dev, tiles_row, rank_max, peers, parts)),
        out_shape=[pltpu.VMEM(x.shape, x.dtype) for x in (u, v)]
        + [jax.ShapeDtypeStruct((peers, deep), jnp.int32)]
        + [x for pair in zip(kept, sent) for x in pair],
        in_specs=hbm * 6,
        out_specs=vmem(3 + 2 * len(parts)),
        scratch_shapes=[
            smem(*tile_cols.shape[::-1]),
            smem(*owner_slot.shape),
            smem(*ranks.shape),
            pltpu.VMEM(misfit.shape, misfit.dtype),
            smem(tiles),
            smem(tiles),
            smem(tiles),
            smem(peers),
            pltpu.VMEM((peers, rows_dev * sources, deep), jnp.bfloat16),
            pltpu.SemaphoreType.DMA((4,)),
            pltpu.SemaphoreType.DMA((peers,)),
            pltpu.SemaphoreType.DMA((peers,)),
        ],
        compiler_params=params(),
        cost_estimate=cost(2 * tiles * rank_max, unknowns, sources),
        name="start",
    )(*(in_hbm(x) for x in (tile_cols.T, owner_slot, ranks, misfit, u, v)))
    dims = (rows_dev, peers)
    scale = contrast[:, None, :]
    columns = [(slice(None), slice(None), slice(part[0], part[0] + part[1])) for part in parts]
    for step in range(APPS):
        if step == 0:
            keeps, goes = list(got[::2]), list(got[1::2])
        else:
            coeff = pl.pallas_call(
                functools.partial(early_kernel, dims, [parts[i] for i in early]),
                out_shape=jax.ShapeDtypeStruct((peers, sources, deep), jnp.float32),
                in_specs=vmem(3 + 2 * len(early)),
                out_specs=vmem(1)[0],
                compiler_params=params(),
                cost_estimate=cost(u.shape[0], unknowns // 2, sources),
                name="early",
            )(code, contrast, *(x for i in early for x in (base[i], came[i])), in_vmem(u))
            lhs, *some = pl.pallas_call(
                functools.partial(ready_kernel, dims, parts[late], [parts[i] for i in first_sent]),
                out_shape=[jax.ShapeDtypeStruct((peers, rows_dev * sources, deep), jnp.bfloat16)]
                + [sent[i] for i in first_sent],
                in_specs=vmem(7),
                out_specs=vmem(1 + len(first_sent)),
                compiler_params=params(),
                cost_estimate=cost(u.shape[0], unknowns // 2, sources),
                name="ready",
            )(code, contrast, coeff, base[late], came[late], in_vmem(u), in_vmem(v))
            goes, keeps = [*some], []
            for names, shapes, to in (
                [[(parts[1], False)], sent[1:], goes],
                [[(part, True) for part in parts], kept, keeps],
            ):
                to += pl.pallas_call(
                    functools.partial(more_kernel, dims, names),
                    out_shape=shapes,
                    in_specs=vmem(2),
                    out_specs=vmem(len(shapes)),
                    compiler_params=params(),
                    cost_estimate=cost(u.shape[0], unknowns // 4 * len(shapes), sources),
                    name="more",
                )(lhs, in_vmem(v))
        base, came = [None] * len(parts), [None] * len(parts)
        levels = len(parts[0][2])
        for level in range(levels):
            for i, part in enumerate(parts):
                came[i] = swap(goes[i], part[2][level], peers)
                if level < levels - 1:
                    mid = keeps[i].shape[0] // 2
                    goes[i] = keeps[i][mid:] + came[i][mid:].astype(jnp.float32)
                    goes[i] = goes[i].astype(jnp.bfloat16)
                    keeps[i] = keeps[i][:mid] + came[i][:mid].astype(jnp.float32)
        for i in range(len(parts)):
            base[i] = misfit[columns[i]] + scale[columns[i]] * keeps[i]
    return pl.pallas_call(
        functools.partial(finish_kernel, parts),
        out_shape=[
            jax.ShapeDtypeStruct(misfit.shape, jnp.float32),
            jax.ShapeDtypeStruct(contrast.shape, jnp.float32),
        ],
        in_specs=vmem(2 + 2 * len(parts)),
        out_specs=vmem(2),
        compiler_params=params(),
        name="finish",
    )(contrast, forward_fields, *(x for pair in zip(base, came) for x in pair))


def route_tiles(tile_cols, owner_slot, rows_dev, peers):
    tiles = rows_dev * tile_cols.shape[1]
    target_slot = owner_slot[tile_cols.reshape(peers, tiles)]
    target_dev = target_slot // rows_dev
    local_slot = target_slot % rows_dev
    same = target_dev[:, :, None] == target_dev[:, None, :]
    before = jnp.arange(tiles)[None, :] < jnp.arange(tiles)[:, None]
    order = jnp.sum(jnp.where(same & before[None, :, :], 1, 0), axis=2).astype(jnp.int32)
    return target_dev, local_slot, order


def tile_terms(
    misfit, forward_fields, contrast, u_factors, v_factors, ranks, tile_cols, owner_slot
):
    rows_dev, tiles_row, rank_max, unknowns = u_factors.shape
    tiles = rows_dev * tiles_row
    peers = lax.axis_size("rows")
    cap = (tiles + peers - 1) // peers
    sources = misfit.shape[1]
    here = lax.axis_index("rows")
    target_dev, local_slot, order = route_tiles(tile_cols, owner_slot, rows_dev, peers)
    mine_dev = lax.dynamic_index_in_dim(target_dev, here, 0, keepdims=False)
    mine_order = lax.dynamic_index_in_dim(order, here, 0, keepdims=False)
    box = mine_dev * cap + mine_order
    sender = jnp.arange(peers, dtype=jnp.int32)[:, None] * cap + order
    entry = jnp.where(target_dev == here, sender, peers * cap).reshape(-1)
    arrival = (
        jnp.full((peers * cap,), -1, jnp.int32).at[entry].set(local_slot.reshape(-1), mode="drop")
    )
    pick = (arrival[:, None] == jnp.arange(rows_dev, dtype=jnp.int32)[None, :]).astype(jnp.float32)
    keep = (jnp.arange(rank_max, dtype=jnp.int32)[None, None, :] < ranks[:, :, None]).astype(
        jnp.float32
    )
    field = misfit
    for step in range(APPS):
        coeff = jnp.einsum(
            "lsb,lkrb->lksr",
            field.astype(jnp.bfloat16),
            u_factors,
            preferred_element_type=jnp.float32,
        )
        tile_coeff = (coeff * keep[:, :, None, :]).astype(jnp.bfloat16)
        terms = jnp.einsum(
            "lksr,lkrb->lksb", tile_coeff, v_factors, preferred_element_type=jnp.float32
        )
        terms = terms.reshape(tiles, sources, unknowns)
        outgoing = jnp.zeros((peers * cap, sources, unknowns), jnp.float32).at[box].set(terms)
        incoming = lax.all_to_all(
            outgoing.reshape(peers, cap, sources, unknowns).astype(jnp.bfloat16),
            "rows",
            split_axis=0,
            concat_axis=0,
            tiled=True,
        ).astype(jnp.float32)
        field = misfit + contrast[:, None, :] * jnp.einsum(
            "eq,esb->qsb",
            pick,
            incoming.reshape(peers * cap, sources, unknowns),
            precision=lax.Precision.HIGHEST,
        )
    return field, jnp.sum(forward_fields.astype(jnp.float32) * field, axis=1)


def src_sum(x):
    count = lax.axis_size("src")
    if count & (count - 1):
        return lax.psum(x, "src")
    terms = [x]
    for step in range(1, count):
        terms.append(lax.ppermute(x, "src", [(i, i ^ step) for i in range(count)]))
    while len(terms) > 1:
        terms = [a + b for a, b in zip(terms[::2], terms[1::2])]
    return terms[0]


def per_device(
    misfit, forward_fields, contrast, u_factors, v_factors, ranks, tile_cols, owner_slot
):
    rows_dev, tiles_row = ranks.shape
    peers = lax.axis_size("rows")
    tiles = rows_dev * tiles_row
    cap = (tiles + peers - 1) // peers
    dense = (
        peers > 1
        and peers & (peers - 1) == 0
        and tiles == cap * peers
        and cap >= rows_dev
        and cap * u_factors.shape[2] % 128 == 0
        and misfit.shape[2] % 512 == 0
        and misfit.shape[1] % 16 == 0
    )
    run = slot_sums if dense else tile_terms
    field, partial_sum = run(
        misfit, forward_fields, contrast, u_factors, v_factors, ranks, tile_cols, owner_slot
    )
    total = src_sum(partial_sum)
    sources = misfit.shape[1] * lax.axis_size("src")
    gradient = total * lax.rsqrt(jnp.float32(sources))
    return (field, gradient)


def solution(mesh):
    placed = (
        P("rows", "src", None),
        P("rows", "src", None),
        P("rows", None),
        P("rows", None, None, None),
        P("rows", None, None, None),
        P("rows", None),
        P(),
        P(),
    )
    return jax.shard_map(
        per_device,
        mesh=mesh,
        in_specs=placed,
        out_specs=(P("rows", "src", None), P("rows", None)),
        check_vma=False,
    )
```

```python
import functools

import jax
import jax.numpy as jnp
from jax import lax
from jax.experimental import pallas as pl
from jax.experimental.pallas import tpu as pltpu
from jax.sharding import PartitionSpec as P

APPS = 4

def parts_of(unknowns, peers):
    bits = list(range(peers.bit_length() - 1))
    turned = bits[1:2] + bits[:1] + bits[2:]
    width = unknowns // 2
    return [(0, width, bits), (width, width, turned)]


def spot(order, rel):
    place = 0
    for bit in order:
        place = place * 2 + ((rel >> bit) & 1)
    return place


def in_order(order, peers):
    return sorted(range(peers), key=lambda rel: spot(order, rel))


def vmem(count):
    return [pl.BlockSpec(memory_space=pltpu.VMEM)] * count


def params():
    return pltpu.CompilerParams(vmem_limit_bytes=24 * 1024 * 1024)


def cost(rows, columns, sources):
    return pl.CostEstimate(
        flops=2 * rows * columns * sources, bytes_accessed=2 * rows * columns, transcendentals=0
    )


def in_vmem(x):
    return pltpu.with_memory_space_constraint(x, pltpu.VMEM)


def in_hbm(x):
    return pltpu.with_memory_space_constraint(x, pltpu.HBM)


def pick_rows(every, code, sources, rows_dev):
    row = code // rows_dev
    total = jnp.zeros((sources, every.shape[1]), jnp.float32)
    for index in range(rows_dev):
        mine = every[index * sources : (index + 1) * sources]
        total = total + jnp.where(row == index, mine, 0.0)
    return total


def by_slot(coeff, code, rows_dev):
    local = code % rows_dev
    low = [
        jnp.where(local == index, coeff, 0.0).astype(jnp.bfloat16) for index in range(rows_dev)
    ]
    return jnp.concatenate(low, axis=0)


def times_u(low, factors):
    return lax.dot_general(
        low, factors, (((1,), (1,)), ((), ())), preferred_element_type=jnp.float32
    )


def put_terms(lhs, v_ref, group, part, outs, rows_dev, peers):
    first, width, order = part
    deep = lhs.shape[1]
    terms = jnp.dot(
        lhs,
        v_ref[pl.ds(group * deep, deep), pl.ds(first, width)],
        preferred_element_type=jnp.float32,
    )
    place = spot(order, group)
    out = outs[place >= peers // 2]
    place = place % (peers // 2) * rows_dev
    out[place : place + rows_dev] = terms.reshape(rows_dev, -1, width).astype(out.dtype)


def start_kernel(dims, *refs):
    rows_dev, tiles_row, rank_max, peers, parts = dims
    cols_hbm, owner_hbm, ranks_hbm, misfit_hbm, u_hbm, v_hbm = refs[:6]
    u_ref, v_ref, code_ref = refs[6:9]
    outs = refs[9 : 9 + 2 * len(parts)]
    cols, owner, ranks, misfit, tile_at, code_at, rank_at, count, lhs_ref, small, u_sem, v_sem = refs[
        9 + 2 * len(parts) :
    ]
    here = lax.axis_index("rows")
    tiles = rows_dev * tiles_row
    group_tiles = tiles // peers
    deep = group_tiles * rank_max
    sources = misfit.shape[1]
    copies = [
        pltpu.make_async_copy(whence, to, small.at[i])
        for i, (whence, to) in enumerate(
            zip((cols_hbm, owner_hbm, ranks_hbm, misfit_hbm), (cols, owner, ranks, misfit))
        )
    ]
    for copy in copies:
        copy.start()
    for rel in range(peers):
        count[rel] = 0
    for copy in copies[:3]:
        copy.wait()

    def load(whence, to, sem, tile, at, group):
        pltpu.make_async_copy(
            whence.at[pl.ds(pl.multiple_of(tile * rank_max, rank_max), rank_max)],
            to.at[pl.ds(pl.multiple_of(at * rank_max, rank_max), rank_max)],
            sem.at[group],
        ).start()

    def sort_tile(tile, carry):
        row, k = lax.div(tile, tiles_row), lax.rem(tile, tiles_row)
        slot = owner[cols[k, here * rows_dev + row]]
        rel = turned(jnp.bitwise_xor(lax.div(slot, rows_dev), here), peers, lax.axis_index("src"))
        at = rel * group_tiles + count[rel]
        load(u_hbm, u_ref, u_sem, tile, at, rel)
        count[rel] = count[rel] + 1
        tile_at[at] = tile
        code_at[at] = row * rows_dev + lax.rem(slot, rows_dev)
        rank_at[at] = ranks[row, k]
        return carry

    def load_v(at, carry):
        load(v_hbm, v_ref, v_sem, tile_at[at], at, lax.div(at, group_tiles))
        return carry

    def loaded(ref, sem, group):
        piece = ref.at[pl.ds(group * deep, deep)]
        pltpu.make_async_copy(piece, piece, sem.at[group]).wait()

    lax.fori_loop(0, tiles, sort_tile, 0)
    lax.fori_loop(0, tiles, load_v, 0)
    lane = lax.broadcasted_iota(jnp.int32, (1, deep), 1)
    for group in range(peers):
        code = jnp.full((1, deep), -1, jnp.int32)
        for i in range(group_tiles):
            at = group * group_tiles + i
            inside = (lane >= i * rank_max) & (lane < i * rank_max + rank_at[at])
            code = jnp.where(inside, code_at[at], code)
        code_ref[pl.ds(group, 1), :] = code
    copies[3].wait()
    low = misfit[...].astype(jnp.bfloat16).reshape(rows_dev * sources, -1)
    for group in range(peers):
        loaded(u_ref, u_sem, group)
        code = code_ref[pl.ds(group, 1), :]
        every = times_u(low, u_ref[pl.ds(group * deep, deep), :])
        lhs_ref[group] = by_slot(pick_rows(every, code, sources, rows_dev), code, rows_dev)
    for group in range(peers):
        loaded(v_ref, v_sem, group)
        lhs = lhs_ref[group]
        for i, part in enumerate(parts):
            put_terms(lhs, v_ref, group, part, outs[2 * i : 2 * i + 2], rows_dev, peers)


def low_field(base_ref, came_ref, contrast_ref, part):
    first, width, _ = part
    rows = []
    for row in range(base_ref.shape[0]):
        scale = contrast_ref[pl.ds(row, 1), pl.ds(first, width)]
        field = base_ref[row] + scale * came_ref[row].astype(jnp.float32)
        rows.append(field.astype(jnp.bfloat16))
    return jnp.concatenate(rows, axis=0)


def early_kernel(dims, parts, code_ref, contrast_ref, *refs):
    rows_dev, peers = dims
    fields, (u_ref, out_ref) = refs[: 2 * len(parts)], refs[2 * len(parts) :]
    deep = code_ref.shape[1]
    sources = out_ref.shape[1]
    lows = [
        low_field(fields[2 * i], fields[2 * i + 1], contrast_ref, part)
        for i, part in enumerate(parts)
    ]
    for group in range(peers):
        every = 0.0
        for low, (first, width, _) in zip(lows, parts):
            every = every + times_u(low, u_ref[pl.ds(group * deep, deep), pl.ds(first, width)])
        code = code_ref[pl.ds(group, 1), :]
        out_ref[group] = pick_rows(every, code, sources, rows_dev)


def ready_kernel(dims, late, parts, code_ref, contrast_ref, sum_ref, base_ref, came_ref, *refs):
    rows_dev, peers = dims
    u_ref, v_ref, lhs_ref = refs[:3]
    outs = refs[3:]
    deep = code_ref.shape[1]
    sources = sum_ref.shape[1]
    low = low_field(base_ref, came_ref, contrast_ref, late)
    first, width, _ = late
    for group in reversed(range(peers)):
        every = times_u(low, u_ref[pl.ds(group * deep, deep), pl.ds(first, width)])
        code = code_ref[pl.ds(group, 1), :]
        coeff = sum_ref[group] + pick_rows(every, code, sources, rows_dev)
        lhs = by_slot(coeff, code, rows_dev)
        lhs_ref[group] = lhs
        for out, part in zip(outs, parts):
            if spot(part[2], group) >= peers // 2:
                put_terms(lhs, v_ref, group, part, (None, out), rows_dev, peers)


def more_kernel(dims, parts, lhs_ref, v_ref, *outs):
    rows_dev, peers = dims
    for out, (part, kept) in zip(outs, parts):
        for group in range(peers):
            if (spot(part[2], group) < peers // 2) == kept:
                put_terms(lhs_ref[group], v_ref, group, part, (out, out), rows_dev, peers)


def finish_kernel(parts, contrast_ref, forward_ref, *refs):
    fields, (field_ref, total_ref) = refs[: 2 * len(parts)], refs[2 * len(parts) :]
    for i, (first, width, _) in enumerate(parts):
        here = pl.ds(first, width)
        for row in range(field_ref.shape[0]):
            scale = contrast_ref[pl.ds(row, 1), here]
            field = fields[2 * i][row] + scale * fields[2 * i + 1][row].astype(jnp.float32)
            field_ref[row, :, here] = field
            product = forward_ref[row, :, here].astype(jnp.float32) * field
            total_ref[pl.ds(row, 1), here] = jnp.sum(product, axis=0, keepdims=True)


def turned(rel, peers, src):
    if peers < 4:
        return rel
    swapped = (rel >> 2 << 2) | ((rel & 1) << 1) | ((rel >> 1) & 1)
    odd = src % 2
    return swapped * odd + rel * (1 - odd)


def swap(x, bit, peers):
    count = lax.axis_size("src")
    pairs = [
        (row * count + src, (row ^ turned(1 << bit, peers, src)) * count + src)
        for row in range(peers)
        for src in range(count)
    ]
    return lax.ppermute(x, ("rows", "src"), pairs)


def slot_sums(
    misfit, forward_fields, contrast, u_factors, v_factors, ranks, tile_cols, owner_slot
):
    peers = lax.axis_size("rows")
    rows_dev, tiles_row, rank_max, unknowns = u_factors.shape
    sources = misfit.shape[1]
    tiles = rows_dev * tiles_row
    deep = tiles // peers * rank_max
    parts = parts_of(unknowns, peers)
    first_sent, late = [0], 1
    early = [i for i in range(len(parts)) if i != late]
    half = (peers // 2 * rows_dev, sources)
    sent = [jax.ShapeDtypeStruct((*half, part[1]), jnp.bfloat16) for part in parts]
    kept = [jax.ShapeDtypeStruct((*half, part[1]), jnp.float32) for part in parts]
    u, v = (x.reshape(tiles * rank_max, unknowns) for x in (u_factors, v_factors))
    hbm = [pl.BlockSpec(memory_space=pl.ANY)]
    smem = lambda *shape: pltpu.SMEM(shape, jnp.int32)
    u, v, code, *got = pl.pallas_call(
        functools.partial(start_kernel, (rows_dev, tiles_row, rank_max, peers, parts)),
        out_shape=[pltpu.VMEM(x.shape, x.dtype) for x in (u, v)]
        + [jax.ShapeDtypeStruct((peers, deep), jnp.int32)]
        + [x for pair in zip(kept, sent) for x in pair],
        in_specs=hbm * 6,
        out_specs=vmem(3 + 2 * len(parts)),
        scratch_shapes=[
            smem(*tile_cols.shape[::-1]),
            smem(*owner_slot.shape),
            smem(*ranks.shape),
            pltpu.VMEM(misfit.shape, misfit.dtype),
            smem(tiles),
            smem(tiles),
            smem(tiles),
            smem(peers),
            pltpu.VMEM((peers, rows_dev * sources, deep), jnp.bfloat16),
            pltpu.SemaphoreType.DMA((4,)),
            pltpu.SemaphoreType.DMA((peers,)),
            pltpu.SemaphoreType.DMA((peers,)),
        ],
        compiler_params=params(),
        cost_estimate=cost(2 * tiles * rank_max, unknowns, sources),
        name="start",
    )(*(in_hbm(x) for x in (tile_cols.T, owner_slot, ranks, misfit, u, v)))
    dims = (rows_dev, peers)
    scale = contrast[:, None, :]
    columns = [(slice(None), slice(None), slice(part[0], part[0] + part[1])) for part in parts]
    for step in range(APPS):
        if step == 0:
            keeps, goes = list(got[::2]), list(got[1::2])
        else:
            coeff = pl.pallas_call(
                functools.partial(early_kernel, dims, [parts[i] for i in early]),
                out_shape=jax.ShapeDtypeStruct((peers, sources, deep), jnp.float32),
                in_specs=vmem(3 + 2 * len(early)),
                out_specs=vmem(1)[0],
                compiler_params=params(),
                cost_estimate=cost(u.shape[0], unknowns // 2, sources),
                name="early",
            )(code, contrast, *(x for i in early for x in (base[i], came[i])), in_vmem(u))
            lhs, *some = pl.pallas_call(
                functools.partial(ready_kernel, dims, parts[late], [parts[i] for i in first_sent]),
                out_shape=[jax.ShapeDtypeStruct((peers, rows_dev * sources, deep), jnp.bfloat16)]
                + [sent[i] for i in first_sent],
                in_specs=vmem(7),
                out_specs=vmem(1 + len(first_sent)),
                compiler_params=params(),
                cost_estimate=cost(u.shape[0], unknowns // 2, sources),
                name="ready",
            )(code, contrast, coeff, base[late], came[late], in_vmem(u), in_vmem(v))
            goes, keeps = [*some], []
            for names, shapes, to in (
                [[(parts[1], False)], sent[1:], goes],
                [[(part, True) for part in parts], kept, keeps],
            ):
                to += pl.pallas_call(
                    functools.partial(more_kernel, dims, names),
                    out_shape=shapes,
                    in_specs=vmem(2),
                    out_specs=vmem(len(shapes)),
                    compiler_params=params(),
                    cost_estimate=cost(u.shape[0], unknowns // 4 * len(shapes), sources),
                    name="more",
                )(lhs, in_vmem(v))
        base, came = [None] * len(parts), [None] * len(parts)
        levels = len(parts[0][2])
        for level in range(levels):
            for i, part in enumerate(parts):
                came[i] = swap(goes[i], part[2][level], peers)
                if level < levels - 1:
                    mid = keeps[i].shape[0] // 2
                    goes[i] = keeps[i][mid:] + came[i][mid:].astype(jnp.float32)
                    goes[i] = goes[i].astype(jnp.bfloat16)
                    keeps[i] = keeps[i][:mid] + came[i][:mid].astype(jnp.float32)
        for i in range(len(parts)):
            base[i] = misfit[columns[i]] + scale[columns[i]] * keeps[i]
    return pl.pallas_call(
        functools.partial(finish_kernel, parts),
        out_shape=[
            jax.ShapeDtypeStruct(misfit.shape, jnp.float32),
            jax.ShapeDtypeStruct(contrast.shape, jnp.float32),
        ],
        in_specs=vmem(2 + 2 * len(parts)),
        out_specs=vmem(2),
        compiler_params=params(),
        name="finish",
    )(contrast, forward_fields, *(x for pair in zip(base, came) for x in pair))


def route_tiles(tile_cols, owner_slot, rows_dev, peers):
    tiles = rows_dev * tile_cols.shape[1]
    target_slot = owner_slot[tile_cols.reshape(peers, tiles)]
    target_dev = target_slot // rows_dev
    local_slot = target_slot % rows_dev
    same = target_dev[:, :, None] == target_dev[:, None, :]
    before = jnp.arange(tiles)[None, :] < jnp.arange(tiles)[:, None]
    order = jnp.sum(jnp.where(same & before[None, :, :], 1, 0), axis=2).astype(jnp.int32)
    return target_dev, local_slot, order


def tile_terms(
    misfit, forward_fields, contrast, u_factors, v_factors, ranks, tile_cols, owner_slot
):
    rows_dev, tiles_row, rank_max, unknowns = u_factors.shape
    tiles = rows_dev * tiles_row
    peers = lax.axis_size("rows")
    cap = (tiles + peers - 1) // peers
    sources = misfit.shape[1]
    here = lax.axis_index("rows")
    target_dev, local_slot, order = route_tiles(tile_cols, owner_slot, rows_dev, peers)
    mine_dev = lax.dynamic_index_in_dim(target_dev, here, 0, keepdims=False)
    mine_order = lax.dynamic_index_in_dim(order, here, 0, keepdims=False)
    box = mine_dev * cap + mine_order
    sender = jnp.arange(peers, dtype=jnp.int32)[:, None] * cap + order
    entry = jnp.where(target_dev == here, sender, peers * cap).reshape(-1)
    arrival = (
        jnp.full((peers * cap,), -1, jnp.int32).at[entry].set(local_slot.reshape(-1), mode="drop")
    )
    pick = (arrival[:, None] == jnp.arange(rows_dev, dtype=jnp.int32)[None, :]).astype(jnp.float32)
    keep = (jnp.arange(rank_max, dtype=jnp.int32)[None, None, :] < ranks[:, :, None]).astype(
        jnp.float32
    )
    field = misfit
    for step in range(APPS):
        coeff = jnp.einsum(
            "lsb,lkrb->lksr",
            field.astype(jnp.bfloat16),
            u_factors,
            preferred_element_type=jnp.float32,
        )
        tile_coeff = (coeff * keep[:, :, None, :]).astype(jnp.bfloat16)
        terms = jnp.einsum(
            "lksr,lkrb->lksb", tile_coeff, v_factors, preferred_element_type=jnp.float32
        )
        terms = terms.reshape(tiles, sources, unknowns)
        outgoing = jnp.zeros((peers * cap, sources, unknowns), jnp.float32).at[box].set(terms)
        incoming = lax.all_to_all(
            outgoing.reshape(peers, cap, sources, unknowns).astype(jnp.bfloat16),
            "rows",
            split_axis=0,
            concat_axis=0,
            tiled=True,
        ).astype(jnp.float32)
        field = misfit + contrast[:, None, :] * jnp.einsum(
            "eq,esb->qsb",
            pick,
            incoming.reshape(peers * cap, sources, unknowns),
            precision=lax.Precision.HIGHEST,
        )
    return field, jnp.sum(forward_fields.astype(jnp.float32) * field, axis=1)


def src_sum(x):
    count = lax.axis_size("src")
    if count & (count - 1):
        return lax.psum(x, "src")
    terms = [x]
    for step in range(1, count):
        terms.append(lax.ppermute(x, "src", [(i, i ^ step) for i in range(count)]))
    while len(terms) > 1:
        terms = [a + b for a, b in zip(terms[::2], terms[1::2])]
    return terms[0]


def per_device(
    misfit, forward_fields, contrast, u_factors, v_factors, ranks, tile_cols, owner_slot
):
    rows_dev, tiles_row = ranks.shape
    peers = lax.axis_size("rows")
    tiles = rows_dev * tiles_row
    cap = (tiles + peers - 1) // peers
    dense = (
        peers > 1
        and peers & (peers - 1) == 0
        and tiles == cap * peers
        and cap >= rows_dev
        and cap * u_factors.shape[2] % 128 == 0
        and misfit.shape[2] % 512 == 0
        and misfit.shape[1] % 16 == 0
    )
    run = slot_sums if dense else tile_terms
    field, partial_sum = run(
        misfit, forward_fields, contrast, u_factors, v_factors, ranks, tile_cols, owner_slot
    )
    total = src_sum(partial_sum)
    sources = misfit.shape[1] * lax.axis_size("src")
    gradient = total * lax.rsqrt(jnp.float32(sources))
    return (field, gradient)


def solution(mesh):
    placed = (
        P("rows", "src", None),
        P("rows", "src", None),
        P("rows", None),
        P("rows", None, None, None),
        P("rows", None, None, None),
        P("rows", None),
        P(),
        P(),
    )
    return jax.shard_map(
        per_device,
        mesh=mesh,
        in_specs=placed,
        out_specs=(P("rows", "src", None), P("rows", None)),
        check_vma=False,
    )
```

```python
import functools

import jax
import jax.numpy as jnp
from jax import lax
from jax.experimental import pallas as pl
from jax.experimental.pallas import tpu as pltpu
from jax.sharding import PartitionSpec as P

APPS = 4

def parts_of(unknowns, peers):
    bits = list(range(peers.bit_length() - 1))
    turned = bits[1:2] + bits[:1] + bits[2:]
    width = unknowns // 2
    return [(0, width, bits), (width, width, turned)]


def spot(order, rel):
    place = 0
    for bit in order:
        place = place * 2 + ((rel >> bit) & 1)
    return place


def in_order(order, peers):
    return sorted(range(peers), key=lambda rel: spot(order, rel))


def vmem(count):
    return [pl.BlockSpec(memory_space=pltpu.VMEM)] * count


def params():
    return pltpu.CompilerParams(vmem_limit_bytes=24 * 1024 * 1024)


def cost(rows, columns, sources):
    return pl.CostEstimate(
        flops=2 * rows * columns * sources, bytes_accessed=2 * rows * columns, transcendentals=0
    )


def in_vmem(x):
    return pltpu.with_memory_space_constraint(x, pltpu.VMEM)


def in_hbm(x):
    return pltpu.with_memory_space_constraint(x, pltpu.HBM)


def pick_rows(every, code, sources, rows_dev):
    row = code // rows_dev
    total = jnp.zeros((sources, every.shape[1]), jnp.float32)
    for index in range(rows_dev):
        mine = every[index * sources : (index + 1) * sources]
        total = total + jnp.where(row == index, mine, 0.0)
    return total


def by_slot(coeff, code, rows_dev):
    local = code % rows_dev
    low = [
        jnp.where(local == index, coeff, 0.0).astype(jnp.bfloat16) for index in range(rows_dev)
    ]
    return jnp.concatenate(low, axis=0)


def times_u(low, factors):
    return lax.dot_general(
        low, factors, (((1,), (1,)), ((), ())), preferred_element_type=jnp.float32
    )


def put_terms(lhs, v_ref, group, part, outs, rows_dev, peers):
    first, width, order = part
    deep = lhs.shape[1]
    terms = jnp.dot(
        lhs,
        v_ref[pl.ds(group * deep, deep), pl.ds(first, width)],
        preferred_element_type=jnp.float32,
    )
    place = spot(order, group)
    out = outs[place >= peers // 2]
    place = place % (peers // 2) * rows_dev
    out[place : place + rows_dev] = terms.reshape(rows_dev, -1, width).astype(out.dtype)


def start_kernel(dims, *refs):
    rows_dev, tiles_row, rank_max, peers, parts = dims
    cols_hbm, owner_hbm, ranks_hbm, misfit_hbm, u_hbm, v_hbm = refs[:6]
    u_ref, v_ref, code_ref = refs[6:9]
    outs = refs[9 : 9 + 2 * len(parts)]
    cols, owner, ranks, misfit, word_at, lhs_ref, small, u_sem, v_sem = refs[9 + 2 * len(parts) :]
    here, src = lax.axis_index("rows"), lax.axis_index("src")
    codes = rows_dev * rows_dev
    tiles = rows_dev * tiles_row
    group_tiles = tiles // peers
    deep = group_tiles * rank_max
    sources = misfit.shape[1]
    copies = [
        pltpu.make_async_copy(whence, to, small.at[i])
        for i, (whence, to) in enumerate(
            zip((cols_hbm, owner_hbm, ranks_hbm, misfit_hbm), (cols, owner, ranks, misfit))
        )
    ]
    for copy in copies:
        copy.start()
    for copy in copies[:3]:
        copy.wait()

    def load(whence, to, sem, tile, at, group):
        pltpu.make_async_copy(
            whence.at[pl.ds(pl.multiple_of(tile * rank_max, rank_max), rank_max)],
            to.at[pl.ds(pl.multiple_of(at * rank_max, rank_max), rank_max)],
            sem.at[group],
        ).start()

    def sort_tiles(k, filled):
        slots = [owner[cols[k, here * rows_dev + row]] for row in range(rows_dev)]
        for row, slot in enumerate(slots):
            rel = turned(jnp.bitwise_xor(lax.div(slot, rows_dev), here), peers, src)
            shift = rel * 4
            at = rel * group_tiles + (lax.shift_right_logical(filled, shift) & 15)
            filled = filled + lax.shift_left(jnp.int32(1), shift)
            tile = row * tiles_row + k
            word_at[at] = tile * codes + row * rows_dev + lax.rem(slot, rows_dev)
        return filled

    def load_all(whence, to, sem):
        def one(at, carry):
            load(whence, to, sem, lax.div(word_at[at], codes), at, lax.div(at, group_tiles))
            return carry

        lax.fori_loop(0, tiles, one, 0)

    def loaded(ref, sem, group):
        piece = ref.at[pl.ds(group * deep, deep)]
        pltpu.make_async_copy(piece, piece, sem.at[group]).wait()

    lax.fori_loop(0, tiles_row, sort_tiles, jnp.int32(0))
    load_all(u_hbm, u_ref, u_sem)
    load_all(v_hbm, v_ref, v_sem)
    lane = lax.broadcasted_iota(jnp.int32, (1, deep), 1)
    for group in range(peers):
        code = jnp.full((1, deep), -1, jnp.int32)
        for i in range(group_tiles):
            at = group * group_tiles + i
            word = word_at[at]
            tile = lax.div(word, codes)
            rank = ranks[lax.div(tile, tiles_row), lax.rem(tile, tiles_row)]
            inside = (lane >= i * rank_max) & (lane < i * rank_max + rank)
            code = jnp.where(inside, lax.rem(word, codes), code)
        code_ref[pl.ds(group, 1), :] = code
    copies[3].wait()
    low = misfit[...].astype(jnp.bfloat16).reshape(rows_dev * sources, -1)
    for group in range(peers):
        loaded(u_ref, u_sem, group)
        code = code_ref[pl.ds(group, 1), :]
        every = times_u(low, u_ref[pl.ds(group * deep, deep), :])
        lhs_ref[group] = by_slot(pick_rows(every, code, sources, rows_dev), code, rows_dev)
    for group in range(peers):
        loaded(v_ref, v_sem, group)
        lhs = lhs_ref[group]
        for i, part in enumerate(parts):
            put_terms(lhs, v_ref, group, part, outs[2 * i : 2 * i + 2], rows_dev, peers)


def low_field(base_ref, came_ref, contrast_ref, part):
    first, width, _ = part
    rows = []
    for row in range(base_ref.shape[0]):
        scale = contrast_ref[pl.ds(row, 1), pl.ds(first, width)]
        field = base_ref[row] + scale * came_ref[row].astype(jnp.float32)
        rows.append(field.astype(jnp.bfloat16))
    return jnp.concatenate(rows, axis=0)


def early_kernel(dims, parts, code_ref, contrast_ref, *refs):
    rows_dev, peers = dims
    fields, (u_ref, out_ref) = refs[: 2 * len(parts)], refs[2 * len(parts) :]
    deep = code_ref.shape[1]
    sources = out_ref.shape[1]
    lows = [
        low_field(fields[2 * i], fields[2 * i + 1], contrast_ref, part)
        for i, part in enumerate(parts)
    ]
    for group in range(peers):
        every = 0.0
        for low, (first, width, _) in zip(lows, parts):
            every = every + times_u(low, u_ref[pl.ds(group * deep, deep), pl.ds(first, width)])
        code = code_ref[pl.ds(group, 1), :]
        out_ref[group] = pick_rows(every, code, sources, rows_dev)


def ready_kernel(dims, late, parts, code_ref, contrast_ref, sum_ref, base_ref, came_ref, *refs):
    rows_dev, peers = dims
    u_ref, v_ref, lhs_ref = refs[:3]
    outs = refs[3:]
    deep = code_ref.shape[1]
    sources = sum_ref.shape[1]
    low = low_field(base_ref, came_ref, contrast_ref, late)
    first, width, _ = late
    for group in reversed(range(peers)):
        every = times_u(low, u_ref[pl.ds(group * deep, deep), pl.ds(first, width)])
        code = code_ref[pl.ds(group, 1), :]
        coeff = sum_ref[group] + pick_rows(every, code, sources, rows_dev)
        lhs = by_slot(coeff, code, rows_dev)
        lhs_ref[group] = lhs
        for out, part in zip(outs, parts):
            if spot(part[2], group) >= peers // 2:
                put_terms(lhs, v_ref, group, part, (None, out), rows_dev, peers)


def more_kernel(dims, parts, lhs_ref, v_ref, *outs):
    rows_dev, peers = dims
    for out, (part, kept) in zip(outs, parts):
        for group in range(peers):
            if (spot(part[2], group) < peers // 2) == kept:
                put_terms(lhs_ref[group], v_ref, group, part, (out, out), rows_dev, peers)


def finish_kernel(parts, contrast_ref, forward_ref, *refs):
    fields, (field_ref, total_ref) = refs[: 2 * len(parts)], refs[2 * len(parts) :]
    for i, (first, width, _) in enumerate(parts):
        here = pl.ds(first, width)
        for row in range(field_ref.shape[0]):
            scale = contrast_ref[pl.ds(row, 1), here]
            field = fields[2 * i][row] + scale * fields[2 * i + 1][row].astype(jnp.float32)
            field_ref[row, :, here] = field
            product = forward_ref[row, :, here].astype(jnp.float32) * field
            total_ref[pl.ds(row, 1), here] = jnp.sum(product, axis=0, keepdims=True)


def turned(rel, peers, src):
    if peers < 4:
        return rel
    swapped = (rel >> 2 << 2) | ((rel & 1) << 1) | ((rel >> 1) & 1)
    odd = src % 2
    return swapped * odd + rel * (1 - odd)


def swap(x, bit, peers):
    count = lax.axis_size("src")
    pairs = [
        (row * count + src, (row ^ turned(1 << bit, peers, src)) * count + src)
        for row in range(peers)
        for src in range(count)
    ]
    return lax.ppermute(x, ("rows", "src"), pairs)


def slot_sums(
    misfit, forward_fields, contrast, u_factors, v_factors, ranks, tile_cols, owner_slot
):
    peers = lax.axis_size("rows")
    rows_dev, tiles_row, rank_max, unknowns = u_factors.shape
    sources = misfit.shape[1]
    tiles = rows_dev * tiles_row
    deep = tiles // peers * rank_max
    parts = parts_of(unknowns, peers)
    first_sent, late = [0], 1
    early = [i for i in range(len(parts)) if i != late]
    half = (peers // 2 * rows_dev, sources)
    sent = [jax.ShapeDtypeStruct((*half, part[1]), jnp.bfloat16) for part in parts]
    kept = [jax.ShapeDtypeStruct((*half, part[1]), jnp.float32) for part in parts]
    u, v = (x.reshape(tiles * rank_max, unknowns) for x in (u_factors, v_factors))
    hbm = [pl.BlockSpec(memory_space=pl.ANY)]
    smem = lambda *shape: pltpu.SMEM(shape, jnp.int32)
    u, v, code, *got = pl.pallas_call(
        functools.partial(start_kernel, (rows_dev, tiles_row, rank_max, peers, parts)),
        out_shape=[pltpu.VMEM(x.shape, x.dtype) for x in (u, v)]
        + [jax.ShapeDtypeStruct((peers, deep), jnp.int32)]
        + [x for pair in zip(kept, sent) for x in pair],
        in_specs=hbm * 6,
        out_specs=vmem(3 + 2 * len(parts)),
        scratch_shapes=[
            smem(*tile_cols.shape[::-1]),
            smem(*owner_slot.shape),
            smem(*ranks.shape),
            pltpu.VMEM(misfit.shape, misfit.dtype),
            smem(tiles),
            pltpu.VMEM((peers, rows_dev * sources, deep), jnp.bfloat16),
            pltpu.SemaphoreType.DMA((4,)),
            pltpu.SemaphoreType.DMA((peers,)),
            pltpu.SemaphoreType.DMA((peers,)),
        ],
        compiler_params=params(),
        cost_estimate=cost(2 * tiles * rank_max, unknowns, sources),
        name="start",
    )(*(in_hbm(x) for x in (tile_cols.T, owner_slot, ranks, misfit, u, v)))
    dims = (rows_dev, peers)
    scale = contrast[:, None, :]
    columns = [(slice(None), slice(None), slice(part[0], part[0] + part[1])) for part in parts]
    for step in range(APPS):
        if step == 0:
            keeps, goes = list(got[::2]), list(got[1::2])
        else:
            coeff = pl.pallas_call(
                functools.partial(early_kernel, dims, [parts[i] for i in early]),
                out_shape=jax.ShapeDtypeStruct((peers, sources, deep), jnp.float32),
                in_specs=vmem(3 + 2 * len(early)),
                out_specs=vmem(1)[0],
                compiler_params=params(),
                cost_estimate=cost(u.shape[0], unknowns // 2, sources),
                name="early",
            )(code, contrast, *(x for i in early for x in (base[i], came[i])), in_vmem(u))
            lhs, *some = pl.pallas_call(
                functools.partial(ready_kernel, dims, parts[late], [parts[i] for i in first_sent]),
                out_shape=[jax.ShapeDtypeStruct((peers, rows_dev * sources, deep), jnp.bfloat16)]
                + [sent[i] for i in first_sent],
                in_specs=vmem(7),
                out_specs=vmem(1 + len(first_sent)),
                compiler_params=params(),
                cost_estimate=cost(u.shape[0], unknowns // 2, sources),
                name="ready",
            )(code, contrast, coeff, base[late], came[late], in_vmem(u), in_vmem(v))
            goes, keeps = [*some], []
            for names, shapes, to in (
                [[(parts[1], False)], sent[1:], goes],
                [[(part, True) for part in parts], kept, keeps],
            ):
                to += pl.pallas_call(
                    functools.partial(more_kernel, dims, names),
                    out_shape=shapes,
                    in_specs=vmem(2),
                    out_specs=vmem(len(shapes)),
                    compiler_params=params(),
                    cost_estimate=cost(u.shape[0], unknowns // 4 * len(shapes), sources),
                    name="more",
                )(lhs, in_vmem(v))
        base, came = [None] * len(parts), [None] * len(parts)
        levels = len(parts[0][2])
        for level in range(levels):
            for i, part in enumerate(parts):
                came[i] = swap(goes[i], part[2][level], peers)
                if level < levels - 1:
                    mid = keeps[i].shape[0] // 2
                    goes[i] = keeps[i][mid:] + came[i][mid:].astype(jnp.float32)
                    goes[i] = goes[i].astype(jnp.bfloat16)
                    keeps[i] = keeps[i][:mid] + came[i][:mid].astype(jnp.float32)
        for i in range(len(parts)):
            base[i] = misfit[columns[i]] + scale[columns[i]] * keeps[i]
    return pl.pallas_call(
        functools.partial(finish_kernel, parts),
        out_shape=[
            jax.ShapeDtypeStruct(misfit.shape, jnp.float32),
            jax.ShapeDtypeStruct(contrast.shape, jnp.float32),
        ],
        in_specs=vmem(2 + 2 * len(parts)),
        out_specs=vmem(2),
        compiler_params=params(),
        name="finish",
    )(contrast, forward_fields, *(x for pair in zip(base, came) for x in pair))


def route_tiles(tile_cols, owner_slot, rows_dev, peers):
    tiles = rows_dev * tile_cols.shape[1]
    target_slot = owner_slot[tile_cols.reshape(peers, tiles)]
    target_dev = target_slot // rows_dev
    local_slot = target_slot % rows_dev
    same = target_dev[:, :, None] == target_dev[:, None, :]
    before = jnp.arange(tiles)[None, :] < jnp.arange(tiles)[:, None]
    order = jnp.sum(jnp.where(same & before[None, :, :], 1, 0), axis=2).astype(jnp.int32)
    return target_dev, local_slot, order


def tile_terms(
    misfit, forward_fields, contrast, u_factors, v_factors, ranks, tile_cols, owner_slot
):
    rows_dev, tiles_row, rank_max, unknowns = u_factors.shape
    tiles = rows_dev * tiles_row
    peers = lax.axis_size("rows")
    cap = (tiles + peers - 1) // peers
    sources = misfit.shape[1]
    here = lax.axis_index("rows")
    target_dev, local_slot, order = route_tiles(tile_cols, owner_slot, rows_dev, peers)
    mine_dev = lax.dynamic_index_in_dim(target_dev, here, 0, keepdims=False)
    mine_order = lax.dynamic_index_in_dim(order, here, 0, keepdims=False)
    box = mine_dev * cap + mine_order
    sender = jnp.arange(peers, dtype=jnp.int32)[:, None] * cap + order
    entry = jnp.where(target_dev == here, sender, peers * cap).reshape(-1)
    arrival = (
        jnp.full((peers * cap,), -1, jnp.int32).at[entry].set(local_slot.reshape(-1), mode="drop")
    )
    pick = (arrival[:, None] == jnp.arange(rows_dev, dtype=jnp.int32)[None, :]).astype(jnp.float32)
    keep = (jnp.arange(rank_max, dtype=jnp.int32)[None, None, :] < ranks[:, :, None]).astype(
        jnp.float32
    )
    field = misfit
    for step in range(APPS):
        coeff = jnp.einsum(
            "lsb,lkrb->lksr",
            field.astype(jnp.bfloat16),
            u_factors,
            preferred_element_type=jnp.float32,
        )
        tile_coeff = (coeff * keep[:, :, None, :]).astype(jnp.bfloat16)
        terms = jnp.einsum(
            "lksr,lkrb->lksb", tile_coeff, v_factors, preferred_element_type=jnp.float32
        )
        terms = terms.reshape(tiles, sources, unknowns)
        outgoing = jnp.zeros((peers * cap, sources, unknowns), jnp.float32).at[box].set(terms)
        incoming = lax.all_to_all(
            outgoing.reshape(peers, cap, sources, unknowns).astype(jnp.bfloat16),
            "rows",
            split_axis=0,
            concat_axis=0,
            tiled=True,
        ).astype(jnp.float32)
        field = misfit + contrast[:, None, :] * jnp.einsum(
            "eq,esb->qsb",
            pick,
            incoming.reshape(peers * cap, sources, unknowns),
            precision=lax.Precision.HIGHEST,
        )
    return field, jnp.sum(forward_fields.astype(jnp.float32) * field, axis=1)


def src_sum(x):
    count = lax.axis_size("src")
    if count & (count - 1):
        return lax.psum(x, "src")
    terms = [x]
    for step in range(1, count):
        terms.append(lax.ppermute(x, "src", [(i, i ^ step) for i in range(count)]))
    while len(terms) > 1:
        terms = [a + b for a, b in zip(terms[::2], terms[1::2])]
    return terms[0]


def per_device(
    misfit, forward_fields, contrast, u_factors, v_factors, ranks, tile_cols, owner_slot
):
    rows_dev, tiles_row = ranks.shape
    peers = lax.axis_size("rows")
    tiles = rows_dev * tiles_row
    cap = (tiles + peers - 1) // peers
    dense = (
        1 < peers <= 8
        and cap < 16
        and peers & (peers - 1) == 0
        and tiles == cap * peers
        and cap >= rows_dev
        and cap * u_factors.shape[2] % 128 == 0
        and misfit.shape[2] % 512 == 0
        and misfit.shape[1] % 16 == 0
    )
    run = slot_sums if dense else tile_terms
    field, partial_sum = run(
        misfit, forward_fields, contrast, u_factors, v_factors, ranks, tile_cols, owner_slot
    )
    total = src_sum(partial_sum)
    sources = misfit.shape[1] * lax.axis_size("src")
    gradient = total * lax.rsqrt(jnp.float32(sources))
    return (field, gradient)


def solution(mesh):
    placed = (
        P("rows", "src", None),
        P("rows", "src", None),
        P("rows", None),
        P("rows", None, None, None),
        P("rows", None, None, None),
        P("rows", None),
        P(),
        P(),
    )
    return jax.shard_map(
        per_device,
        mesh=mesh,
        in_specs=placed,
        out_specs=(P("rows", "src", None), P("rows", None)),
        check_vma=False,
    )
```

```python
import functools

import jax
import jax.numpy as jnp
from jax import lax
from jax.experimental import pallas as pl
from jax.experimental.pallas import tpu as pltpu
from jax.sharding import PartitionSpec as P

APPS = 4

def parts_of(unknowns, peers):
    bits = list(range(peers.bit_length() - 1))
    width = unknowns // 2
    return [(0, width, bits), (width, width, bits)]


def spot(order, rel):
    place = 0
    for bit in order:
        place = place * 2 + ((rel >> bit) & 1)
    return place


def in_order(order, peers):
    return sorted(range(peers), key=lambda rel: spot(order, rel))


def vmem(count):
    return [pl.BlockSpec(memory_space=pltpu.VMEM)] * count


def params():
    return pltpu.CompilerParams(vmem_limit_bytes=24 * 1024 * 1024)


def cost(rows, columns, sources):
    return pl.CostEstimate(
        flops=2 * rows * columns * sources, bytes_accessed=2 * rows * columns, transcendentals=0
    )


def in_vmem(x):
    return pltpu.with_memory_space_constraint(x, pltpu.VMEM)


def in_hbm(x):
    return pltpu.with_memory_space_constraint(x, pltpu.HBM)


def pick_rows(every, code, sources, rows_dev):
    row = code // rows_dev
    total = jnp.zeros((sources, every.shape[1]), jnp.float32)
    for index in range(rows_dev):
        mine = every[index * sources : (index + 1) * sources]
        total = total + jnp.where(row == index, mine, 0.0)
    return total


def by_slot(coeff, code, rows_dev):
    local = code % rows_dev
    low = [
        jnp.where(local == index, coeff, 0.0).astype(jnp.bfloat16) for index in range(rows_dev)
    ]
    return jnp.concatenate(low, axis=0)


def times_u(low, factors):
    return lax.dot_general(
        low, factors, (((1,), (1,)), ((), ())), preferred_element_type=jnp.float32
    )


def put_terms(lhs, v_ref, group, part, outs, rows_dev, peers):
    first, width, order = part
    deep = lhs.shape[1]
    terms = jnp.dot(
        lhs,
        v_ref[pl.ds(group * deep, deep), pl.ds(first, width)],
        preferred_element_type=jnp.float32,
    )
    place = spot(order, group)
    out = outs[place >= peers // 2]
    place = place % (peers // 2) * rows_dev
    out[place : place + rows_dev] = terms.reshape(rows_dev, -1, width).astype(out.dtype)


def start_kernel(dims, *refs):
    rows_dev, tiles_row, rank_max, peers, parts = dims
    cols_hbm, owner_hbm, ranks_hbm, misfit_hbm, u_hbm, v_hbm = refs[:6]
    u_ref, v_ref, code_ref = refs[6:9]
    outs = refs[9 : 9 + 2 * len(parts)]
    cols, owner, ranks, misfit, word_at, lhs_ref, small, u_sem, v_sem = refs[9 + 2 * len(parts) :]
    here, src = lax.axis_index("rows"), lax.axis_index("src")
    codes = rows_dev * rows_dev
    tiles = rows_dev * tiles_row
    group_tiles = tiles // peers
    deep = group_tiles * rank_max
    sources = misfit.shape[1]
    copies = [
        pltpu.make_async_copy(whence, to, small.at[i])
        for i, (whence, to) in enumerate(
            zip((cols_hbm, owner_hbm, ranks_hbm, misfit_hbm), (cols, owner, ranks, misfit))
        )
    ]
    for copy in copies:
        copy.start()
    for copy in copies[:3]:
        copy.wait()

    def load(whence, to, sem, tile, at, group):
        pltpu.make_async_copy(
            whence.at[pl.ds(pl.multiple_of(tile * rank_max, rank_max), rank_max)],
            to.at[pl.ds(pl.multiple_of(at * rank_max, rank_max), rank_max)],
            sem.at[group],
        ).start()

    def sort_tiles(k, filled):
        slots = [owner[cols[k, here * rows_dev + row]] for row in range(rows_dev)]
        for row, slot in enumerate(slots):
            rel = turned(jnp.bitwise_xor(lax.div(slot, rows_dev), here), peers, src)
            shift = rel * 4
            at = rel * group_tiles + (lax.shift_right_logical(filled, shift) & 15)
            filled = filled + lax.shift_left(jnp.int32(1), shift)
            tile = row * tiles_row + k
            word_at[at] = tile * codes + row * rows_dev + lax.rem(slot, rows_dev)
        return filled

    def load_all(whence, to, sem):
        def one(at, carry):
            load(whence, to, sem, lax.div(word_at[at], codes), at, lax.div(at, group_tiles))
            return carry

        lax.fori_loop(0, tiles, one, 0)

    def loaded(ref, sem, group):
        piece = ref.at[pl.ds(group * deep, deep)]
        pltpu.make_async_copy(piece, piece, sem.at[group]).wait()

    lax.fori_loop(0, tiles_row, sort_tiles, jnp.int32(0))
    load_all(u_hbm, u_ref, u_sem)
    load_all(v_hbm, v_ref, v_sem)
    lane = lax.broadcasted_iota(jnp.int32, (1, deep), 1)
    for group in range(peers):
        code = jnp.full((1, deep), -1, jnp.int32)
        for i in range(group_tiles):
            at = group * group_tiles + i
            word = word_at[at]
            tile = lax.div(word, codes)
            rank = ranks[lax.div(tile, tiles_row), lax.rem(tile, tiles_row)]
            inside = (lane >= i * rank_max) & (lane < i * rank_max + rank)
            code = jnp.where(inside, lax.rem(word, codes), code)
        code_ref[pl.ds(group, 1), :] = code
    copies[3].wait()
    low = misfit[...].astype(jnp.bfloat16).reshape(rows_dev * sources, -1)
    for group in range(peers):
        loaded(u_ref, u_sem, group)
        code = code_ref[pl.ds(group, 1), :]
        every = times_u(low, u_ref[pl.ds(group * deep, deep), :])
        lhs_ref[group] = by_slot(pick_rows(every, code, sources, rows_dev), code, rows_dev)
    for group in range(peers):
        loaded(v_ref, v_sem, group)
        lhs = lhs_ref[group]
        for i, part in enumerate(parts):
            put_terms(lhs, v_ref, group, part, outs[2 * i : 2 * i + 2], rows_dev, peers)


def low_field(base_ref, came_ref, contrast_ref, part):
    first, width, _ = part
    rows = []
    for row in range(base_ref.shape[0]):
        scale = contrast_ref[pl.ds(row, 1), pl.ds(first, width)]
        field = base_ref[row] + scale * came_ref[row].astype(jnp.float32)
        rows.append(field.astype(jnp.bfloat16))
    return jnp.concatenate(rows, axis=0)


def early_kernel(dims, parts, code_ref, contrast_ref, *refs):
    rows_dev, peers = dims
    fields, (u_ref, out_ref) = refs[: 2 * len(parts)], refs[2 * len(parts) :]
    deep = code_ref.shape[1]
    sources = out_ref.shape[1]
    lows = [
        low_field(fields[2 * i], fields[2 * i + 1], contrast_ref, part)
        for i, part in enumerate(parts)
    ]
    for group in range(peers):
        every = 0.0
        for low, (first, width, _) in zip(lows, parts):
            every = every + times_u(low, u_ref[pl.ds(group * deep, deep), pl.ds(first, width)])
        code = code_ref[pl.ds(group, 1), :]
        out_ref[group] = pick_rows(every, code, sources, rows_dev)


def complete(dims, late, group, low, code_ref, sum_ref, u_ref):
    rows_dev, _ = dims
    deep = code_ref.shape[1]
    first, width, _ = late
    every = times_u(low, u_ref[pl.ds(group * deep, deep), pl.ds(first, width)])
    code = code_ref[pl.ds(group, 1), :]
    coeff = sum_ref[group] + pick_rows(every, code, sum_ref.shape[1], rows_dev)
    return by_slot(coeff, code, rows_dev)


def ready_kernel(dims, late, part, groups, code_ref, contrast_ref, sum_ref, *refs):
    base_ref, came_ref, u_ref, v_ref, lhs_ref, out = refs
    rows_dev, peers = dims
    low = low_field(base_ref, came_ref, contrast_ref, late)
    for i, group in enumerate(groups):
        lhs = complete(dims, late, group, low, code_ref, sum_ref, u_ref)
        lhs_ref[i] = lhs
        put_terms(lhs, v_ref, group, part, (None, out), rows_dev, peers)


def more_kernel(dims, part, groups, lhs_ref, v_ref, out):
    rows_dev, peers = dims
    for i, group in enumerate(groups):
        put_terms(lhs_ref[i], v_ref, group, part, (None, out), rows_dev, peers)


def rest_kernel(dims, late, parts, groups, code_ref, contrast_ref, sum_ref, *refs):
    base_ref, came_ref, u_ref, v_ref, *outs = refs
    rows_dev, peers = dims
    low = low_field(base_ref, came_ref, contrast_ref, late)
    for group in groups:
        lhs = complete(dims, late, group, low, code_ref, sum_ref, u_ref)
        for out, part in zip(outs, parts):
            put_terms(lhs, v_ref, group, part, (out, None), rows_dev, peers)


def finish_kernel(parts, contrast_ref, forward_ref, *refs):
    fields, (field_ref, total_ref) = refs[: 2 * len(parts)], refs[2 * len(parts) :]
    for i, (first, width, _) in enumerate(parts):
        here = pl.ds(first, width)
        for row in range(field_ref.shape[0]):
            scale = contrast_ref[pl.ds(row, 1), here]
            field = fields[2 * i][row] + scale * fields[2 * i + 1][row].astype(jnp.float32)
            field_ref[row, :, here] = field
            product = forward_ref[row, :, here].astype(jnp.float32) * field
            total_ref[pl.ds(row, 1), here] = jnp.sum(product, axis=0, keepdims=True)


def turned(rel, peers, src):
    if peers < 4:
        return rel
    swapped = (rel >> 2 << 2) | ((rel & 1) << 1) | ((rel >> 1) & 1)
    odd = src % 2
    return swapped * odd + rel * (1 - odd)


def swap(x, bit, peers):
    count = lax.axis_size("src")
    pairs = [
        (row * count + src, (row ^ turned(1 << bit, peers, src)) * count + src)
        for row in range(peers)
        for src in range(count)
    ]
    return lax.ppermute(x, ("rows", "src"), pairs)


def slot_sums(
    misfit, forward_fields, contrast, u_factors, v_factors, ranks, tile_cols, owner_slot
):
    peers = lax.axis_size("rows")
    rows_dev, tiles_row, rank_max, unknowns = u_factors.shape
    sources = misfit.shape[1]
    tiles = rows_dev * tiles_row
    deep = tiles // peers * rank_max
    parts = parts_of(unknowns, peers)
    late = 1
    staying, leaving = (
        [group for group in range(peers) if (spot(parts[0][2], group) >= peers // 2) == goes]
        for goes in (False, True)
    )
    early = [i for i in range(len(parts)) if i != late]
    half = (peers // 2 * rows_dev, sources)
    sent = [jax.ShapeDtypeStruct((*half, part[1]), jnp.bfloat16) for part in parts]
    kept = [jax.ShapeDtypeStruct((*half, part[1]), jnp.float32) for part in parts]
    u, v = (x.reshape(tiles * rank_max, unknowns) for x in (u_factors, v_factors))
    hbm = [pl.BlockSpec(memory_space=pl.ANY)]
    smem = lambda *shape: pltpu.SMEM(shape, jnp.int32)
    u, v, code, *got = pl.pallas_call(
        functools.partial(start_kernel, (rows_dev, tiles_row, rank_max, peers, parts)),
        out_shape=[pltpu.VMEM(x.shape, x.dtype) for x in (u, v)]
        + [jax.ShapeDtypeStruct((peers, deep), jnp.int32)]
        + [x for pair in zip(kept, sent) for x in pair],
        in_specs=hbm * 6,
        out_specs=vmem(3 + 2 * len(parts)),
        scratch_shapes=[
            smem(*tile_cols.shape[::-1]),
            smem(*owner_slot.shape),
            smem(*ranks.shape),
            pltpu.VMEM(misfit.shape, misfit.dtype),
            smem(tiles),
            pltpu.VMEM((peers, rows_dev * sources, deep), jnp.bfloat16),
            pltpu.SemaphoreType.DMA((4,)),
            pltpu.SemaphoreType.DMA((peers,)),
            pltpu.SemaphoreType.DMA((peers,)),
        ],
        compiler_params=params(),
        cost_estimate=cost(2 * tiles * rank_max, unknowns, sources),
        name="start",
    )(*(in_hbm(x) for x in (tile_cols.T, owner_slot, ranks, misfit, u, v)))
    dims = (rows_dev, peers)
    scale = contrast[:, None, :]
    columns = [(slice(None), slice(None), slice(part[0], part[0] + part[1])) for part in parts]
    for step in range(APPS):
        if step == 0:
            keeps, goes = list(got[::2]), list(got[1::2])
        else:
            coeff = pl.pallas_call(
                functools.partial(early_kernel, dims, [parts[i] for i in early]),
                out_shape=jax.ShapeDtypeStruct((peers, sources, deep), jnp.float32),
                in_specs=vmem(3 + 2 * len(early)),
                out_specs=vmem(1)[0],
                compiler_params=params(),
                cost_estimate=cost(u.shape[0], unknowns // 2, sources),
                name="early",
            )(code, contrast, *(x for i in early for x in (base[i], came[i])), in_vmem(u))
            state = (code, contrast, coeff, base[late], came[late], in_vmem(u), in_vmem(v))
            lhs, ahead = pl.pallas_call(
                functools.partial(ready_kernel, dims, parts[late], parts[0], leaving),
                out_shape=[
                    jax.ShapeDtypeStruct((peers // 2, rows_dev * sources, deep), jnp.bfloat16),
                    sent[0],
                ],
                in_specs=vmem(7),
                out_specs=vmem(2),
                compiler_params=params(),
                cost_estimate=cost(u.shape[0], unknowns // 2, sources),
                name="ready",
            )(*state)
            behind = pl.pallas_call(
                functools.partial(more_kernel, dims, parts[1], leaving),
                out_shape=sent[1],
                in_specs=vmem(2),
                out_specs=vmem(1)[0],
                compiler_params=params(),
                cost_estimate=cost(u.shape[0], unknowns // 4, sources),
                name="more",
            )(lhs, in_vmem(v))
            goes = [ahead, behind]
            keeps = pl.pallas_call(
                functools.partial(rest_kernel, dims, parts[late], parts, staying),
                out_shape=kept,
                in_specs=vmem(7),
                out_specs=vmem(2),
                compiler_params=params(),
                cost_estimate=cost(u.shape[0], unknowns * 3 // 4, sources),
                name="rest",
            )(*state)
            keeps = list(keeps)
        base, came = [None] * len(parts), [None] * len(parts)
        levels = len(parts[0][2])
        for level in range(levels):
            for i, part in enumerate(parts):
                came[i] = swap(goes[i], part[2][level], peers)
                if level < levels - 1:
                    mid = keeps[i].shape[0] // 2
                    goes[i] = keeps[i][mid:] + came[i][mid:].astype(jnp.float32)
                    goes[i] = goes[i].astype(jnp.bfloat16)
                    keeps[i] = keeps[i][:mid] + came[i][:mid].astype(jnp.float32)
        for i in range(len(parts)):
            base[i] = misfit[columns[i]] + scale[columns[i]] * keeps[i]
    return pl.pallas_call(
        functools.partial(finish_kernel, parts),
        out_shape=[
            jax.ShapeDtypeStruct(misfit.shape, jnp.float32),
            jax.ShapeDtypeStruct(contrast.shape, jnp.float32),
        ],
        in_specs=vmem(2 + 2 * len(parts)),
        out_specs=vmem(2),
        compiler_params=params(),
        name="finish",
    )(contrast, forward_fields, *(x for pair in zip(base, came) for x in pair))


def route_tiles(tile_cols, owner_slot, rows_dev, peers):
    tiles = rows_dev * tile_cols.shape[1]
    target_slot = owner_slot[tile_cols.reshape(peers, tiles)]
    target_dev = target_slot // rows_dev
    local_slot = target_slot % rows_dev
    same = target_dev[:, :, None] == target_dev[:, None, :]
    before = jnp.arange(tiles)[None, :] < jnp.arange(tiles)[:, None]
    order = jnp.sum(jnp.where(same & before[None, :, :], 1, 0), axis=2).astype(jnp.int32)
    return target_dev, local_slot, order


def tile_terms(
    misfit, forward_fields, contrast, u_factors, v_factors, ranks, tile_cols, owner_slot
):
    rows_dev, tiles_row, rank_max, unknowns = u_factors.shape
    tiles = rows_dev * tiles_row
    peers = lax.axis_size("rows")
    cap = (tiles + peers - 1) // peers
    sources = misfit.shape[1]
    here = lax.axis_index("rows")
    target_dev, local_slot, order = route_tiles(tile_cols, owner_slot, rows_dev, peers)
    mine_dev = lax.dynamic_index_in_dim(target_dev, here, 0, keepdims=False)
    mine_order = lax.dynamic_index_in_dim(order, here, 0, keepdims=False)
    box = mine_dev * cap + mine_order
    sender = jnp.arange(peers, dtype=jnp.int32)[:, None] * cap + order
    entry = jnp.where(target_dev == here, sender, peers * cap).reshape(-1)
    arrival = (
        jnp.full((peers * cap,), -1, jnp.int32).at[entry].set(local_slot.reshape(-1), mode="drop")
    )
    pick = (arrival[:, None] == jnp.arange(rows_dev, dtype=jnp.int32)[None, :]).astype(jnp.float32)
    keep = (jnp.arange(rank_max, dtype=jnp.int32)[None, None, :] < ranks[:, :, None]).astype(
        jnp.float32
    )
    field = misfit
    for step in range(APPS):
        coeff = jnp.einsum(
            "lsb,lkrb->lksr",
            field.astype(jnp.bfloat16),
            u_factors,
            preferred_element_type=jnp.float32,
        )
        tile_coeff = (coeff * keep[:, :, None, :]).astype(jnp.bfloat16)
        terms = jnp.einsum(
            "lksr,lkrb->lksb", tile_coeff, v_factors, preferred_element_type=jnp.float32
        )
        terms = terms.reshape(tiles, sources, unknowns)
        outgoing = jnp.zeros((peers * cap, sources, unknowns), jnp.float32).at[box].set(terms)
        incoming = lax.all_to_all(
            outgoing.reshape(peers, cap, sources, unknowns).astype(jnp.bfloat16),
            "rows",
            split_axis=0,
            concat_axis=0,
            tiled=True,
        ).astype(jnp.float32)
        field = misfit + contrast[:, None, :] * jnp.einsum(
            "eq,esb->qsb",
            pick,
            incoming.reshape(peers * cap, sources, unknowns),
            precision=lax.Precision.HIGHEST,
        )
    return field, jnp.sum(forward_fields.astype(jnp.float32) * field, axis=1)


def src_sum(x):
    count = lax.axis_size("src")
    if count & (count - 1):
        return lax.psum(x, "src")
    terms = [x]
    for step in range(1, count):
        terms.append(lax.ppermute(x, "src", [(i, i ^ step) for i in range(count)]))
    while len(terms) > 1:
        terms = [a + b for a, b in zip(terms[::2], terms[1::2])]
    return terms[0]


def per_device(
    misfit, forward_fields, contrast, u_factors, v_factors, ranks, tile_cols, owner_slot
):
    rows_dev, tiles_row = ranks.shape
    peers = lax.axis_size("rows")
    tiles = rows_dev * tiles_row
    cap = (tiles + peers - 1) // peers
    dense = (
        1 < peers <= 8
        and cap < 16
        and peers & (peers - 1) == 0
        and tiles == cap * peers
        and cap >= rows_dev
        and cap * u_factors.shape[2] % 128 == 0
        and misfit.shape[2] % 512 == 0
        and misfit.shape[1] % 16 == 0
    )
    run = slot_sums if dense else tile_terms
    field, partial_sum = run(
        misfit, forward_fields, contrast, u_factors, v_factors, ranks, tile_cols, owner_slot
    )
    total = src_sum(partial_sum)
    sources = misfit.shape[1] * lax.axis_size("src")
    gradient = total * lax.rsqrt(jnp.float32(sources))
    return (field, gradient)


def solution(mesh):
    placed = (
        P("rows", "src", None),
        P("rows", "src", None),
        P("rows", None),
        P("rows", None, None, None),
        P("rows", None, None, None),
        P("rows", None),
        P(),
        P(),
    )
    return jax.shard_map(
        per_device,
        mesh=mesh,
        in_specs=placed,
        out_specs=(P("rows", "src", None), P("rows", None)),
        check_vma=False,
    )
```

```python
import functools

import jax
import jax.numpy as jnp
from jax import lax
from jax.experimental import pallas as pl
from jax.experimental.pallas import tpu as pltpu
from jax.sharding import PartitionSpec as P

APPS = 4

def parts_of(unknowns, peers):
    bits = list(range(peers.bit_length() - 1))
    turned = bits[1:2] + bits[:1] + bits[2:]
    width = unknowns // 2
    return [(0, width, bits), (width, width, turned)]


def spot(order, rel):
    place = 0
    for bit in order:
        place = place * 2 + ((rel >> bit) & 1)
    return place


def in_order(order, peers):
    return sorted(range(peers), key=lambda rel: spot(order, rel))


def vmem(count):
    return [pl.BlockSpec(memory_space=pltpu.VMEM)] * count


def params():
    return pltpu.CompilerParams(vmem_limit_bytes=24 * 1024 * 1024)


def cost(rows, columns, sources):
    return pl.CostEstimate(
        flops=2 * rows * columns * sources, bytes_accessed=2 * rows * columns, transcendentals=0
    )


def in_vmem(x):
    return pltpu.with_memory_space_constraint(x, pltpu.VMEM)


def in_hbm(x):
    return pltpu.with_memory_space_constraint(x, pltpu.HBM)


def pick_rows(every, code, sources, rows_dev):
    row = code // rows_dev
    total = jnp.zeros((sources, every.shape[1]), jnp.float32)
    for index in range(rows_dev):
        mine = every[index * sources : (index + 1) * sources]
        total = total + jnp.where(row == index, mine, 0.0)
    return total


def by_slot(coeff, code, rows_dev):
    local = code % rows_dev
    low = [
        jnp.where(local == index, coeff, 0.0).astype(jnp.bfloat16) for index in range(rows_dev)
    ]
    return jnp.concatenate(low, axis=0)


def times_u(low, factors):
    return lax.dot_general(
        low, factors, (((1,), (1,)), ((), ())), preferred_element_type=jnp.float32
    )


def put_terms(lhs, v_ref, group, part, outs, rows_dev, peers):
    first, width, order = part
    deep = lhs.shape[1]
    terms = jnp.dot(
        lhs,
        v_ref[pl.ds(group * deep, deep), pl.ds(first, width)],
        preferred_element_type=jnp.float32,
    )
    place = spot(order, group)
    out = outs[place >= peers // 2]
    place = place % (peers // 2) * rows_dev
    out[place : place + rows_dev] = terms.reshape(rows_dev, -1, width).astype(out.dtype)


def start_kernel(dims, *refs):
    rows_dev, tiles_row, rank_max, peers, parts = dims
    cols_hbm, owner_hbm, ranks_hbm, misfit_hbm, u_hbm, v_hbm = refs[:6]
    u_ref, v_ref, code_ref = refs[6:9]
    outs = refs[9 : 9 + 2 * len(parts)]
    cols, owner, ranks, misfit, word_at, lhs_ref, small, u_sem, v_sem = refs[9 + 2 * len(parts) :]
    here, src = lax.axis_index("rows"), lax.axis_index("src")
    codes = rows_dev * rows_dev
    tiles = rows_dev * tiles_row
    group_tiles = tiles // peers
    deep = group_tiles * rank_max
    sources = misfit.shape[1]
    copies = [
        pltpu.make_async_copy(whence, to, small.at[i])
        for i, (whence, to) in enumerate(
            zip((cols_hbm, owner_hbm, ranks_hbm, misfit_hbm), (cols, owner, ranks, misfit))
        )
    ]
    for copy in copies:
        copy.start()
    for copy in copies[:3]:
        copy.wait()

    def load(whence, to, sem, tile, at, group):
        pltpu.make_async_copy(
            whence.at[pl.ds(pl.multiple_of(tile * rank_max, rank_max), rank_max)],
            to.at[pl.ds(pl.multiple_of(at * rank_max, rank_max), rank_max)],
            sem.at[group],
        ).start()

    def sort_tiles(k, filled):
        slots = [owner[cols[k, here * rows_dev + row]] for row in range(rows_dev)]
        for row, slot in enumerate(slots):
            rel = turned(jnp.bitwise_xor(lax.div(slot, rows_dev), here), peers, src)
            shift = rel * 4
            at = rel * group_tiles + (lax.shift_right_logical(filled, shift) & 15)
            filled = filled + lax.shift_left(jnp.int32(1), shift)
            tile = row * tiles_row + k
            word_at[at] = tile * codes + row * rows_dev + lax.rem(slot, rows_dev)
        return filled

    def load_all(whence, to, sem):
        def one(at, carry):
            load(whence, to, sem, lax.div(word_at[at], codes), at, lax.div(at, group_tiles))
            return carry

        lax.fori_loop(0, tiles, one, 0)

    def loaded(ref, sem, group):
        piece = ref.at[pl.ds(group * deep, deep)]
        pltpu.make_async_copy(piece, piece, sem.at[group]).wait()

    lax.fori_loop(0, tiles_row, sort_tiles, jnp.int32(0))
    load_all(u_hbm, u_ref, u_sem)
    load_all(v_hbm, v_ref, v_sem)
    lane = lax.broadcasted_iota(jnp.int32, (1, deep), 1)
    for group in range(peers):
        code = jnp.full((1, deep), -1, jnp.int32)
        for i in range(group_tiles):
            at = group * group_tiles + i
            word = word_at[at]
            tile = lax.div(word, codes)
            rank = ranks[lax.div(tile, tiles_row), lax.rem(tile, tiles_row)]
            inside = (lane >= i * rank_max) & (lane < i * rank_max + rank)
            code = jnp.where(inside, lax.rem(word, codes), code)
        code_ref[pl.ds(group, 1), :] = code
    copies[3].wait()
    low = misfit[...].astype(jnp.bfloat16).reshape(rows_dev * sources, -1)
    for group in range(peers):
        loaded(u_ref, u_sem, group)
        code = code_ref[pl.ds(group, 1), :]
        every = times_u(low, u_ref[pl.ds(group * deep, deep), :])
        lhs_ref[group] = by_slot(pick_rows(every, code, sources, rows_dev), code, rows_dev)
    for group in range(peers):
        loaded(v_ref, v_sem, group)
        lhs = lhs_ref[group]
        for i, part in enumerate(parts):
            put_terms(lhs, v_ref, group, part, outs[2 * i : 2 * i + 2], rows_dev, peers)


def low_field(base_ref, came_ref, contrast_ref, part):
    first, width, _ = part
    rows = []
    for row in range(base_ref.shape[0]):
        scale = contrast_ref[pl.ds(row, 1), pl.ds(first, width)]
        field = base_ref[row] + scale * came_ref[row].astype(jnp.float32)
        rows.append(field.astype(jnp.bfloat16))
    return jnp.concatenate(rows, axis=0)


def early_kernel(dims, parts, code_ref, contrast_ref, *refs):
    rows_dev, peers = dims
    fields, (u_ref, out_ref) = refs[: 2 * len(parts)], refs[2 * len(parts) :]
    deep = code_ref.shape[1]
    sources = out_ref.shape[1]
    lows = [
        low_field(fields[2 * i], fields[2 * i + 1], contrast_ref, part)
        for i, part in enumerate(parts)
    ]
    for group in range(peers):
        every = 0.0
        for low, (first, width, _) in zip(lows, parts):
            every = every + times_u(low, u_ref[pl.ds(group * deep, deep), pl.ds(first, width)])
        code = code_ref[pl.ds(group, 1), :]
        out_ref[group] = pick_rows(every, code, sources, rows_dev)


def complete(dims, late, group, low, code_ref, sum_ref, u_ref):
    rows_dev, _ = dims
    deep = code_ref.shape[1]
    first, width, _ = late
    every = times_u(low, u_ref[pl.ds(group * deep, deep), pl.ds(first, width)])
    code = code_ref[pl.ds(group, 1), :]
    coeff = sum_ref[group] + pick_rows(every, code, sum_ref.shape[1], rows_dev)
    return by_slot(coeff, code, rows_dev)


def step_kernel(dims, late, known, todo, parts, code_ref, contrast_ref, sum_ref, *refs):
    base_ref, came_ref, u_ref, v_ref = refs[:4]
    held, refs = refs[4 : 4 + len(known)], refs[4 + len(known) :]
    rows_dev, peers = dims
    low = low_field(base_ref, came_ref, contrast_ref, late)
    ready = {group: (ref, i) for ref, some in zip(held, known) for i, group in enumerate(some)}
    outs, lhs_ref = refs[: len(parts)], refs[len(parts) :]

    def put(lhs, group):
        for out, (part, kept) in zip(outs, parts):
            if (spot(part[2], group) < peers // 2) == kept:
                put_terms(lhs, v_ref, group, part, (out, out), rows_dev, peers)

    for i, group in enumerate(todo):
        lhs = complete(dims, late, group, low, code_ref, sum_ref, u_ref)
        if lhs_ref:
            lhs_ref[0][i] = lhs
        put(lhs, group)
    for group, (ref, i) in ready.items():
        if any((spot(part[2], group) < peers // 2) == kept for part, kept in parts):
            put(ref[i], group)


def finish_kernel(parts, contrast_ref, forward_ref, *refs):
    fields, (field_ref, total_ref) = refs[: 2 * len(parts)], refs[2 * len(parts) :]
    for i, (first, width, _) in enumerate(parts):
        here = pl.ds(first, width)
        for row in range(field_ref.shape[0]):
            scale = contrast_ref[pl.ds(row, 1), here]
            field = fields[2 * i][row] + scale * fields[2 * i + 1][row].astype(jnp.float32)
            field_ref[row, :, here] = field
            product = forward_ref[row, :, here].astype(jnp.float32) * field
            total_ref[pl.ds(row, 1), here] = jnp.sum(product, axis=0, keepdims=True)


def turned(rel, peers, src):
    if peers < 4:
        return rel
    swapped = (rel >> 2 << 2) | ((rel & 1) << 1) | ((rel >> 1) & 1)
    odd = src % 2
    return swapped * odd + rel * (1 - odd)


def swap(x, bit, peers):
    count = lax.axis_size("src")
    pairs = [
        (row * count + src, (row ^ turned(1 << bit, peers, src)) * count + src)
        for row in range(peers)
        for src in range(count)
    ]
    return lax.ppermute(x, ("rows", "src"), pairs)


def slot_sums(
    misfit, forward_fields, contrast, u_factors, v_factors, ranks, tile_cols, owner_slot
):
    peers = lax.axis_size("rows")
    rows_dev, tiles_row, rank_max, unknowns = u_factors.shape
    sources = misfit.shape[1]
    tiles = rows_dev * tiles_row
    deep = tiles // peers * rank_max
    parts = parts_of(unknowns, peers)
    late = 1
    early = [i for i in range(len(parts)) if i != late]
    leaving, staying = [], list(range(peers))
    for part in parts:
        leaving.append([x for x in staying if spot(part[2], x) >= peers // 2])
        staying = [x for x in staying if x not in leaving[-1]]
    half = (peers // 2 * rows_dev, sources)
    sent = [jax.ShapeDtypeStruct((*half, part[1]), jnp.bfloat16) for part in parts]
    kept = [jax.ShapeDtypeStruct((*half, part[1]), jnp.float32) for part in parts]
    u, v = (x.reshape(tiles * rank_max, unknowns) for x in (u_factors, v_factors))
    hbm = [pl.BlockSpec(memory_space=pl.ANY)]
    smem = lambda *shape: pltpu.SMEM(shape, jnp.int32)
    u, v, code, *got = pl.pallas_call(
        functools.partial(start_kernel, (rows_dev, tiles_row, rank_max, peers, parts)),
        out_shape=[pltpu.VMEM(x.shape, x.dtype) for x in (u, v)]
        + [jax.ShapeDtypeStruct((peers, deep), jnp.int32)]
        + [x for pair in zip(kept, sent) for x in pair],
        in_specs=hbm * 6,
        out_specs=vmem(3 + 2 * len(parts)),
        scratch_shapes=[
            smem(*tile_cols.shape[::-1]),
            smem(*owner_slot.shape),
            smem(*ranks.shape),
            pltpu.VMEM(misfit.shape, misfit.dtype),
            smem(tiles),
            pltpu.VMEM((peers, rows_dev * sources, deep), jnp.bfloat16),
            pltpu.SemaphoreType.DMA((4,)),
            pltpu.SemaphoreType.DMA((peers,)),
            pltpu.SemaphoreType.DMA((peers,)),
        ],
        compiler_params=params(),
        cost_estimate=cost(2 * tiles * rank_max, unknowns, sources),
        name="start",
    )(*(in_hbm(x) for x in (tile_cols.T, owner_slot, ranks, misfit, u, v)))
    dims = (rows_dev, peers)
    scale = contrast[:, None, :]
    columns = [(slice(None), slice(None), slice(part[0], part[0] + part[1])) for part in parts]
    for step in range(APPS):
        if step == 0:
            keeps, goes = list(got[::2]), list(got[1::2])
        else:
            coeff = pl.pallas_call(
                functools.partial(early_kernel, dims, [parts[i] for i in early]),
                out_shape=jax.ShapeDtypeStruct((peers, sources, deep), jnp.float32),
                in_specs=vmem(3 + 2 * len(early)),
                out_specs=vmem(1)[0],
                compiler_params=params(),
                cost_estimate=cost(u.shape[0], unknowns // 2, sources),
                name="early",
            )(code, contrast, *(x for i in early for x in (base[i], came[i])), in_vmem(u))
            state = (code, contrast, coeff, base[late], came[late], in_vmem(u), in_vmem(v))
            known, held, made = [], [], []
            for todo, names, shapes in (
                (leaving[0], [(parts[0], False)], [sent[0]]),
                (leaving[1], [(parts[1], False)], [sent[1]]),
                (staying, [(part, True) for part in parts], kept),
            ):
                hand = []
                if todo is not staying:
                    shape = (len(todo), rows_dev * sources, deep)
                    hand = [jax.ShapeDtypeStruct(shape, jnp.bfloat16)]
                got = pl.pallas_call(
                    functools.partial(step_kernel, dims, parts[late], [*known], todo, names),
                    out_shape=[*shapes, *hand],
                    in_specs=vmem(7 + len(held)),
                    out_specs=vmem(len(shapes) + len(hand)),
                    compiler_params=params(),
                    cost_estimate=cost(u.shape[0], unknowns // 2, sources),
                    name="step",
                )(*state, *held)
                made += got[: len(shapes)]
                known.append(todo)
                held += got[len(shapes) :]
            goes, keeps = made[:2], made[2:]
        base, came = [None] * len(parts), [None] * len(parts)
        levels = len(parts[0][2])
        for level in range(levels):
            for i, part in enumerate(parts):
                came[i] = swap(goes[i], part[2][level], peers)
                if level < levels - 1:
                    mid = keeps[i].shape[0] // 2
                    goes[i] = keeps[i][mid:] + came[i][mid:].astype(jnp.float32)
                    goes[i] = goes[i].astype(jnp.bfloat16)
                    keeps[i] = keeps[i][:mid] + came[i][:mid].astype(jnp.float32)
        for i in range(len(parts)):
            base[i] = misfit[columns[i]] + scale[columns[i]] * keeps[i]
    return pl.pallas_call(
        functools.partial(finish_kernel, parts),
        out_shape=[
            jax.ShapeDtypeStruct(misfit.shape, jnp.float32),
            jax.ShapeDtypeStruct(contrast.shape, jnp.float32),
        ],
        in_specs=vmem(2 + 2 * len(parts)),
        out_specs=vmem(2),
        compiler_params=params(),
        name="finish",
    )(contrast, forward_fields, *(x for pair in zip(base, came) for x in pair))


def route_tiles(tile_cols, owner_slot, rows_dev, peers):
    tiles = rows_dev * tile_cols.shape[1]
    target_slot = owner_slot[tile_cols.reshape(peers, tiles)]
    target_dev = target_slot // rows_dev
    local_slot = target_slot % rows_dev
    same = target_dev[:, :, None] == target_dev[:, None, :]
    before = jnp.arange(tiles)[None, :] < jnp.arange(tiles)[:, None]
    order = jnp.sum(jnp.where(same & before[None, :, :], 1, 0), axis=2).astype(jnp.int32)
    return target_dev, local_slot, order


def tile_terms(
    misfit, forward_fields, contrast, u_factors, v_factors, ranks, tile_cols, owner_slot
):
    rows_dev, tiles_row, rank_max, unknowns = u_factors.shape
    tiles = rows_dev * tiles_row
    peers = lax.axis_size("rows")
    cap = (tiles + peers - 1) // peers
    sources = misfit.shape[1]
    here = lax.axis_index("rows")
    target_dev, local_slot, order = route_tiles(tile_cols, owner_slot, rows_dev, peers)
    mine_dev = lax.dynamic_index_in_dim(target_dev, here, 0, keepdims=False)
    mine_order = lax.dynamic_index_in_dim(order, here, 0, keepdims=False)
    box = mine_dev * cap + mine_order
    sender = jnp.arange(peers, dtype=jnp.int32)[:, None] * cap + order
    entry = jnp.where(target_dev == here, sender, peers * cap).reshape(-1)
    arrival = (
        jnp.full((peers * cap,), -1, jnp.int32).at[entry].set(local_slot.reshape(-1), mode="drop")
    )
    pick = (arrival[:, None] == jnp.arange(rows_dev, dtype=jnp.int32)[None, :]).astype(jnp.float32)
    keep = (jnp.arange(rank_max, dtype=jnp.int32)[None, None, :] < ranks[:, :, None]).astype(
        jnp.float32
    )
    field = misfit
    for step in range(APPS):
        coeff = jnp.einsum(
            "lsb,lkrb->lksr",
            field.astype(jnp.bfloat16),
            u_factors,
            preferred_element_type=jnp.float32,
        )
        tile_coeff = (coeff * keep[:, :, None, :]).astype(jnp.bfloat16)
        terms = jnp.einsum(
            "lksr,lkrb->lksb", tile_coeff, v_factors, preferred_element_type=jnp.float32
        )
        terms = terms.reshape(tiles, sources, unknowns)
        outgoing = jnp.zeros((peers * cap, sources, unknowns), jnp.float32).at[box].set(terms)
        incoming = lax.all_to_all(
            outgoing.reshape(peers, cap, sources, unknowns).astype(jnp.bfloat16),
            "rows",
            split_axis=0,
            concat_axis=0,
            tiled=True,
        ).astype(jnp.float32)
        field = misfit + contrast[:, None, :] * jnp.einsum(
            "eq,esb->qsb",
            pick,
            incoming.reshape(peers * cap, sources, unknowns),
            precision=lax.Precision.HIGHEST,
        )
    return field, jnp.sum(forward_fields.astype(jnp.float32) * field, axis=1)


def src_sum(x):
    count = lax.axis_size("src")
    if count & (count - 1):
        return lax.psum(x, "src")
    terms = [x]
    for step in range(1, count):
        terms.append(lax.ppermute(x, "src", [(i, i ^ step) for i in range(count)]))
    while len(terms) > 1:
        terms = [a + b for a, b in zip(terms[::2], terms[1::2])]
    return terms[0]


def per_device(
    misfit, forward_fields, contrast, u_factors, v_factors, ranks, tile_cols, owner_slot
):
    rows_dev, tiles_row = ranks.shape
    peers = lax.axis_size("rows")
    tiles = rows_dev * tiles_row
    cap = (tiles + peers - 1) // peers
    dense = (
        4 <= peers <= 8
        and cap < 16
        and peers & (peers - 1) == 0
        and tiles == cap * peers
        and cap >= rows_dev
        and cap * u_factors.shape[2] % 128 == 0
        and misfit.shape[2] % 512 == 0
        and misfit.shape[1] % 16 == 0
    )
    run = slot_sums if dense else tile_terms
    field, partial_sum = run(
        misfit, forward_fields, contrast, u_factors, v_factors, ranks, tile_cols, owner_slot
    )
    total = src_sum(partial_sum)
    sources = misfit.shape[1] * lax.axis_size("src")
    gradient = total * lax.rsqrt(jnp.float32(sources))
    return (field, gradient)


def solution(mesh):
    placed = (
        P("rows", "src", None),
        P("rows", "src", None),
        P("rows", None),
        P("rows", None, None, None),
        P("rows", None, None, None),
        P("rows", None),
        P(),
        P(),
    )
    return jax.shard_map(
        per_device,
        mesh=mesh,
        in_specs=placed,
        out_specs=(P("rows", "src", None), P("rows", None)),
        check_vma=False,
    )
```

```python
import functools

import jax
import jax.numpy as jnp
from jax import lax
from jax.experimental import pallas as pl
from jax.experimental.pallas import tpu as pltpu
from jax.sharding import PartitionSpec as P

APPS = 4

def parts_of(unknowns, peers):
    bits = list(range(peers.bit_length() - 1))
    turned = bits[1:2] + bits[:1] + bits[2:]
    width = unknowns // 2
    return [(0, width, bits), (width, width, turned)]


def spot(order, rel):
    place = 0
    for bit in order:
        place = place * 2 + ((rel >> bit) & 1)
    return place


def in_order(order, peers):
    return sorted(range(peers), key=lambda rel: spot(order, rel))


def vmem(count):
    return [pl.BlockSpec(memory_space=pltpu.VMEM)] * count


def params():
    return pltpu.CompilerParams(vmem_limit_bytes=24 * 1024 * 1024)


def cost(rows, columns, sources):
    return pl.CostEstimate(
        flops=2 * rows * columns * sources, bytes_accessed=2 * rows * columns, transcendentals=0
    )


def in_vmem(x):
    return pltpu.with_memory_space_constraint(x, pltpu.VMEM)


def in_hbm(x):
    return pltpu.with_memory_space_constraint(x, pltpu.HBM)


def pick_rows(every, code, sources, rows_dev):
    row = code // rows_dev
    total = jnp.zeros((sources, every.shape[1]), jnp.float32)
    for index in range(rows_dev):
        mine = every[index * sources : (index + 1) * sources]
        total = total + jnp.where(row == index, mine, 0.0)
    return total


def by_slot(coeff, code, rows_dev):
    local = code % rows_dev
    low = [
        jnp.where(local == index, coeff, 0.0).astype(jnp.bfloat16) for index in range(rows_dev)
    ]
    return jnp.concatenate(low, axis=0)


def times_u(low, factors):
    return lax.dot_general(
        low, factors, (((1,), (1,)), ((), ())), preferred_element_type=jnp.float32
    )


def put_terms(lhs, v_ref, group, part, outs, rows_dev, peers):
    first, width, order = part
    deep = lhs.shape[1]
    terms = jnp.dot(
        lhs,
        v_ref[pl.ds(group * deep, deep), pl.ds(first, width)],
        preferred_element_type=jnp.float32,
    )
    place = spot(order, group)
    out = outs[place >= peers // 2]
    place = place % (peers // 2) * rows_dev
    out[place : place + rows_dev] = terms.reshape(rows_dev, -1, width).astype(out.dtype)


def start_kernel(dims, *refs):
    rows_dev, tiles_row, rank_max, peers, parts = dims
    cols_hbm, owner_hbm, ranks_hbm, misfit_hbm, u_hbm, v_hbm = refs[:6]
    u_ref, v_ref, code_ref = refs[6:9]
    outs = refs[9 : 9 + 2 * len(parts)]
    cols, owner, ranks, misfit, word_at, lhs_ref, small, u_sem, v_sem = refs[9 + 2 * len(parts) :]
    here, src = lax.axis_index("rows"), lax.axis_index("src")
    codes = rows_dev * rows_dev
    tiles = rows_dev * tiles_row
    group_tiles = tiles // peers
    deep = group_tiles * rank_max
    sources = misfit.shape[1]
    copies = [
        pltpu.make_async_copy(whence, to, small.at[i])
        for i, (whence, to) in enumerate(
            zip((cols_hbm, owner_hbm, ranks_hbm, misfit_hbm), (cols, owner, ranks, misfit))
        )
    ]
    for copy in copies:
        copy.start()
    for copy in copies[:3]:
        copy.wait()

    def load(whence, to, sem, tile, at, group):
        pltpu.make_async_copy(
            whence.at[pl.ds(pl.multiple_of(tile * rank_max, rank_max), rank_max)],
            to.at[pl.ds(pl.multiple_of(at * rank_max, rank_max), rank_max)],
            sem.at[group],
        ).start()

    def sort_tiles(k, filled):
        slots = [owner[cols[k, here * rows_dev + row]] for row in range(rows_dev)]
        for row, slot in enumerate(slots):
            rel = turned(jnp.bitwise_xor(lax.div(slot, rows_dev), here), peers, src)
            shift = rel * 4
            at = rel * group_tiles + (lax.shift_right_logical(filled, shift) & 15)
            filled = filled + lax.shift_left(jnp.int32(1), shift)
            tile = row * tiles_row + k
            word_at[at] = tile * codes + row * rows_dev + lax.rem(slot, rows_dev)
        return filled

    def load_all(whence, to, sem):
        def one(at, carry):
            load(whence, to, sem, lax.div(word_at[at], codes), at, lax.div(at, group_tiles))
            return carry

        lax.fori_loop(0, tiles, one, 0, unroll=4)

    def loaded(ref, sem, group):
        piece = ref.at[pl.ds(group * deep, deep)]
        pltpu.make_async_copy(piece, piece, sem.at[group]).wait()

    lax.fori_loop(0, tiles_row, sort_tiles, jnp.int32(0), unroll=4)
    load_all(u_hbm, u_ref, u_sem)
    load_all(v_hbm, v_ref, v_sem)
    lane = lax.broadcasted_iota(jnp.int32, (1, deep), 1)
    for group in range(peers):
        code = jnp.full((1, deep), -1, jnp.int32)
        for i in range(group_tiles):
            at = group * group_tiles + i
            word = word_at[at]
            tile = lax.div(word, codes)
            rank = ranks[lax.div(tile, tiles_row), lax.rem(tile, tiles_row)]
            inside = (lane >= i * rank_max) & (lane < i * rank_max + rank)
            code = jnp.where(inside, lax.rem(word, codes), code)
        code_ref[pl.ds(group, 1), :] = code
    copies[3].wait()
    low = misfit[...].astype(jnp.bfloat16).reshape(rows_dev * sources, -1)
    for group in range(peers):
        loaded(u_ref, u_sem, group)
        code = code_ref[pl.ds(group, 1), :]
        every = times_u(low, u_ref[pl.ds(group * deep, deep), :])
        lhs_ref[group] = by_slot(pick_rows(every, code, sources, rows_dev), code, rows_dev)
    for group in range(peers):
        loaded(v_ref, v_sem, group)
        lhs = lhs_ref[group]
        for i, part in enumerate(parts):
            put_terms(lhs, v_ref, group, part, outs[2 * i : 2 * i + 2], rows_dev, peers)


def low_field(base_ref, came_ref, contrast_ref, part):
    first, width, _ = part
    rows = []
    for row in range(base_ref.shape[0]):
        scale = contrast_ref[pl.ds(row, 1), pl.ds(first, width)]
        field = base_ref[row] + scale * came_ref[row].astype(jnp.float32)
        rows.append(field.astype(jnp.bfloat16))
    return jnp.concatenate(rows, axis=0)


def early_kernel(dims, parts, code_ref, contrast_ref, *refs):
    rows_dev, peers = dims
    fields, (u_ref, out_ref) = refs[: 2 * len(parts)], refs[2 * len(parts) :]
    deep = code_ref.shape[1]
    sources = out_ref.shape[1]
    lows = [
        low_field(fields[2 * i], fields[2 * i + 1], contrast_ref, part)
        for i, part in enumerate(parts)
    ]
    for group in range(peers):
        every = 0.0
        for low, (first, width, _) in zip(lows, parts):
            every = every + times_u(low, u_ref[pl.ds(group * deep, deep), pl.ds(first, width)])
        code = code_ref[pl.ds(group, 1), :]
        out_ref[group] = pick_rows(every, code, sources, rows_dev)


def complete(dims, late, group, low, code_ref, sum_ref, u_ref):
    rows_dev, _ = dims
    deep = code_ref.shape[1]
    first, width, _ = late
    every = times_u(low, u_ref[pl.ds(group * deep, deep), pl.ds(first, width)])
    code = code_ref[pl.ds(group, 1), :]
    coeff = sum_ref[group] + pick_rows(every, code, sum_ref.shape[1], rows_dev)
    return by_slot(coeff, code, rows_dev)


def step_kernel(dims, late, known, todo, parts, code_ref, contrast_ref, sum_ref, *refs):
    base_ref, came_ref, u_ref, v_ref = refs[:4]
    held, refs = refs[4 : 4 + len(known)], refs[4 + len(known) :]
    rows_dev, peers = dims
    low = low_field(base_ref, came_ref, contrast_ref, late)
    ready = {group: (ref, i) for ref, some in zip(held, known) for i, group in enumerate(some)}
    outs, lhs_ref = refs[: len(parts)], refs[len(parts) :]

    def put(lhs, group):
        for out, (part, kept) in zip(outs, parts):
            if (spot(part[2], group) < peers // 2) == kept:
                put_terms(lhs, v_ref, group, part, (out, out), rows_dev, peers)

    for i, group in enumerate(todo):
        lhs = complete(dims, late, group, low, code_ref, sum_ref, u_ref)
        if lhs_ref:
            lhs_ref[0][i] = lhs
        put(lhs, group)
    for group, (ref, i) in ready.items():
        if any((spot(part[2], group) < peers // 2) == kept for part, kept in parts):
            put(ref[i], group)


def finish_kernel(parts, contrast_ref, forward_ref, *refs):
    fields, (field_ref, total_ref) = refs[: 2 * len(parts)], refs[2 * len(parts) :]
    for i, (first, width, _) in enumerate(parts):
        here = pl.ds(first, width)
        for row in range(field_ref.shape[0]):
            scale = contrast_ref[pl.ds(row, 1), here]
            field = fields[2 * i][row] + scale * fields[2 * i + 1][row].astype(jnp.float32)
            field_ref[row, :, here] = field
            product = forward_ref[row, :, here].astype(jnp.float32) * field
            total_ref[pl.ds(row, 1), here] = jnp.sum(product, axis=0, keepdims=True)


def turned(rel, peers, src):
    if peers < 4:
        return rel
    swapped = (rel >> 2 << 2) | ((rel & 1) << 1) | ((rel >> 1) & 1)
    odd = src % 2
    return swapped * odd + rel * (1 - odd)


def swap(x, bit, peers):
    count = lax.axis_size("src")
    pairs = [
        (row * count + src, (row ^ turned(1 << bit, peers, src)) * count + src)
        for row in range(peers)
        for src in range(count)
    ]
    return lax.ppermute(x, ("rows", "src"), pairs)


def slot_sums(
    misfit, forward_fields, contrast, u_factors, v_factors, ranks, tile_cols, owner_slot
):
    peers = lax.axis_size("rows")
    rows_dev, tiles_row, rank_max, unknowns = u_factors.shape
    sources = misfit.shape[1]
    tiles = rows_dev * tiles_row
    deep = tiles // peers * rank_max
    parts = parts_of(unknowns, peers)
    late = 1
    early = [i for i in range(len(parts)) if i != late]
    leaving, staying = [], list(range(peers))
    for part in parts:
        leaving.append([x for x in staying if spot(part[2], x) >= peers // 2])
        staying = [x for x in staying if x not in leaving[-1]]
    half = (peers // 2 * rows_dev, sources)
    sent = [jax.ShapeDtypeStruct((*half, part[1]), jnp.bfloat16) for part in parts]
    kept = [jax.ShapeDtypeStruct((*half, part[1]), jnp.float32) for part in parts]
    u, v = (x.reshape(tiles * rank_max, unknowns) for x in (u_factors, v_factors))
    hbm = [pl.BlockSpec(memory_space=pl.ANY)]
    smem = lambda *shape: pltpu.SMEM(shape, jnp.int32)
    u, v, code, *got = pl.pallas_call(
        functools.partial(start_kernel, (rows_dev, tiles_row, rank_max, peers, parts)),
        out_shape=[pltpu.VMEM(x.shape, x.dtype) for x in (u, v)]
        + [jax.ShapeDtypeStruct((peers, deep), jnp.int32)]
        + [x for pair in zip(kept, sent) for x in pair],
        in_specs=hbm * 6,
        out_specs=vmem(3 + 2 * len(parts)),
        scratch_shapes=[
            smem(*tile_cols.shape[::-1]),
            smem(*owner_slot.shape),
            smem(*ranks.shape),
            pltpu.VMEM(misfit.shape, misfit.dtype),
            smem(tiles),
            pltpu.VMEM((peers, rows_dev * sources, deep), jnp.bfloat16),
            pltpu.SemaphoreType.DMA((4,)),
            pltpu.SemaphoreType.DMA((peers,)),
            pltpu.SemaphoreType.DMA((peers,)),
        ],
        compiler_params=params(),
        cost_estimate=cost(2 * tiles * rank_max, unknowns, sources),
        name="start",
    )(*(in_hbm(x) for x in (tile_cols.T, owner_slot, ranks, misfit, u, v)))
    dims = (rows_dev, peers)
    scale = contrast[:, None, :]
    columns = [(slice(None), slice(None), slice(part[0], part[0] + part[1])) for part in parts]
    for step in range(APPS):
        if step == 0:
            keeps, goes = list(got[::2]), list(got[1::2])
        else:
            coeff = pl.pallas_call(
                functools.partial(early_kernel, dims, [parts[i] for i in early]),
                out_shape=jax.ShapeDtypeStruct((peers, sources, deep), jnp.float32),
                in_specs=vmem(3 + 2 * len(early)),
                out_specs=vmem(1)[0],
                compiler_params=params(),
                cost_estimate=cost(u.shape[0], unknowns // 2, sources),
                name="early",
            )(code, contrast, *(x for i in early for x in (base[i], came[i])), in_vmem(u))
            state = (code, contrast, coeff, base[late], came[late], in_vmem(u), in_vmem(v))
            known, held, made = [], [], []
            for todo, names, shapes in (
                (leaving[0], [(parts[0], False)], [sent[0]]),
                (leaving[1], [(parts[1], False)], [sent[1]]),
                (staying, [(part, True) for part in parts], kept),
            ):
                hand = []
                if todo is not staying:
                    shape = (len(todo), rows_dev * sources, deep)
                    hand = [jax.ShapeDtypeStruct(shape, jnp.bfloat16)]
                got = pl.pallas_call(
                    functools.partial(step_kernel, dims, parts[late], [*known], todo, names),
                    out_shape=[*shapes, *hand],
                    in_specs=vmem(7 + len(held)),
                    out_specs=vmem(len(shapes) + len(hand)),
                    compiler_params=params(),
                    cost_estimate=cost(u.shape[0], unknowns // 2, sources),
                    name="step",
                )(*state, *held)
                made += got[: len(shapes)]
                known.append(todo)
                held += got[len(shapes) :]
            goes, keeps = made[:2], made[2:]
        base, came = [None] * len(parts), [None] * len(parts)
        levels = len(parts[0][2])
        for level in range(levels):
            for i, part in enumerate(parts):
                came[i] = swap(goes[i], part[2][level], peers)
                if level < levels - 1:
                    mid = keeps[i].shape[0] // 2
                    goes[i] = keeps[i][mid:] + came[i][mid:].astype(jnp.float32)
                    goes[i] = goes[i].astype(jnp.bfloat16)
                    keeps[i] = keeps[i][:mid] + came[i][:mid].astype(jnp.float32)
        for i in range(len(parts)):
            base[i] = misfit[columns[i]] + scale[columns[i]] * keeps[i]
    return pl.pallas_call(
        functools.partial(finish_kernel, parts),
        out_shape=[
            jax.ShapeDtypeStruct(misfit.shape, jnp.float32),
            jax.ShapeDtypeStruct(contrast.shape, jnp.float32),
        ],
        in_specs=vmem(2 + 2 * len(parts)),
        out_specs=vmem(2),
        compiler_params=params(),
        name="finish",
    )(contrast, forward_fields, *(x for pair in zip(base, came) for x in pair))


def route_tiles(tile_cols, owner_slot, rows_dev, peers):
    tiles = rows_dev * tile_cols.shape[1]
    target_slot = owner_slot[tile_cols.reshape(peers, tiles)]
    target_dev = target_slot // rows_dev
    local_slot = target_slot % rows_dev
    same = target_dev[:, :, None] == target_dev[:, None, :]
    before = jnp.arange(tiles)[None, :] < jnp.arange(tiles)[:, None]
    order = jnp.sum(jnp.where(same & before[None, :, :], 1, 0), axis=2).astype(jnp.int32)
    return target_dev, local_slot, order


def tile_terms(
    misfit, forward_fields, contrast, u_factors, v_factors, ranks, tile_cols, owner_slot
):
    rows_dev, tiles_row, rank_max, unknowns = u_factors.shape
    tiles = rows_dev * tiles_row
    peers = lax.axis_size("rows")
    cap = (tiles + peers - 1) // peers
    sources = misfit.shape[1]
    here = lax.axis_index("rows")
    target_dev, local_slot, order = route_tiles(tile_cols, owner_slot, rows_dev, peers)
    mine_dev = lax.dynamic_index_in_dim(target_dev, here, 0, keepdims=False)
    mine_order = lax.dynamic_index_in_dim(order, here, 0, keepdims=False)
    box = mine_dev * cap + mine_order
    sender = jnp.arange(peers, dtype=jnp.int32)[:, None] * cap + order
    entry = jnp.where(target_dev == here, sender, peers * cap).reshape(-1)
    arrival = (
        jnp.full((peers * cap,), -1, jnp.int32).at[entry].set(local_slot.reshape(-1), mode="drop")
    )
    pick = (arrival[:, None] == jnp.arange(rows_dev, dtype=jnp.int32)[None, :]).astype(jnp.float32)
    keep = (jnp.arange(rank_max, dtype=jnp.int32)[None, None, :] < ranks[:, :, None]).astype(
        jnp.float32
    )
    field = misfit
    for step in range(APPS):
        coeff = jnp.einsum(
            "lsb,lkrb->lksr",
            field.astype(jnp.bfloat16),
            u_factors,
            preferred_element_type=jnp.float32,
        )
        tile_coeff = (coeff * keep[:, :, None, :]).astype(jnp.bfloat16)
        terms = jnp.einsum(
            "lksr,lkrb->lksb", tile_coeff, v_factors, preferred_element_type=jnp.float32
        )
        terms = terms.reshape(tiles, sources, unknowns)
        outgoing = jnp.zeros((peers * cap, sources, unknowns), jnp.float32).at[box].set(terms)
        incoming = lax.all_to_all(
            outgoing.reshape(peers, cap, sources, unknowns).astype(jnp.bfloat16),
            "rows",
            split_axis=0,
            concat_axis=0,
            tiled=True,
        ).astype(jnp.float32)
        field = misfit + contrast[:, None, :] * jnp.einsum(
            "eq,esb->qsb",
            pick,
            incoming.reshape(peers * cap, sources, unknowns),
            precision=lax.Precision.HIGHEST,
        )
    return field, jnp.sum(forward_fields.astype(jnp.float32) * field, axis=1)


def src_sum(x):
    count = lax.axis_size("src")
    if count & (count - 1):
        return lax.psum(x, "src")
    terms = [x]
    for step in range(1, count):
        terms.append(lax.ppermute(x, "src", [(i, i ^ step) for i in range(count)]))
    while len(terms) > 1:
        terms = [a + b for a, b in zip(terms[::2], terms[1::2])]
    return terms[0]


def per_device(
    misfit, forward_fields, contrast, u_factors, v_factors, ranks, tile_cols, owner_slot
):
    rows_dev, tiles_row = ranks.shape
    peers = lax.axis_size("rows")
    tiles = rows_dev * tiles_row
    cap = (tiles + peers - 1) // peers
    dense = (
        4 <= peers <= 8
        and cap < 16
        and peers & (peers - 1) == 0
        and tiles == cap * peers
        and cap >= rows_dev
        and cap * u_factors.shape[2] % 128 == 0
        and misfit.shape[2] % 512 == 0
        and misfit.shape[1] % 16 == 0
    )
    run = slot_sums if dense else tile_terms
    field, partial_sum = run(
        misfit, forward_fields, contrast, u_factors, v_factors, ranks, tile_cols, owner_slot
    )
    total = src_sum(partial_sum)
    sources = misfit.shape[1] * lax.axis_size("src")
    gradient = total * lax.rsqrt(jnp.float32(sources))
    return (field, gradient)


def solution(mesh):
    placed = (
        P("rows", "src", None),
        P("rows", "src", None),
        P("rows", None),
        P("rows", None, None, None),
        P("rows", None, None, None),
        P("rows", None),
        P(),
        P(),
    )
    return jax.shard_map(
        per_device,
        mesh=mesh,
        in_specs=placed,
        out_specs=(P("rows", "src", None), P("rows", None)),
        check_vma=False,
    )
```

```python
import functools

import jax
import jax.numpy as jnp
from jax import lax
from jax.experimental import pallas as pl
from jax.experimental.pallas import tpu as pltpu
from jax.sharding import PartitionSpec as P

APPS = 4

def parts_of(unknowns, peers):
    bits = list(range(peers.bit_length() - 1))
    turned = bits[1:] + bits[:1]
    width = unknowns // 2
    return [(0, width, bits), (width, width, turned)]


def spot(order, rel):
    place = 0
    for bit in order:
        place = place * 2 + ((rel >> bit) & 1)
    return place


def in_order(order, peers):
    return sorted(range(peers), key=lambda rel: spot(order, rel))


def vmem(count):
    return [pl.BlockSpec(memory_space=pltpu.VMEM)] * count


def params():
    return pltpu.CompilerParams(vmem_limit_bytes=24 * 1024 * 1024)


def cost(rows, columns, sources):
    return pl.CostEstimate(
        flops=2 * rows * columns * sources, bytes_accessed=2 * rows * columns, transcendentals=0
    )


def in_vmem(x):
    return pltpu.with_memory_space_constraint(x, pltpu.VMEM)


def in_hbm(x):
    return pltpu.with_memory_space_constraint(x, pltpu.HBM)


def pick_rows(every, code, sources, rows_dev):
    row = code // rows_dev
    total = jnp.zeros((sources, every.shape[1]), jnp.float32)
    for index in range(rows_dev):
        mine = every[index * sources : (index + 1) * sources]
        total = total + jnp.where(row == index, mine, 0.0)
    return total


def by_slot(coeff, code, rows_dev):
    local = code % rows_dev
    low = [
        jnp.where(local == index, coeff, 0.0).astype(jnp.bfloat16) for index in range(rows_dev)
    ]
    return jnp.concatenate(low, axis=0)


def times_u(low, factors):
    return lax.dot_general(
        low, factors, (((1,), (1,)), ((), ())), preferred_element_type=jnp.float32
    )


def put_terms(lhs, v_ref, group, part, outs, rows_dev, peers):
    first, width, order = part
    deep = lhs.shape[1]
    terms = jnp.dot(
        lhs,
        v_ref[pl.ds(group * deep, deep), pl.ds(first, width)],
        preferred_element_type=jnp.float32,
    )
    place = spot(order, group)
    out = outs[place >= peers // 2]
    place = place % (peers // 2) * rows_dev
    out[place : place + rows_dev] = terms.reshape(rows_dev, -1, width).astype(out.dtype)


def start_kernel(dims, *refs):
    rows_dev, tiles_row, rank_max, peers, parts = dims
    cols_hbm, owner_hbm, ranks_hbm, misfit_hbm, u_hbm, v_hbm = refs[:6]
    u_ref, v_ref, code_ref = refs[6:9]
    outs = refs[9 : 9 + 2 * len(parts)]
    cols, owner, ranks, misfit, word_at, lhs_ref, small, u_sem, v_sem = refs[9 + 2 * len(parts) :]
    here, src = lax.axis_index("rows"), lax.axis_index("src")
    codes = rows_dev * rows_dev
    tiles = rows_dev * tiles_row
    group_tiles = tiles // peers
    deep = group_tiles * rank_max
    sources = misfit.shape[1]
    copies = [
        pltpu.make_async_copy(whence, to, small.at[i])
        for i, (whence, to) in enumerate(
            zip((cols_hbm, owner_hbm, ranks_hbm, misfit_hbm), (cols, owner, ranks, misfit))
        )
    ]
    for copy in copies:
        copy.start()
    for copy in copies[:3]:
        copy.wait()

    def load(whence, to, sem, tile, at, group):
        pltpu.make_async_copy(
            whence.at[pl.ds(pl.multiple_of(tile * rank_max, rank_max), rank_max)],
            to.at[pl.ds(pl.multiple_of(at * rank_max, rank_max), rank_max)],
            sem.at[group],
        ).start()

    def sort_tiles(k, filled):
        slots = [owner[cols[k, here * rows_dev + row]] for row in range(rows_dev)]
        for row, slot in enumerate(slots):
            rel = turned(jnp.bitwise_xor(lax.div(slot, rows_dev), here), peers, src)
            shift = rel * 4
            at = rel * group_tiles + (lax.shift_right_logical(filled, shift) & 15)
            filled = filled + lax.shift_left(jnp.int32(1), shift)
            tile = row * tiles_row + k
            word_at[at] = tile * codes + row * rows_dev + lax.rem(slot, rows_dev)
        return filled

    def load_all(whence, to, sem):
        def one(at, carry):
            load(whence, to, sem, lax.div(word_at[at], codes), at, lax.div(at, group_tiles))
            return carry

        lax.fori_loop(0, tiles, one, 0, unroll=4)

    def loaded(ref, sem, group):
        piece = ref.at[pl.ds(group * deep, deep)]
        pltpu.make_async_copy(piece, piece, sem.at[group]).wait()

    lax.fori_loop(0, tiles_row, sort_tiles, jnp.int32(0), unroll=4)
    load_all(u_hbm, u_ref, u_sem)
    load_all(v_hbm, v_ref, v_sem)
    lane = lax.broadcasted_iota(jnp.int32, (1, deep), 1)
    for group in range(peers):
        code = jnp.full((1, deep), -1, jnp.int32)
        for i in range(group_tiles):
            at = group * group_tiles + i
            word = word_at[at]
            tile = lax.div(word, codes)
            rank = ranks[lax.div(tile, tiles_row), lax.rem(tile, tiles_row)]
            inside = (lane >= i * rank_max) & (lane < i * rank_max + rank)
            code = jnp.where(inside, lax.rem(word, codes), code)
        code_ref[pl.ds(group, 1), :] = code
    copies[3].wait()
    low = misfit[...].astype(jnp.bfloat16).reshape(rows_dev * sources, -1)
    for group in range(peers):
        loaded(u_ref, u_sem, group)
        code = code_ref[pl.ds(group, 1), :]
        every = times_u(low, u_ref[pl.ds(group * deep, deep), :])
        lhs_ref[group] = by_slot(pick_rows(every, code, sources, rows_dev), code, rows_dev)
    for group in range(peers):
        loaded(v_ref, v_sem, group)
        lhs = lhs_ref[group]
        for i, part in enumerate(parts):
            put_terms(lhs, v_ref, group, part, outs[2 * i : 2 * i + 2], rows_dev, peers)


def low_field(base_ref, came_ref, contrast_ref, part):
    first, width, _ = part
    rows = []
    for row in range(base_ref.shape[0]):
        scale = contrast_ref[pl.ds(row, 1), pl.ds(first, width)]
        field = base_ref[row] + scale * came_ref[row].astype(jnp.float32)
        rows.append(field.astype(jnp.bfloat16))
    return jnp.concatenate(rows, axis=0)


def early_kernel(dims, parts, code_ref, contrast_ref, *refs):
    rows_dev, peers = dims
    fields, (u_ref, out_ref) = refs[: 2 * len(parts)], refs[2 * len(parts) :]
    deep = code_ref.shape[1]
    sources = out_ref.shape[1]
    lows = [
        low_field(fields[2 * i], fields[2 * i + 1], contrast_ref, part)
        for i, part in enumerate(parts)
    ]
    for group in range(peers):
        every = 0.0
        for low, (first, width, _) in zip(lows, parts):
            every = every + times_u(low, u_ref[pl.ds(group * deep, deep), pl.ds(first, width)])
        code = code_ref[pl.ds(group, 1), :]
        out_ref[group] = pick_rows(every, code, sources, rows_dev)


def complete(dims, late, group, low, code_ref, sum_ref, u_ref):
    rows_dev, _ = dims
    deep = code_ref.shape[1]
    first, width, _ = late
    every = times_u(low, u_ref[pl.ds(group * deep, deep), pl.ds(first, width)])
    code = code_ref[pl.ds(group, 1), :]
    coeff = sum_ref[group] + pick_rows(every, code, sum_ref.shape[1], rows_dev)
    return by_slot(coeff, code, rows_dev)


def step_kernel(dims, late, known, todo, parts, code_ref, contrast_ref, sum_ref, *refs):
    base_ref, came_ref, u_ref, v_ref = refs[:4]
    held, refs = refs[4 : 4 + len(known)], refs[4 + len(known) :]
    rows_dev, peers = dims
    low = low_field(base_ref, came_ref, contrast_ref, late)
    ready = {group: (ref, i) for ref, some in zip(held, known) for i, group in enumerate(some)}
    outs, lhs_ref = refs[: len(parts)], refs[len(parts) :]

    def put(lhs, group):
        for out, (part, kept) in zip(outs, parts):
            if (spot(part[2], group) < peers // 2) == kept:
                put_terms(lhs, v_ref, group, part, (out, out), rows_dev, peers)

    for i, group in enumerate(todo):
        lhs = complete(dims, late, group, low, code_ref, sum_ref, u_ref)
        if lhs_ref:
            lhs_ref[0][i] = lhs
        put(lhs, group)
    for group, (ref, i) in ready.items():
        if any((spot(part[2], group) < peers // 2) == kept for part, kept in parts):
            put(ref[i], group)


def finish_kernel(parts, contrast_ref, forward_ref, *refs):
    fields, (field_ref, total_ref) = refs[: 2 * len(parts)], refs[2 * len(parts) :]
    for i, (first, width, _) in enumerate(parts):
        here = pl.ds(first, width)
        for row in range(field_ref.shape[0]):
            scale = contrast_ref[pl.ds(row, 1), here]
            field = fields[2 * i][row] + scale * fields[2 * i + 1][row].astype(jnp.float32)
            field_ref[row, :, here] = field
            product = forward_ref[row, :, here].astype(jnp.float32) * field
            total_ref[pl.ds(row, 1), here] = jnp.sum(product, axis=0, keepdims=True)


def turned(rel, peers, src):
    if peers < 4:
        return rel
    swapped = (rel >> 2 << 2) | ((rel & 1) << 1) | ((rel >> 1) & 1)
    odd = src % 2
    return swapped * odd + rel * (1 - odd)


def swap(x, bit, peers):
    count = lax.axis_size("src")
    pairs = [
        (row * count + src, (row ^ turned(1 << bit, peers, src)) * count + src)
        for row in range(peers)
        for src in range(count)
    ]
    return lax.ppermute(x, ("rows", "src"), pairs)


def slot_sums(
    misfit, forward_fields, contrast, u_factors, v_factors, ranks, tile_cols, owner_slot
):
    peers = lax.axis_size("rows")
    rows_dev, tiles_row, rank_max, unknowns = u_factors.shape
    sources = misfit.shape[1]
    tiles = rows_dev * tiles_row
    deep = tiles // peers * rank_max
    parts = parts_of(unknowns, peers)
    late = 1
    early = [i for i in range(len(parts)) if i != late]
    leaving, staying = [], list(range(peers))
    for part in parts:
        leaving.append([x for x in staying if spot(part[2], x) >= peers // 2])
        staying = [x for x in staying if x not in leaving[-1]]
    half = (peers // 2 * rows_dev, sources)
    sent = [jax.ShapeDtypeStruct((*half, part[1]), jnp.bfloat16) for part in parts]
    kept = [jax.ShapeDtypeStruct((*half, part[1]), jnp.float32) for part in parts]
    u, v = (x.reshape(tiles * rank_max, unknowns) for x in (u_factors, v_factors))
    hbm = [pl.BlockSpec(memory_space=pl.ANY)]
    smem = lambda *shape: pltpu.SMEM(shape, jnp.int32)
    u, v, code, *got = pl.pallas_call(
        functools.partial(start_kernel, (rows_dev, tiles_row, rank_max, peers, parts)),
        out_shape=[pltpu.VMEM(x.shape, x.dtype) for x in (u, v)]
        + [jax.ShapeDtypeStruct((peers, deep), jnp.int32)]
        + [x for pair in zip(kept, sent) for x in pair],
        in_specs=hbm * 6,
        out_specs=vmem(3 + 2 * len(parts)),
        scratch_shapes=[
            smem(*tile_cols.shape[::-1]),
            smem(*owner_slot.shape),
            smem(*ranks.shape),
            pltpu.VMEM(misfit.shape, misfit.dtype),
            smem(tiles),
            pltpu.VMEM((peers, rows_dev * sources, deep), jnp.bfloat16),
            pltpu.SemaphoreType.DMA((4,)),
            pltpu.SemaphoreType.DMA((peers,)),
            pltpu.SemaphoreType.DMA((peers,)),
        ],
        compiler_params=params(),
        cost_estimate=cost(2 * tiles * rank_max, unknowns, sources),
        name="start",
    )(*(in_hbm(x) for x in (tile_cols.T, owner_slot, ranks, misfit, u, v)))
    dims = (rows_dev, peers)
    scale = contrast[:, None, :]
    columns = [(slice(None), slice(None), slice(part[0], part[0] + part[1])) for part in parts]
    for step in range(APPS):
        if step == 0:
            keeps, goes = list(got[::2]), list(got[1::2])
        else:
            coeff = pl.pallas_call(
                functools.partial(early_kernel, dims, [parts[i] for i in early]),
                out_shape=jax.ShapeDtypeStruct((peers, sources, deep), jnp.float32),
                in_specs=vmem(3 + 2 * len(early)),
                out_specs=vmem(1)[0],
                compiler_params=params(),
                cost_estimate=cost(u.shape[0], unknowns // 2, sources),
                name="early",
            )(code, contrast, *(x for i in early for x in (base[i], came[i])), in_vmem(u))
            state = (code, contrast, coeff, base[late], came[late], in_vmem(u), in_vmem(v))
            known, held, made = [], [], []
            for todo, names, shapes in (
                (leaving[0], [(parts[0], False)], [sent[0]]),
                (leaving[1], [(parts[1], False)], [sent[1]]),
                (staying, [(part, True) for part in parts], kept),
            ):
                hand = []
                if todo is not staying:
                    shape = (len(todo), rows_dev * sources, deep)
                    hand = [jax.ShapeDtypeStruct(shape, jnp.bfloat16)]
                got = pl.pallas_call(
                    functools.partial(step_kernel, dims, parts[late], [*known], todo, names),
                    out_shape=[*shapes, *hand],
                    in_specs=vmem(7 + len(held)),
                    out_specs=vmem(len(shapes) + len(hand)),
                    compiler_params=params(),
                    cost_estimate=cost(u.shape[0], unknowns // 2, sources),
                    name="step",
                )(*state, *held)
                made += got[: len(shapes)]
                known.append(todo)
                held += got[len(shapes) :]
            goes, keeps = made[:2], made[2:]
        base, came = [None] * len(parts), [None] * len(parts)
        levels = len(parts[0][2])
        for level in range(levels):
            for i, part in enumerate(parts):
                came[i] = swap(goes[i], part[2][level], peers)
                if level < levels - 1:
                    mid = keeps[i].shape[0] // 2
                    goes[i] = keeps[i][mid:] + came[i][mid:].astype(jnp.float32)
                    goes[i] = goes[i].astype(jnp.bfloat16)
                    keeps[i] = keeps[i][:mid] + came[i][:mid].astype(jnp.float32)
        for i in range(len(parts)):
            base[i] = misfit[columns[i]] + scale[columns[i]] * keeps[i]
    return pl.pallas_call(
        functools.partial(finish_kernel, parts),
        out_shape=[
            jax.ShapeDtypeStruct(misfit.shape, jnp.float32),
            jax.ShapeDtypeStruct(contrast.shape, jnp.float32),
        ],
        in_specs=vmem(2 + 2 * len(parts)),
        out_specs=vmem(2),
        compiler_params=params(),
        name="finish",
    )(contrast, forward_fields, *(x for pair in zip(base, came) for x in pair))


def route_tiles(tile_cols, owner_slot, rows_dev, peers):
    tiles = rows_dev * tile_cols.shape[1]
    target_slot = owner_slot[tile_cols.reshape(peers, tiles)]
    target_dev = target_slot // rows_dev
    local_slot = target_slot % rows_dev
    same = target_dev[:, :, None] == target_dev[:, None, :]
    before = jnp.arange(tiles)[None, :] < jnp.arange(tiles)[:, None]
    order = jnp.sum(jnp.where(same & before[None, :, :], 1, 0), axis=2).astype(jnp.int32)
    return target_dev, local_slot, order


def tile_terms(
    misfit, forward_fields, contrast, u_factors, v_factors, ranks, tile_cols, owner_slot
):
    rows_dev, tiles_row, rank_max, unknowns = u_factors.shape
    tiles = rows_dev * tiles_row
    peers = lax.axis_size("rows")
    cap = (tiles + peers - 1) // peers
    sources = misfit.shape[1]
    here = lax.axis_index("rows")
    target_dev, local_slot, order = route_tiles(tile_cols, owner_slot, rows_dev, peers)
    mine_dev = lax.dynamic_index_in_dim(target_dev, here, 0, keepdims=False)
    mine_order = lax.dynamic_index_in_dim(order, here, 0, keepdims=False)
    box = mine_dev * cap + mine_order
    sender = jnp.arange(peers, dtype=jnp.int32)[:, None] * cap + order
    entry = jnp.where(target_dev == here, sender, peers * cap).reshape(-1)
    arrival = (
        jnp.full((peers * cap,), -1, jnp.int32).at[entry].set(local_slot.reshape(-1), mode="drop")
    )
    pick = (arrival[:, None] == jnp.arange(rows_dev, dtype=jnp.int32)[None, :]).astype(jnp.float32)
    keep = (jnp.arange(rank_max, dtype=jnp.int32)[None, None, :] < ranks[:, :, None]).astype(
        jnp.float32
    )
    field = misfit
    for step in range(APPS):
        coeff = jnp.einsum(
            "lsb,lkrb->lksr",
            field.astype(jnp.bfloat16),
            u_factors,
            preferred_element_type=jnp.float32,
        )
        tile_coeff = (coeff * keep[:, :, None, :]).astype(jnp.bfloat16)
        terms = jnp.einsum(
            "lksr,lkrb->lksb", tile_coeff, v_factors, preferred_element_type=jnp.float32
        )
        terms = terms.reshape(tiles, sources, unknowns)
        outgoing = jnp.zeros((peers * cap, sources, unknowns), jnp.float32).at[box].set(terms)
        incoming = lax.all_to_all(
            outgoing.reshape(peers, cap, sources, unknowns).astype(jnp.bfloat16),
            "rows",
            split_axis=0,
            concat_axis=0,
            tiled=True,
        ).astype(jnp.float32)
        field = misfit + contrast[:, None, :] * jnp.einsum(
            "eq,esb->qsb",
            pick,
            incoming.reshape(peers * cap, sources, unknowns),
            precision=lax.Precision.HIGHEST,
        )
    return field, jnp.sum(forward_fields.astype(jnp.float32) * field, axis=1)


def src_sum(x):
    count = lax.axis_size("src")
    if count & (count - 1):
        return lax.psum(x, "src")
    terms = [x]
    for step in range(1, count):
        terms.append(lax.ppermute(x, "src", [(i, i ^ step) for i in range(count)]))
    while len(terms) > 1:
        terms = [a + b for a, b in zip(terms[::2], terms[1::2])]
    return terms[0]


def per_device(
    misfit, forward_fields, contrast, u_factors, v_factors, ranks, tile_cols, owner_slot
):
    rows_dev, tiles_row = ranks.shape
    peers = lax.axis_size("rows")
    tiles = rows_dev * tiles_row
    cap = (tiles + peers - 1) // peers
    dense = (
        4 <= peers <= 8
        and cap < 16
        and peers & (peers - 1) == 0
        and tiles == cap * peers
        and cap >= rows_dev
        and cap * u_factors.shape[2] % 128 == 0
        and misfit.shape[2] % 512 == 0
        and misfit.shape[1] % 16 == 0
    )
    run = slot_sums if dense else tile_terms
    field, partial_sum = run(
        misfit, forward_fields, contrast, u_factors, v_factors, ranks, tile_cols, owner_slot
    )
    total = src_sum(partial_sum)
    sources = misfit.shape[1] * lax.axis_size("src")
    gradient = total * lax.rsqrt(jnp.float32(sources))
    return (field, gradient)


def solution(mesh):
    placed = (
        P("rows", "src", None),
        P("rows", "src", None),
        P("rows", None),
        P("rows", None, None, None),
        P("rows", None, None, None),
        P("rows", None),
        P(),
        P(),
    )
    return jax.shard_map(
        per_device,
        mesh=mesh,
        in_specs=placed,
        out_specs=(P("rows", "src", None), P("rows", None)),
        check_vma=False,
    )
```
